256 devices in a mesh: gx: 16 (over z, core), gy: 16 (over x, y).
Axes of the slice: x: 4, y: 4, z: 8, core: 2. Of those that a mesh axis runs over, the one named last changes fastest.
Arguments:
- velocity_guess: float32 [3, 256, 256, 256], P(None, 'gx', 'gy'), may hold values from -1.2 to 1.2
- forcing: float32 [3, 256, 256, 256], P(None, 'gx', 'gy'), may hold values from -6 to 6
- cell_type: int32 [256, 256, 256], P('gx', 'gy'), may hold values from 0 to 3
- viscosities: float32 [4], replicated, may hold values from 0.2 to 5
Outputs:
- level0_iterate: float32 [3, 256, 256, 256], P(None, 'gx', 'gy')
- level1_correction: float32 [3, 128, 128, 128], P(None, 'gx', 'gy')
- level2_correction: float32 [3, 64, 64, 64], P(None, 'gx', 'gy')
- level3_correction: float32 [3, 32, 32, 32], P(None, 'gx', 'gy')
- level4_correction: float32 [3, 16, 16, 16], P(None, 'gx', 'gy')
- coarsest_residual: float32 [3, 16, 16, 16], P(None, 'gx', 'gy')
The draws below stay inside these ranges and needn't reach their ends.
All inputs are finite; a program needn't handle non-finite values.
Results may differ from the reference program's by a relative error of at most 0.00027.
Values sent between devices are 32-bit elements; how exact they have to be, the bound alone decides.
No kernel may reach another device: no remote copies, remote signals or barrier semaphores. Data moves between devices by JAX's collectives and lax.ppermute only.
A program may use at most 128 MiB of HBM per device.

```python
import math
import jax
import jax.numpy as jnp

CZ = 256
SWEEPS = 3
LEVELS = 4
TYPES = 4
NX = 256
NY = 256


def with_ends(entries, rng, low, top_value):
    extent = entries.shape
    place = [jax.random.randint(jax.random.fold_in(rng, axis), (), 0, extent[axis]) for axis in range(len(extent))]
    entries = entries.at[tuple(place)].set(low)
    longest = extent.index(max(extent))
    place[longest] = (place[longest] + 1) % extent[longest]
    return entries.at[tuple(place)].set(top_value)


def level_of(stream_key, extent, shards, smallest, high):
    factor_of = 1.0
    for axis_at, blocks in shards:
        draws = jax.random.uniform(jax.random.fold_in(jax.random.fold_in(stream_key, 6), axis_at), (blocks,), jnp.float32, smallest / len(shards), high / len(shards))
        factor_of = factor_of * jnp.repeat(jnp.exp(draws), extent[axis_at] // blocks).reshape((-1,) + (1,) * (len(extent) - 1 - axis_at))
    return factor_of


def centred(rng, dims, spread, limit, split=(), dtype=jnp.bfloat16):
    level = level_of(rng, dims, split, -0.22, 0.18) if split else 1.0
    result = jax.random.normal(rng, dims, jnp.float32) * spread * level
    return jnp.minimum(jnp.maximum(result, -limit), limit).astype(dtype)


def setup_inputs(seed: int = 0) -> dict:
    key_of = jax.random.split(jax.random.key(seed), 5)
    return {
        "velocity_guess": centred(key_of[0], (3, NX, NY, CZ), 0.2, 1.2, ((1, 16), (2, 16)), jnp.float32),
        "forcing": centred(key_of[1], (3, NX, NY, CZ), 1.0, 6.0, ((1, 16), (2, 16)), jnp.float32),
        "cell_type": with_ends(jax.random.randint(key_of[2], (NX, NY, CZ), 0, TYPES), jax.random.fold_in(key_of[2], 1), 0, TYPES - 1).astype(jnp.int32),
        "viscosities": jnp.clip(jnp.exp(jax.random.uniform(key_of[3], (TYPES,), jnp.float32, math.log(0.2), math.log(5.0))), 0.2, 5.0),
    }


damping = 0.8
mass_term = 0.05


def coefficients(viscosity, level_scale):
    padded = jnp.pad(viscosity, ((0, 0), (0, 0), (1, 1)))
    centre = padded[1:-1, 1:-1, 1:-1]
    face_terms = (0.5 * (centre + padded[:-2, 1:-1, 1:-1]),
                  0.5 * (centre + padded[2:, 1:-1, 1:-1]),
                  0.5 * (centre + padded[1:-1, :-2, 1:-1]),
                  0.5 * (centre + padded[1:-1, 2:, 1:-1]),
                  0.5 * (centre + padded[1:-1, 1:-1, :-2]),
                  0.5 * (centre + padded[1:-1, 1:-1, 2:]))
    face_sum = face_terms[0] + face_terms[1] + face_terms[2] + face_terms[3] + face_terms[4] + face_terms[5]
    return face_terms, mass_term + level_scale * face_sum


def operate(velocity, face_terms, diagonal, level_scale):
    padded = jnp.pad(velocity, ((0, 0), (0, 0), (0, 0), (1, 1)))
    centre = padded[:, 1:-1, 1:-1, 1:-1]
    flux = (face_terms[0] * padded[:, :-2, 1:-1, 1:-1] + face_terms[1] * padded[:, 2:, 1:-1, 1:-1]
            + face_terms[2] * padded[:, 1:-1, :-2, 1:-1] + face_terms[3] * padded[:, 1:-1, 2:, 1:-1]
            + face_terms[4] * padded[:, 1:-1, 1:-1, :-2] + face_terms[5] * padded[:, 1:-1, 1:-1, 2:])
    return diagonal * centre - level_scale * flux


def restrict(values):
    channels, rows_x, rows_y, rows_z = values.shape
    return values.reshape(channels, rows_x // 2, 2, rows_y // 2, 2, rows_z // 2, 2).mean(axis=(2, 4, 6))


def pad_plane(values):
    return jnp.pad(values, ((0, 0), (1, 1), (1, 1), (0, 0)))


def reference(velocity_guess, forcing, cell_type, viscosities):
    viscosity = viscosities[cell_type]
    velocity = velocity_guess
    source = forcing
    results = []
    residual = forcing
    for grid_level in range(LEVELS + 1):
        level_scale = 0.25 ** grid_level
        face_terms, diagonal = coefficients(jnp.pad(viscosity, ((1, 1), (1, 1), (0, 0))), level_scale)
        if grid_level > 0:
            velocity = jnp.zeros_like(source)
        for sweep_index in range(SWEEPS):
            velocity = velocity + damping * (source - operate(pad_plane(velocity), face_terms, diagonal, level_scale)) / diagonal
        residual = source - operate(pad_plane(velocity), face_terms, diagonal, level_scale)
        results.append(velocity)
        if grid_level < LEVELS:
            packet = restrict(jnp.concatenate([residual, viscosity[None]], axis=0))
            source = packet[:3]
            viscosity = packet[3]
    return (results[0], results[1], results[2], results[3], results[4], residual)
```

```python
import functools

import jax
import jax.numpy as jnp
from jax import lax
from jax.experimental import pallas as pl
from jax.experimental.pallas import tpu as pltpu
from jax.sharding import PartitionSpec as P

SWEEPS = 3
LEVELS = 4
HALO = SWEEPS + 1

damping = 0.8
mass_term = 0.05


def passed_along(value, axis, steps):
    count = lax.axis_size(axis)
    initial, last = (max(0, -steps), min(count, count - steps))
    return lax.ppermute(value, axis, [(source, source + steps) for source in range(initial, last)])


def split_dot(rows, pool):
    total = None
    for part in range(3):
        piece = rows.astype(jnp.bfloat16)
        term = jnp.dot(piece, pool, preferred_element_type=jnp.float32)
        total = term if total is None else total + term
        if part < 2:
            rows = rows - piece.astype(jnp.float32)
    return total


def pair_pool(lanes):
    source = lax.broadcasted_iota(jnp.int32, (lanes, 128), 0)
    target = lax.broadcasted_iota(jnp.int32, (lanes, 128), 1)
    return jnp.where(source // 2 == target, 0.125, 0.0).astype(jnp.bfloat16)


def make_coefficients(scale, m, cx, cym, cyp, czm, czp, weight, diag):
    planes, rows, lanes = m.shape
    half = 0.5 * scale
    lane = lax.broadcasted_iota(jnp.int32, (rows, lanes), 1)
    cx[0] = half * (m[0] + m[1])

    def plane(i, _):
        centre = m[i]
        upper = m[i + 1]
        y_lower = pltpu.roll(centre, 1, 0)
        y_upper = pltpu.roll(centre, rows - 1, 0)
        z_lower = jnp.where(lane == 0, 0.0, pltpu.roll(centre, 1, 1))
        z_upper = jnp.where(lane == lanes - 1, 0.0, pltpu.roll(centre, lanes - 1, 1))
        f_xl, f_xu = half * (centre + m[i - 1]), half * (centre + upper)
        f_yl, f_yu = half * (centre + y_lower), half * (centre + y_upper)
        f_zl, f_zu = half * (centre + z_lower), half * (centre + z_upper)
        total = mass_term + (f_xl + f_xu + f_yl + f_yu + f_zl + f_zu)
        cx[i] = f_xu
        cym[i], cyp[i] = f_yl, f_yu
        czm[i] = jnp.where(lane == 0, 0.0, f_zl)
        czp[i] = jnp.where(lane == lanes - 1, 0.0, f_zu)
        diag[i] = total
        weight[i] = jnp.where(centre > 0.0, damping / total, 0.0)
        return 0

    lax.fori_loop(1, planes - 1, plane, 0)


def flux_of(u, c, i, cx, cym, cyp, czm, czp):
    rows, lanes = u.shape[2:]
    centre = u[c, i]
    flux = cx[i - 1] * u[c, i - 1] + cx[i] * u[c, i + 1]
    flux += cym[i] * pltpu.roll(centre, 1, 0) + cyp[i] * pltpu.roll(centre, rows - 1, 0)
    flux += czm[i] * pltpu.roll(centre, 1, 1) + czp[i] * pltpu.roll(centre, lanes - 1, 1)
    return centre, flux


def relax(lo, hi, source, target, f, weight, faces, out=None):
    def plane(i, _):
        for c in range(3):
            centre, flux = flux_of(source, c, i, *faces)
            target[c, i] = (1.0 - damping) * centre + weight[i] * (f[c, i] + flux)
        return 0

    lax.fori_loop(lo, hi, plane, 0)


def start_from_zero(lo, hi, target, f, weight):
    def plane(i, _):
        for c in range(3):
            target[c, i] = weight[i] * f[c, i]
        return 0

    lax.fori_loop(lo, hi, plane, 0)


def residual_pairs(own, own_rows, u, f, m, diag, faces, pairs):
    def pair(p, _):
        i = HALO + 2 * p
        for c in range(3):
            both = None
            for j in (i, i + 1):
                centre, flux = flux_of(u, c, j, *faces)
                value = f[c, j] + flux - diag[j] * centre
                both = value if both is None else both + value
            pairs[c, p] = both[:own_rows]
        pairs[3, p] = (m[i] + m[i + 1])[:own_rows]
        return 0

    lax.fori_loop(0, own // 2, pair, 0)


def fine_kernel(u_in, f_in, m_in, ylo, yhi, xlo, xhi, u_out, packet,
                ua, ub, f, m, cx, cym, cyp, czm, czp, weight, diag, pairs, pooled):
    own, rows = u_in.shape[1:3]
    body = pl.ds(HALO, own)
    for c in range(3):
        ua[c, body, :rows] = u_in[c]
        ua[c, body, rows:rows + HALO] = yhi[c]
        ua[c, body, rows + HALO:] = ylo[c]
        ua[c, :HALO] = xlo[HALO * c:HALO * (c + 1)]
        ua[c, HALO + own:] = xhi[HALO * c:HALO * (c + 1)]
        f[c, body, :rows] = f_in[c]
        f[c, body, rows:rows + HALO] = yhi[3 + c]
        f[c, body, rows + HALO:] = ylo[3 + c]
        at = 3 * HALO + (HALO - 1) * c
        f[c, 1:HALO] = xlo[at:at + HALO - 1]
        f[c, HALO + own:HALO + own + HALO - 1] = xhi[at:at + HALO - 1]
    m[body, :rows] = m_in[...]
    m[body, rows:rows + HALO] = yhi[6]
    m[body, rows + HALO:] = ylo[6]
    at = 3 * HALO + 3 * (HALO - 1)
    m[:HALO] = xlo[at:]
    m[HALO + own:] = xhi[at:]
    planes = own + 2 * HALO
    make_coefficients(1.0, m, cx, cym, cyp, czm, czp, weight, diag)
    faces = (cx, cym, cyp, czm, czp)
    relax(1, planes - 1, ua, ub, f, weight, faces)
    relax(2, planes - 2, ub, ua, f, weight, faces)
    relax(3, planes - 3, ua, ub, f, weight, faces)
    for c in range(3):
        u_out[c] = ub[c, body, :rows]
    residual_pairs(own, rows, ub, f, m, diag, faces, pairs)
    lanes = pairs.shape[-1]
    summed = split_dot(pairs[...].reshape(-1, lanes), pair_pool(lanes))
    pooled[...] = summed.reshape(pooled.shape)
    packet[...] = pooled[:, pl.ds(0, rows // 2, 2), :] + pooled[:, pl.ds(1, rows // 2, 2), :]


def middle_kernel(scale, p_in, ylo, yhi, xlo, xhi, u_out, packet,
                  ua, ub, f, m, cx, cym, cyp, czm, czp, weight, diag, pairs, pooled):
    own, rows = p_in.shape[1:3]
    body = pl.ds(HALO, own)
    planes = own + 2 * HALO
    total_rows = m.shape[1]
    for c in range(4):
        if c < 3:
            place = f.at[c]
        else:
            place = m
        if total_rows > rows + 2 * HALO:
            place[body] = jnp.zeros((own,) + m.shape[1:], jnp.float32)
        place[body, :rows] = p_in[c]
        place[body, rows:rows + HALO] = yhi[c]
        place[body, total_rows - HALO:] = ylo[c]
        place[:HALO] = xlo[c]
        place[HALO + own:] = xhi[c]
    make_coefficients(scale, m, cx, cym, cyp, czm, czp, weight, diag)
    faces = (cx, cym, cyp, czm, czp)
    start_from_zero(1, planes - 1, ub, f, weight)
    relax(2, planes - 2, ub, ua, f, weight, faces)
    relax(3, planes - 3, ua, ub, f, weight, faces)
    lanes = u_out.shape[-1]
    for c in range(3):
        u_out[c] = ub[c, body, :rows, :lanes]
    residual_pairs(own, rows, ub, f, m, diag, faces, pairs)
    if rows > 4:
        lanes = pairs.shape[-1]
        summed = split_dot(pairs[...].reshape(-1, lanes), pair_pool(lanes))
        pooled[...] = summed.reshape(pooled.shape)
        packet[...] = pooled[:, pl.ds(0, rows // 2, 2), :] + pooled[:, pl.ds(1, rows // 2, 2), :]
    else:
        for c in range(4):
            for p in range(own // 2):
                for q in range(rows // 2):
                    at = 128 * (p * (rows // 2) + q)
                    pooled[c:c + 1, at:at + 128] = (
                        pairs[c, p, 2 * q:2 * q + 1] + pairs[c, p, 2 * q + 1:2 * q + 2]
                    )
        depth = pooled.shape[1]
        source = lax.broadcasted_iota(jnp.int32, (depth, 128), 0)
        target = lax.broadcasted_iota(jnp.int32, (depth, 128), 1)
        hit = (source // 128 * 32 + source % 128 // 2 == target) & (source % 128 < 64)
        pool = jnp.where(hit, 0.125, 0.0).astype(jnp.bfloat16)
        packet[...] = split_dot(pooled[...], pool)[:4]


def last_kernel(place, g, u3_out, u4_out, r4_out, ua, ub, f, m, faces, weight, diag,
                f4, m4, faces4, weight4, diag4, va, vb):
    count = g.shape[0]
    rows, lanes = g.shape[2:]
    shape = (rows, lanes)
    lane = lax.broadcasted_iota(jnp.int32, shape, 1)
    row = lax.broadcasted_iota(jnp.int32, shape, 0)
    x_bit, y_bit, z = lane // 64, lane // 32 % 2, lane % 32
    zero = jnp.zeros(shape, jnp.float32)

    def neighbours3(at, i):
        centre = at(i)
        flipped = pltpu.roll(centre, 64, 1)
        from_lower_row = jnp.where(row == 0, 0.0, pltpu.roll(flipped, 1, 0))
        from_upper_row = jnp.where(row == rows - 1, 0.0, pltpu.roll(flipped, rows - 1, 0))
        xl = jnp.where(x_bit == 1, flipped, from_lower_row)
        xu = jnp.where(x_bit == 0, flipped, from_upper_row)
        below = pltpu.roll(at(i - 1), lanes - 32, 1) if i > 0 else zero
        above = pltpu.roll(at(i + 1), 32, 1) if i < count - 1 else zero
        yl = jnp.where(y_bit == 1, pltpu.roll(centre, 32, 1), below)
        yu = jnp.where(y_bit == 0, pltpu.roll(centre, lanes - 32, 1), above)
        zl = jnp.where(z == 0, 0.0, pltpu.roll(centre, 1, 1))
        zu = jnp.where(z == 31, 0.0, pltpu.roll(centre, lanes - 1, 1))
        return centre, (xl, xu, yl, yu, zl, zu)

    def neighbours4(at, i):
        centre = at(i)
        xl = jnp.where(row == 0, 0.0, pltpu.roll(centre, 1, 0))
        xu = jnp.where(row == rows - 1, 0.0, pltpu.roll(centre, rows - 1, 0))
        yl = at(i - 1) if i > 0 else zero
        yu = at(i + 1) if i < count - 1 else zero
        zl = jnp.where(z < 2, 0.0, pltpu.roll(centre, 2, 1))
        zu = jnp.where(z >= 30, 0.0, pltpu.roll(centre, lanes - 2, 1))
        return centre, (xl, xu, yl, yu, zl, zu)

    def level(scale, neighbours, f_at, m_at, faces, weight, diag, ua, ub, residual):
        half = 0.5 * scale
        for i in range(count):
            centre, near = neighbours(m_at, i)
            total = jnp.full(shape, mass_term, jnp.float32)
            for k in range(6):
                face = half * (centre + near[k])
                faces[k, i] = face
                total = total + face
            diag[i] = total
            weight[i] = damping / total
            for c in range(3):
                ua[c, i] = weight[i] * f_at(c, i)
        for source, target in ((ua, ub), (ub, ua)):
            for i in range(count):
                for c in range(3):
                    centre, near = neighbours(lambda j: source[c, j], i)
                    flux = faces[0, i] * near[0]
                    for k in range(1, 6):
                        flux = flux + faces[k, i] * near[k]
                    target[c, i] = (1.0 - damping) * centre + weight[i] * (f_at(c, i) + flux)
        for i in range(count):
            for c in range(3):
                centre, near = neighbours(lambda j: ua[c, j], i)
                flux = faces[0, i] * near[0]
                for k in range(1, 6):
                    flux = flux + faces[k, i] * near[k]
                residual(c, i, f_at(c, i) + flux - diag[i] * centre)

    def pool(value):
        value = value + pltpu.roll(value, 64, 1)
        value = value + pltpu.roll(value, 32, 1)
        return 0.125 * (value + pltpu.roll(value, lanes - 1, 1))

    def to_level4(c, i, value):
        f4[c, i] = pool(value)

    level(0.25**3, neighbours3, lambda c, i: g[i, c], lambda i: g[i, 3],
          faces, weight, diag, ua, ub, to_level4)
    for i in range(count):
        m4[i] = pool(g[i, 3])

    def keep(c, i, value):
        vb[c, i] = value

    level(0.25**4, neighbours4, lambda c, i: f4[c, i], lambda i: m4[i],
          faces4, weight4, diag4, va, vb, keep)
    x_at, y_at = place[0], place[1]
    mine = row == x_at
    for c in range(3):
        u3_out[c:c + 1] = jnp.sum(jnp.where(mine, ua[c, y_at], 0.0), axis=0, keepdims=True)
        u4_out[c:c + 1] = jnp.sum(jnp.where(mine, va[c, y_at], 0.0), axis=0, keepdims=True)
        r4_out[c:c + 1] = jnp.sum(jnp.where(mine, vb[c, y_at], 0.0), axis=0, keepdims=True)


def on_chip(count):
    return [pl.BlockSpec(memory_space=pltpu.VMEM)] * count


def planes_scratch(planes, rows, lanes, own, own_rows, pooled):
    block = (planes, rows, lanes)
    return (
        [pltpu.VMEM((3,) + block, jnp.float32)] * 3
        + [pltpu.VMEM(block, jnp.float32)] * 8
        + [pltpu.VMEM((4, own // 2, own_rows, lanes), jnp.float32), pltpu.VMEM(pooled, jnp.float32)]
    )


LIMIT = pltpu.CompilerParams(vmem_limit_bytes=48 * 1024 * 1024)


def on_device(velocity_guess, forcing, cell_type, viscosities):
    f32 = jnp.float32
    viscosity = jnp.where(
        cell_type < 2,
        jnp.where(cell_type == 0, viscosities[0], viscosities[1]),
        jnp.where(cell_type == 2, viscosities[2], viscosities[3]),
    )
    own, rows, lanes = viscosity.shape
    stacked = jnp.concatenate([velocity_guess, forcing, viscosity[None]], axis=0)
    ylo = passed_along(stacked[:, :, rows - HALO:], "gy", 1)
    yhi = passed_along(stacked[:, :, :HALO], "gy", -1)

    def wide(lo, width_u, width_f, low_side):
        def layers(channels, width):
            first = own - width if low_side else 0
            chosen = slice(first, first + width)
            part = jnp.concatenate(
                [stacked[channels, chosen], yhi[channels, chosen], ylo[channels, chosen]], axis=2
            )
            return part.reshape(-1, rows + 2 * HALO, lanes)

        return jnp.concatenate(
            [layers(slice(0, 3), width_u), layers(slice(3, 6), width_f), layers(slice(6, 7), width_u)], axis=0
        )

    xlo = passed_along(wide(0, HALO, HALO - 1, True), "gx", 1)
    xhi = passed_along(wide(0, HALO, HALO - 1, False), "gx", -1)
    u0, packet = pl.pallas_call(
        fine_kernel,
        out_shape=(
            jax.ShapeDtypeStruct(velocity_guess.shape, f32),
            jax.ShapeDtypeStruct((4 * own // 2, rows // 2, lanes // 2), f32),
        ),
        in_specs=on_chip(7),
        out_specs=tuple(on_chip(2)),
        scratch_shapes=planes_scratch(
            own + 2 * HALO, rows + 2 * HALO, lanes, own, rows, (4 * own // 2, rows, 128)
        ),
        compiler_params=LIMIT,
    )(velocity_guess, forcing, viscosity, ylo, yhi, xlo, xhi)
    results = [u0]
    for grid_level in (1, 2):
        own, rows = own // 2, rows // 2
        packet = packet.reshape(4, own, rows, 128)
        valid = 256 >> grid_level
        ylo = passed_along(packet[:, :, rows - HALO:], "gy", 1)
        yhi = passed_along(packet[:, :, :HALO], "gy", -1)
        parts = [packet, yhi, ylo]
        total_rows = rows + 2 * HALO
        if total_rows % 8:
            parts = [packet, yhi, jnp.zeros_like(yhi), ylo]
            total_rows += HALO
        tall = jnp.concatenate(parts, axis=2)
        xlo = passed_along(tall[:, own - HALO:], "gx", 1)
        xhi = passed_along(tall[:, :HALO], "gx", -1)
        if grid_level == 1:
            packet_shape, pooled_shape = (4 * own // 2, rows // 2, 128), (4 * own // 2, rows, 128)
        else:
            packet_shape, pooled_shape = (4, 128), (8, 512)
        u_own, packet = pl.pallas_call(
            functools.partial(middle_kernel, 0.25**grid_level),
            out_shape=(
                jax.ShapeDtypeStruct((3, own, rows, valid), f32),
                jax.ShapeDtypeStruct(packet_shape, f32),
            ),
            in_specs=on_chip(5),
            out_specs=tuple(on_chip(2)),
            scratch_shapes=planes_scratch(own + 2 * HALO, total_rows, 128, own, rows, pooled_shape),
            compiler_params=LIMIT,
        )(packet, ylo, yhi, xlo, xhi)
        results.append(u_own)
    count_x, count_y = lax.axis_size("gx"), lax.axis_size("gy")
    column = lax.all_to_all(jnp.broadcast_to(packet[None], (count_x, 4, 128)), "gx", 0, 0)
    column = column.transpose(1, 0, 2)
    gathered = lax.all_to_all(
        jnp.broadcast_to(column[None], (count_y, 4, count_x, 128)), "gy", 0, 0
    )
    place = jnp.stack([lax.axis_index("gx"), lax.axis_index("gy")]).astype(jnp.int32)
    block = (count_y, count_x, 128)
    field, vector, six = (pltpu.VMEM(lead + block, f32) for lead in ((), (3,), (6,)))
    u3, u4, r4 = pl.pallas_call(
        last_kernel,
        out_shape=(jax.ShapeDtypeStruct((3, 128), f32),) * 3,
        in_specs=[pl.BlockSpec(memory_space=pltpu.SMEM)] + on_chip(1),
        out_specs=tuple(on_chip(3)),
        scratch_shapes=[vector, vector, vector, field, six, field, field,
                        vector, field, six, field, field, vector, vector],
        compiler_params=LIMIT,
    )(place, gathered)
    results.append(u3.reshape(3, 2, 2, 32))
    results.append(u4[:, :32:2].reshape(3, 1, 1, 16))
    return (*results, r4[:, :32:2].reshape(3, 1, 1, 16))


def solution(mesh):
    return jax.shard_map(
        on_device,
        mesh=mesh,
        in_specs=(P(None, "gx", "gy", None), P(None, "gx", "gy", None), P("gx", "gy", None), P()),
        out_specs=(P(None, "gx", "gy", None),) * 6,
        check_vma=False,
    )
```

```python
import functools

import jax
import jax.numpy as jnp
from jax import lax
from jax.experimental import pallas as pl
from jax.experimental.pallas import tpu as pltpu
from jax.sharding import PartitionSpec as P

SWEEPS = 3
LEVELS = 4
HALO = SWEEPS + 1
REACH = 5

damping = 0.8
mass_term = 0.05


def passed_round(value, axis, steps):
    count = lax.axis_size(axis)
    return lax.ppermute(value, axis, [(source, (source + steps) % count) for source in range(count)])


def split_dot(rows, pool):
    total = None
    for part in range(3):
        piece = rows.astype(jnp.bfloat16)
        term = jnp.dot(piece, pool, preferred_element_type=jnp.float32)
        total = term if total is None else total + term
        if part < 2:
            rows = rows - piece.astype(jnp.float32)
    return total


def inside_rows(place, own_rows, total_rows, shape, along_x=True):
    row = lax.broadcasted_iota(jnp.int32, shape, 0)
    above = jnp.where(place[1] < place[3] - 1, own_rows + HALO, own_rows)
    below = jnp.where(place[1] > 0, total_rows - HALO, total_rows)
    above = jnp.where(along_x, above, 0)
    below = jnp.where(along_x, below, total_rows)
    return (row < above) | (row >= below)


def pair_pool(lanes):
    source = lax.broadcasted_iota(jnp.int32, (lanes, 128), 0)
    target = lax.broadcasted_iota(jnp.int32, (lanes, 128), 1)
    return jnp.where(source // 2 == target, 0.125, 0.0).astype(jnp.bfloat16)


def make_coefficients(scale, lo, hi, m, cx, cym, cyp, czm, czp, weight, diag, unroll=False):
    rows, lanes = m.shape[1:]
    half = 0.5 * scale
    lane = lax.broadcasted_iota(jnp.int32, (rows, lanes), 1)
    cx[lo - 1] = half * (m[lo - 1] + m[lo])

    def plane(i, _):
        centre = m[i]
        upper = m[i + 1]
        y_lower = pltpu.roll(centre, 1, 0)
        y_upper = pltpu.roll(centre, rows - 1, 0)
        z_lower = jnp.where(lane == 0, 0.0, pltpu.roll(centre, 1, 1))
        z_upper = jnp.where(lane == lanes - 1, 0.0, pltpu.roll(centre, lanes - 1, 1))
        f_xl, f_xu = half * (centre + m[i - 1]), half * (centre + upper)
        f_yl, f_yu = half * (centre + y_lower), half * (centre + y_upper)
        f_zl, f_zu = half * (centre + z_lower), half * (centre + z_upper)
        total = mass_term + (f_xl + f_xu + f_yl + f_yu + f_zl + f_zu)
        cx[i] = f_xu
        cym[i], cyp[i] = f_yl, f_yu
        czm[i] = jnp.where(lane == 0, 0.0, f_zl)
        czp[i] = jnp.where(lane == lanes - 1, 0.0, f_zu)
        diag[i] = total
        weight[i] = jnp.where(centre > 0.0, damping / total, 0.0)
        return 0

    lax.fori_loop(lo, hi, plane, 0, unroll=unroll)


def flux_of(u, c, i, cx, cym, cyp, czm, czp):
    rows, lanes = u.shape[2:]
    centre = u[c, i]
    flux = cx[i - 1] * u[c, i - 1] + cx[i] * u[c, i + 1]
    flux += cym[i] * pltpu.roll(centre, 1, 0) + cyp[i] * pltpu.roll(centre, rows - 1, 0)
    flux += czm[i] * pltpu.roll(centre, 1, 1) + czp[i] * pltpu.roll(centre, lanes - 1, 1)
    return centre, flux


def relax(lo, hi, source, target, f, weight, faces, unroll=False):
    def plane(i, _):
        for c in range(3):
            centre, flux = flux_of(source, c, i, *faces)
            target[c, i] = (1.0 - damping) * centre + weight[i] * (f[c, i] + flux)
        return 0

    lax.fori_loop(lo, hi, plane, 0, unroll=unroll)


def start_from_zero(lo, hi, target, f, weight, unroll=False):
    def plane(i, _):
        for c in range(3):
            target[c, i] = weight[i] * f[c, i]
        return 0

    lax.fori_loop(lo, hi, plane, 0, unroll=unroll)


def residual_pairs(at, count, first, own_rows, u, f, m, diag, faces, pairs, unroll=False):
    def pair(p, _):
        i = at + 2 * p
        for c in range(3):
            both = None
            for j in (i, i + 1):
                centre, flux = flux_of(u, c, j, *faces)
                value = f[c, j] + flux - diag[j] * centre
                both = value if both is None else both + value
            pairs[c, first + p] = both[:own_rows]
        pairs[3, first + p] = (m[i] + m[i + 1])[:own_rows]
        return 0

    lax.fori_loop(0, count, pair, 0, unroll=unroll)


def pool_pairs(pairs, pooled):
    lanes = pairs.shape[-1]
    rows = pooled.shape[1]
    summed = split_dot(pairs[...].reshape(-1, lanes), pair_pool(lanes))
    pooled[...] = summed.reshape(pooled.shape)
    return pooled[:, pl.ds(0, rows // 2, 2), :] + pooled[:, pl.ds(1, rows // 2, 2), :]


def inner_kernel(place, u_in, f_in, m_in, ylo, yhi, u_mid, packet_mid, u_edge, f_edge, m_edge,
                 ua, ub, f, m, cx, cym, cyp, czm, czp, weight, diag, pairs, pooled):
    own, rows = u_in.shape[1:3]
    body = pl.ds(HALO, own)
    last = HALO + own
    has_lower, has_upper = place[1] > 0, place[1] < place[3] - 1
    for c in range(3):
        ua[c, body, :rows] = u_in[c]
        ua[c, body, rows:rows + HALO] = jnp.where(has_upper, yhi[c], 0.0)
        ua[c, body, rows + HALO:] = jnp.where(has_lower, ylo[c], 0.0)
        f[c, body, :rows] = f_in[c]
        f[c, body, rows:rows + HALO] = yhi[3 + c]
        f[c, body, rows + HALO:] = ylo[3 + c]
    m[body, :rows] = m_in[...]
    m[body, rows:rows + HALO] = jnp.where(has_upper, yhi[6], 0.0)
    m[body, rows + HALO:] = jnp.where(has_lower, ylo[6], 0.0)

    def edges(stage, u, depth):
        u_edge[stage, 0] = u[:, HALO + depth:HALO + depth + 2]
        u_edge[stage, 1] = u[:, last - depth - 2:last - depth]

    edges(0, ua, 0)
    f_edge[0], f_edge[1] = f[:, HALO:2 * HALO], f[:, last - HALO:last]
    m_edge[0], m_edge[1] = m[HALO:2 * HALO + 1], m[last - HALO - 1:last]
    make_coefficients(1.0, HALO + 1, last - 1, m, cx, cym, cyp, czm, czp, weight, diag)
    faces = (cx, cym, cyp, czm, czp)
    relax(HALO + 1, last - 1, ua, ub, f, weight, faces)
    edges(1, ub, 1)
    relax(HALO + 2, last - 2, ub, ua, f, weight, faces)
    edges(2, ua, 2)
    relax(HALO + 3, last - 3, ua, ub, f, weight, faces)
    edges(3, ub, 3)
    u_mid[...] = ub[:, HALO + 3:last - 3, :rows]
    residual_pairs(2 * HALO, own // 2 - HALO, 0, rows, ub, f, m, diag, faces, pairs)
    packet_mid[...] = pool_pairs(pairs, pooled)


def outer_kernel(place, u_mid, packet_mid, u_edge, f_edge, m_edge, xlo, xhi, u_out, packet,
                 ua, ub, f, m, cx, cym, cyp, czm, czp, weight, diag, pairs, pooled):
    own, rows = u_out.shape[1:3]
    planes = m.shape[1]
    count_f = HALO - 1
    at_f, at_m = 3 * HALO, 3 * HALO + 3 * count_f
    half = own // 2
    for end, halo in ((0, xlo), (1, xhi)):
        outer = 0 if end == 0 else planes - HALO
        inner = HALO if end == 0 else 0
        present = place[0] > 0 if end == 0 else place[0] < place[2] - 1
        inside = inside_rows(place, rows, m.shape[2], m.shape[2:], present)
        for c in range(3):
            ua[end, c, outer:outer + HALO] = jnp.where(inside, halo[HALO * c:HALO * (c + 1)], 0.0)
            nearest = HALO if end == 0 else planes - HALO - 2
            ua[end, c, nearest:nearest + 2] = u_edge[0, end, c]
            beyond = 1 if end == 0 else planes - HALO
            f[end, c, beyond:beyond + count_f] = halo[at_f + count_f * c:at_f + count_f * (c + 1)]
            own_f = HALO if end == 0 else planes - 2 * HALO
            f[end, c, own_f:own_f + HALO] = f_edge[end, c]
        m[end, outer:outer + HALO] = jnp.where(inside, halo[at_m:], 0.0)
        m[end, inner:inner + HALO + 1] = m_edge[end]
        parts = (cx.at[end], cym.at[end], cyp.at[end], czm.at[end], czp.at[end])
        u_a, u_b, f_e, w_e, d_e = ua.at[end], ub.at[end], f.at[end], weight.at[end], diag.at[end]
        make_coefficients(1.0, 1, planes - 1, m.at[end], *parts, w_e, d_e)
        for stage, (source, target) in enumerate(((u_a, u_b), (u_b, u_a), (u_a, u_b))):
            first = 1 + stage if end == 0 else planes - 1 - HALO - stage
            relax(first, first + HALO, source, target, f_e, w_e, parts)
            known = first + HALO if end == 0 else first - 2
            for c in range(3):
                target[c, known:known + 2] = u_edge[stage + 1, end, c]
        at = HALO if end == 0 else 1
        residual_pairs(at, HALO // 2, HALO // 2 * end, rows, u_b, f_e, m.at[end], d_e, parts, pairs)
        for c in range(3):
            if end == 0:
                u_out[c, :HALO - 1] = ub[end, c, HALO:2 * HALO - 1, :rows]
            else:
                u_out[c, own - HALO + 1:] = ub[end, c, planes - 2 * HALO + 1:planes - HALO, :rows]
    u_out[:, HALO - 1:own - HALO + 1] = u_mid[...]
    ends = pool_pairs(pairs, pooled)
    for c in range(4):
        at = HALO * c
        packet[half * c:half * c + 2] = ends[at:at + 2]
        packet[half * c + 2:half * (c + 1) - 2] = packet_mid[(half - HALO) * c:(half - HALO) * (c + 1)]
        packet[half * (c + 1) - 2:half * (c + 1)] = ends[at + 2:at + 4]


def middle_kernel(scale, place, p_in, ylo, yhi, xlo, xhi, u_out, packet,
                  ua, ub, f, m, cx, cym, cyp, czm, czp, weight, diag, pairs, pooled):
    own, rows = p_in.shape[1:3]
    body = pl.ds(HALO, own)
    planes = own + 2 * HALO
    total_rows = m.shape[1]
    for c in range(4):
        if c < 3:
            field = f.at[c]
        else:
            field = m
        if total_rows > rows + 2 * HALO:
            field[body] = jnp.zeros((own,) + m.shape[1:], jnp.float32)
        field[body, :rows] = p_in[c]
        field[body, rows:rows + HALO] = yhi[c]
        field[body, total_rows - HALO:] = ylo[c]
        field[:HALO] = xlo[c]
        field[HALO + own:] = xhi[c]
    shape = m.shape[1:]
    in_rows = inside_rows(place, rows, total_rows, shape)
    in_lower = inside_rows(place, rows, total_rows, shape, place[0] > 0)
    in_upper = inside_rows(place, rows, total_rows, shape, place[0] < place[2] - 1)
    m[body] = jnp.where(in_rows, m[body], 0.0)
    m[:HALO] = jnp.where(in_lower, m[:HALO], 0.0)
    m[HALO + own:] = jnp.where(in_upper, m[HALO + own:], 0.0)
    make_coefficients(scale, 1, planes - 1, m, cx, cym, cyp, czm, czp, weight, diag, unroll=True)
    faces = (cx, cym, cyp, czm, czp)
    start_from_zero(1, planes - 1, ub, f, weight, unroll=True)
    relax(2, planes - 2, ub, ua, f, weight, faces, unroll=True)
    relax(3, planes - 3, ua, ub, f, weight, faces, unroll=True)
    lanes = u_out.shape[-1]
    for c in range(3):
        u_out[c] = ub[c, body, :rows, :lanes]
    residual_pairs(HALO, own // 2, 0, rows, ub, f, m, diag, faces, pairs, unroll=True)
    if rows > 4:
        packet[...] = pool_pairs(pairs, pooled)
    else:
        for c in range(4):
            for p in range(own // 2):
                for q in range(rows // 2):
                    at = 128 * (p * (rows // 2) + q)
                    pooled[c:c + 1, at:at + 128] = (
                        pairs[c, p, 2 * q:2 * q + 1] + pairs[c, p, 2 * q + 1:2 * q + 2]
                    )
        depth = pooled.shape[1]
        source = lax.broadcasted_iota(jnp.int32, (depth, 128), 0)
        target = lax.broadcasted_iota(jnp.int32, (depth, 128), 1)
        hit = (source // 128 * 32 + source % 128 // 2 == target) & (source % 128 < 64)
        pool = jnp.where(hit, 0.125, 0.0).astype(jnp.bfloat16)
        packet[...] = split_dot(pooled[...], pool)[:4]


def last_kernel(place, g, u3_out, u4_out, r4_out, fw, mw, ua, ub, faces, weight, diag,
                f4, m4, faces4, weight4, diag4, va, vb, rows_out):
    count = g.shape[0]
    rows, lanes = g.shape[2:]
    shape = (rows, lanes)
    lane = lax.broadcasted_iota(jnp.int32, shape, 1)
    row = lax.broadcasted_iota(jnp.int32, shape, 0)
    x_one, y_one, z = lane // 64 == 1, lane // 32 % 2 == 1, lane % 32
    first_row, last_row = row == 0, row == rows - 1
    zero = jnp.zeros(shape, jnp.float32)
    x_at, y_at = place[0], place[1]
    window = 2 * REACH + 1
    for w in range(window):
        i = y_at + (w - REACH)
        inside = (i >= 0) & (i < count)
        i = jnp.clip(i, 0, count - 1)
        for c in range(3):
            fw[c, w] = jnp.where(inside, g[i, c], 0.0)
        mw[w] = jnp.where(inside, g[i, 3], 0.0)

    def shifted_rows(value):
        return pltpu.roll(value, 1, 0), pltpu.roll(value, rows - 1, 0)

    def near3(get, w):
        centre = get(w)
        other = pltpu.roll(centre, 64, 1)
        lower, upper = shifted_rows(other)
        x_out = jnp.where(x_one, upper, lower)
        y_in = jnp.where(y_one, pltpu.roll(centre, 32, 1), pltpu.roll(centre, lanes - 32, 1))
        below = pltpu.roll(get(w - 1), lanes - 32, 1) if w > 0 else zero
        above = pltpu.roll(get(w + 1), 32, 1) if w < window - 1 else zero
        y_out = jnp.where(y_one, above, below)
        return centre, (other, x_out, y_in, y_out, pltpu.roll(centre, 1, 1), pltpu.roll(centre, lanes - 1, 1))

    x_edge = (x_one & last_row) | (jnp.logical_not(x_one) & first_row)
    outside3 = (None, x_edge, None, None, z == 0, z == 31)

    def near4(get, w):
        centre = get(w)
        lower, upper = shifted_rows(centre)
        return centre, (lower, upper, get(w - 1), get(w + 1),
                        pltpu.roll(centre, 2, 1), pltpu.roll(centre, lanes - 2, 1))

    outside4 = (first_row, last_row, None, None, z < 2, z >= 30)

    def level(scale, near, outside, f, m, faces, weight, diag, ua, ub, spans, residual):
        half = 0.5 * scale
        for w in spans[0]:
            centre, sides = near(lambda j: m[j], w)
            total = jnp.full(shape, mass_term, jnp.float32)
            for k in range(6):
                side = sides[k] if outside[k] is None else jnp.where(outside[k], 0.0, sides[k])
                face = half * (centre + side)
                total = total + face
                faces[k, w] = face if outside[k] is None else jnp.where(outside[k], 0.0, face)
            diag[w] = total
            weight[w] = jnp.where(centre > 0.0, damping / total, 0.0)
            for c in range(3):
                ua[c, w] = weight[w] * f[c, w]

        def flux_at(u, c, w):
            centre, sides = near(lambda j: u[c, j], w)
            flux = faces[0, w] * sides[0]
            for k in range(1, 6):
                flux = flux + faces[k, w] * sides[k]
            return centre, flux

        for source, target, span in ((ua, ub, spans[1]), (ub, ua, spans[2])):
            for w in span:
                for c in range(3):
                    centre, flux = flux_at(source, c, w)
                    target[c, w] = (1.0 - damping) * centre + weight[w] * (f[c, w] + flux)
        for w in spans[3]:
            for c in range(3):
                centre, flux = flux_at(ua, c, w)
                residual(c, w, f[c, w] + flux - diag[w] * centre)

    def pool(value):
        value = value + pltpu.roll(value, 64, 1)
        value = value + pltpu.roll(value, 32, 1)
        return 0.125 * (value + pltpu.roll(value, lanes - 1, 1))

    def to_level4(c, w, value):
        f4[c, w] = pool(value)

    spans = (range(window), range(1, window - 1), range(1, window - 1), range(2, window - 2))
    level(0.25**3, near3, outside3, fw, mw, faces, weight, diag, ua, ub, spans, to_level4)
    for w in range(1, window - 1):
        m4[w] = pool(mw[w])
    mine = row == x_at

    def own_row(value):
        return jnp.sum(jnp.where(mine, value, 0.0), axis=0, keepdims=True)

    def keep(c, w, value):
        rows_out[3 + c:4 + c] = own_row(value)

    spans = tuple(range(2 + k, window - 2 - k) for k in range(4))
    level(0.25**4, near4, outside4, f4, m4, faces4, weight4, diag4, va, vb, spans, keep)
    for c in range(3):
        value = own_row(ua[c, REACH])
        rows_out[c:c + 1] = own_row(va[c, REACH])
        for k in range(4):
            turned = value if k == 0 else pltpu.roll(value, lanes - 32 * k, 1)
            u3_out[c, k // 2, k % 2:k % 2 + 1] = turned[:, :32]
    source = lax.broadcasted_iota(jnp.int32, (lanes, lanes), 0)
    target = lax.broadcasted_iota(jnp.int32, (lanes, lanes), 1)
    take = jnp.where((source == 2 * target) & (target < 16), 1.0, 0.0).astype(jnp.bfloat16)
    ends = split_dot(rows_out[...], take)
    for c in range(3):
        u4_out[c, 0] = ends[c:c + 1, :16]
        r4_out[c, 0] = ends[3 + c:4 + c, :16]


def pack_kernel(viscosities, u_in, f_in, types, up, down, viscosity):
    rows = u_in.shape[2]
    kind = types[...]
    value = jnp.where(
        kind < 2,
        jnp.where(kind == 0, viscosities[0], viscosities[1]),
        jnp.where(kind == 2, viscosities[2], viscosities[3]),
    )
    viscosity[...] = value
    for c in range(3):
        up[c], down[c] = u_in[c, :, rows - HALO:], u_in[c, :, :HALO]
        up[3 + c], down[3 + c] = f_in[c, :, rows - HALO:], f_in[c, :, :HALO]
    up[6], down[6] = value[:, rows - HALO:], value[:, :HALO]


def on_chip(count):
    return [pl.BlockSpec(memory_space=pltpu.VMEM)] * count


def planes_scratch(planes, rows, lanes, pairs, own_rows, pooled, ends=()):
    block = (planes, rows, lanes)
    return (
        [pltpu.VMEM(ends + (3,) + block, jnp.float32)] * 3
        + [pltpu.VMEM(ends + block, jnp.float32)] * 8
        + [pltpu.VMEM((4, pairs, own_rows, lanes), jnp.float32), pltpu.VMEM(pooled, jnp.float32)]
    )


LIMIT = pltpu.CompilerParams(vmem_limit_bytes=20 * 1024 * 1024)


def on_device(velocity_guess, forcing, cell_type, viscosities):
    f32 = jnp.float32
    count_x, count_y = lax.axis_size("gx"), lax.axis_size("gy")
    place = jnp.stack([lax.axis_index("gx"), lax.axis_index("gy"), count_x, count_y]).astype(jnp.int32)
    in_smem = [pl.BlockSpec(memory_space=pltpu.SMEM)]
    own, rows, lanes = cell_type.shape
    edge = jax.ShapeDtypeStruct((7, own, HALO, lanes), f32)
    up, down, viscosity = pl.pallas_call(
        pack_kernel,
        out_shape=(edge, edge, jax.ShapeDtypeStruct(cell_type.shape, f32)),
        in_specs=in_smem + on_chip(3),
        out_specs=tuple(on_chip(3)),
        compiler_params=LIMIT,
    )(viscosities, velocity_guess, forcing, cell_type)
    ylo = passed_round(up, "gy", 1)
    yhi = passed_round(down, "gy", -1)

    def wide(first, *inner):
        def layers(own_part, at, layer):
            part = jnp.concatenate([own_part[:, layer], yhi[at, layer], ylo[at, layer]], axis=2)
            return part.reshape(-1, rows + 2 * HALO, lanes)

        return jnp.concatenate(
            [
                layers(velocity_guess, slice(0, 3), slice(first, first + HALO)),
                layers(forcing, slice(3, 6), slice(*inner)),
                layers(viscosity[None], slice(6, 7), slice(first, first + HALO)),
            ],
            axis=0,
        )

    xlo = passed_round(wide(own - HALO, own - HALO + 1, own), "gx", 1)
    xhi = passed_round(wide(0, 0, HALO - 1), "gx", -1)
    tall = rows + 2 * HALO
    middle = own // 2 - HALO
    state = (
        (3, own - 2 * HALO + 2, rows, lanes),
        (4 * middle, rows // 2, lanes // 2),
        (4, 2, 3, 2, tall, lanes),
        (2, 3, HALO, tall, lanes),
        (2, HALO + 1, tall, lanes),
    )
    known = pl.pallas_call(
        inner_kernel,
        out_shape=tuple(jax.ShapeDtypeStruct(shape, f32) for shape in state),
        in_specs=in_smem + on_chip(5),
        out_specs=tuple(on_chip(5)),
        scratch_shapes=planes_scratch(own + 2 * HALO, tall, lanes, middle, rows, (4 * middle, rows, 128)),
        compiler_params=LIMIT,
        cost_estimate=pl.CostEstimate(flops=60_000_000, bytes_accessed=6_000_000, transcendentals=0),
    )(place, velocity_guess, forcing, viscosity, ylo, yhi)
    u0, packet = pl.pallas_call(
        outer_kernel,
        out_shape=(
            jax.ShapeDtypeStruct(velocity_guess.shape, f32),
            jax.ShapeDtypeStruct((4 * own // 2, rows // 2, lanes // 2), f32),
        ),
        in_specs=in_smem + on_chip(7),
        out_specs=tuple(on_chip(2)),
        scratch_shapes=planes_scratch(2 * HALO + 1, tall, lanes, HALO, rows, (4 * HALO, rows, 128), (2,)),
        compiler_params=LIMIT,
    )(place, *known, xlo, xhi)
    results = [u0]
    for grid_level in (1, 2):
        own, rows = own // 2, rows // 2
        packet = packet.reshape(4, own, rows, 128)
        valid = 256 >> grid_level
        ylo = passed_round(packet[:, :, rows - HALO:], "gy", 1)
        yhi = passed_round(packet[:, :, :HALO], "gy", -1)
        parts = [packet, yhi, ylo]
        total_rows = rows + 2 * HALO
        if total_rows % 8:
            parts = [packet, yhi, jnp.zeros_like(yhi), ylo]
            total_rows += HALO
        tall = jnp.concatenate(parts, axis=2)
        xlo = passed_round(tall[:, own - HALO:], "gx", 1)
        xhi = passed_round(tall[:, :HALO], "gx", -1)
        if grid_level == 1:
            packet_shape, pooled_shape = (4 * own // 2, rows // 2, 128), (4 * own // 2, rows, 128)
        else:
            packet_shape, pooled_shape = (4, 128), (8, 512)
        u_own, packet = pl.pallas_call(
            functools.partial(middle_kernel, 0.25**grid_level),
            out_shape=(
                jax.ShapeDtypeStruct((3, own, rows, valid), f32),
                jax.ShapeDtypeStruct(packet_shape, f32),
            ),
            in_specs=in_smem + on_chip(5),
            out_specs=tuple(on_chip(2)),
            scratch_shapes=planes_scratch(own + 2 * HALO, total_rows, 128, own // 2, rows, pooled_shape),
            compiler_params=LIMIT,
        )(place, packet, ylo, yhi, xlo, xhi)
        results.append(u_own)
    column = lax.all_to_all(jnp.broadcast_to(packet[None], (count_x, 4, 128)), "gx", 0, 0)
    column = column.transpose(1, 0, 2)
    gathered = lax.all_to_all(
        jnp.broadcast_to(column[None], (count_y, 4, count_x, 128)), "gy", 0, 0
    )
    block = (2 * REACH + 1, count_x, 128)
    field, vector, six = (pltpu.VMEM(lead + block, f32) for lead in ((), (3,), (6,)))
    last = pl.pallas_call(
        last_kernel,
        out_shape=tuple(jax.ShapeDtypeStruct(shape, f32) for shape in ((3, 2, 2, 32), (3, 1, 1, 16), (3, 1, 1, 16))),
        in_specs=in_smem + on_chip(1),
        out_specs=tuple(on_chip(3)),
        scratch_shapes=[vector, field, vector, vector, six, field, field,
                        vector, field, six, field, field, vector, vector, pltpu.VMEM((8, 128), f32)],
        compiler_params=LIMIT,
    )(place, gathered)
    return (*results, *last)


def solution(mesh):
    return jax.shard_map(
        on_device,
        mesh=mesh,
        in_specs=(P(None, "gx", "gy", None), P(None, "gx", "gy", None), P("gx", "gy", None), P()),
        out_specs=(P(None, "gx", "gy", None),) * 6,
        check_vma=False,
    )
```

```python
import functools

import jax
import jax.numpy as jnp
from jax import lax
from jax.experimental import pallas as pl
from jax.experimental.pallas import tpu as pltpu
from jax.sharding import PartitionSpec as P

SWEEPS = 3
LEVELS = 4
HALO = SWEEPS + 1
REACH = 5

damping = 0.8
mass_term = 0.05


def passed_round(value, axis, steps):
    count = lax.axis_size(axis)
    return lax.ppermute(value, axis, [(source, (source + steps) % count) for source in range(count)])


def split_dot(rows, pool):
    total = None
    for part in range(3):
        piece = rows.astype(jnp.bfloat16)
        term = jnp.dot(piece, pool, preferred_element_type=jnp.float32)
        total = term if total is None else total + term
        if part < 2:
            rows = rows - piece.astype(jnp.float32)
    return total


def inside_rows(place, own_rows, total_rows, shape, along_x=True):
    row = lax.broadcasted_iota(jnp.int32, shape, 0)
    above = jnp.where(place[1] < place[3] - 1, own_rows + HALO, own_rows)
    below = jnp.where(place[1] > 0, total_rows - HALO, total_rows)
    above = jnp.where(along_x, above, 0)
    below = jnp.where(along_x, below, total_rows)
    return (row < above) | (row >= below)


def pair_pool(lanes):
    source = lax.broadcasted_iota(jnp.int32, (lanes, 128), 0)
    target = lax.broadcasted_iota(jnp.int32, (lanes, 128), 1)
    return jnp.where(source // 2 == target, 0.125, 0.0).astype(jnp.bfloat16)


def make_coefficients(scale, lo, hi, m, cx, cym, cyp, czm, czp, weight, diag, unroll=False):
    rows, lanes = m.shape[1:]
    half = 0.5 * scale
    lane = lax.broadcasted_iota(jnp.int32, (rows, lanes), 1)
    cx[lo - 1] = half * (m[lo - 1] + m[lo])

    def plane(i, _):
        centre = m[i]
        upper = m[i + 1]
        y_lower = pltpu.roll(centre, 1, 0)
        y_upper = pltpu.roll(centre, rows - 1, 0)
        z_lower = jnp.where(lane == 0, 0.0, pltpu.roll(centre, 1, 1))
        z_upper = jnp.where(lane == lanes - 1, 0.0, pltpu.roll(centre, lanes - 1, 1))
        f_xl, f_xu = half * (centre + m[i - 1]), half * (centre + upper)
        f_yl, f_yu = half * (centre + y_lower), half * (centre + y_upper)
        f_zl, f_zu = half * (centre + z_lower), half * (centre + z_upper)
        total = mass_term + (f_xl + f_xu + f_yl + f_yu + f_zl + f_zu)
        cx[i] = f_xu
        cym[i], cyp[i] = f_yl, f_yu
        czm[i] = jnp.where(lane == 0, 0.0, f_zl)
        czp[i] = jnp.where(lane == lanes - 1, 0.0, f_zu)
        diag[i] = total
        weight[i] = jnp.where(centre > 0.0, damping / total, 0.0)
        return 0

    lax.fori_loop(lo, hi, plane, 0, unroll=unroll)


def flux_of(u, c, i, cx, cym, cyp, czm, czp):
    rows, lanes = u.shape[2:]
    centre = u[c, i]
    flux = cx[i - 1] * u[c, i - 1] + cx[i] * u[c, i + 1]
    flux += cym[i] * pltpu.roll(centre, 1, 0) + cyp[i] * pltpu.roll(centre, rows - 1, 0)
    flux += czm[i] * pltpu.roll(centre, 1, 1) + czp[i] * pltpu.roll(centre, lanes - 1, 1)
    return centre, flux


def relax(lo, hi, source, target, f, weight, faces, unroll=False):
    def plane(i, _):
        for c in range(3):
            centre, flux = flux_of(source, c, i, *faces)
            target[c, i] = (1.0 - damping) * centre + weight[i] * (f[c, i] + flux)
        return 0

    lax.fori_loop(lo, hi, plane, 0, unroll=unroll)


def start_from_zero(lo, hi, target, f, weight, unroll=False):
    def plane(i, _):
        for c in range(3):
            target[c, i] = weight[i] * f[c, i]
        return 0

    lax.fori_loop(lo, hi, plane, 0, unroll=unroll)


def residual_pairs(at, count, first, own_rows, u, f, m, diag, faces, pairs, unroll=False):
    def pair(p, _):
        i = at + 2 * p
        for c in range(3):
            both = None
            for j in (i, i + 1):
                centre, flux = flux_of(u, c, j, *faces)
                value = f[c, j] + flux - diag[j] * centre
                both = value if both is None else both + value
            pairs[c, first + p] = both[:own_rows]
        pairs[3, first + p] = (m[i] + m[i + 1])[:own_rows]
        return 0

    lax.fori_loop(0, count, pair, 0, unroll=unroll)


def pool_pairs(pairs, pooled):
    lanes = pairs.shape[-1]
    rows = pooled.shape[1]
    summed = split_dot(pairs[...].reshape(-1, lanes), pair_pool(lanes))
    pooled[...] = summed.reshape(pooled.shape)
    return pooled[:, pl.ds(0, rows // 2, 2), :] + pooled[:, pl.ds(1, rows // 2, 2), :]


def inner_kernel(place, viscosities, u_in, f_in, types, ylo, yhi, u_mid, packet_mid, u_edge, f_edge, m_edge,
                 ua, ub, f, m, cx, cym, cyp, czm, czp, weight, diag, pairs, pooled):
    own, rows = u_in.shape[1:3]
    body = pl.ds(HALO, own)
    last = HALO + own
    has_lower, has_upper = place[1] > 0, place[1] < place[3] - 1
    for c in range(3):
        ua[c, body, :rows] = u_in[c]
        ua[c, body, rows:rows + HALO] = jnp.where(has_upper, yhi[c], 0.0)
        ua[c, body, rows + HALO:] = jnp.where(has_lower, ylo[c], 0.0)
        f[c, body, :rows] = f_in[c]
        f[c, body, rows:rows + HALO] = yhi[3 + c]
        f[c, body, rows + HALO:] = ylo[3 + c]
    m[body, :rows] = viscosity_of(types[...], viscosities)
    m[body, rows:rows + HALO] = jnp.where(has_upper, yhi[6], 0.0)
    m[body, rows + HALO:] = jnp.where(has_lower, ylo[6], 0.0)

    def edges(stage, u, depth):
        u_edge[stage, 0] = u[:, HALO + depth:HALO + depth + 2]
        u_edge[stage, 1] = u[:, last - depth - 2:last - depth]

    edges(0, ua, 0)
    f_edge[0], f_edge[1] = f[:, HALO:2 * HALO], f[:, last - HALO:last]
    m_edge[0], m_edge[1] = m[HALO:2 * HALO + 1], m[last - HALO - 1:last]
    make_coefficients(1.0, HALO + 1, last - 1, m, cx, cym, cyp, czm, czp, weight, diag, True)
    faces = (cx, cym, cyp, czm, czp)
    relax(HALO + 1, last - 1, ua, ub, f, weight, faces, True)
    edges(1, ub, 1)
    relax(HALO + 2, last - 2, ub, ua, f, weight, faces, True)
    edges(2, ua, 2)
    relax(HALO + 3, last - 3, ua, ub, f, weight, faces, True)
    edges(3, ub, 3)
    u_mid[...] = ub[:, HALO + 3:last - 3, :rows]
    residual_pairs(2 * HALO, own // 2 - HALO, 0, rows, ub, f, m, diag, faces, pairs, True)
    packet_mid[...] = pool_pairs(pairs, pooled)


def outer_kernel(place, u_mid, packet_mid, u_edge, f_edge, m_edge, xlo, xhi, clo, chi, u_out, packet,
                 ua, ub, f, m, cx, cym, cyp, czm, czp, weight, diag, pairs, pooled):
    own, rows = u_out.shape[1:3]
    planes = m.shape[1]
    count_f = HALO - 1
    at_f, at_m = 3 * HALO, 3 * HALO + 3 * count_f
    half = own // 2
    corner_shape = clo.shape[1:]
    for end, halo, corner in ((0, xlo, clo), (1, xhi, chi)):
        outer = 0 if end == 0 else planes - HALO
        inner = HALO if end == 0 else 0
        present = place[0] > 0 if end == 0 else place[0] < place[2] - 1
        inside = inside_rows(place, 0, 2 * HALO, corner_shape, present)

        def put_corner(field, channel, masked):
            at, deep = corner_layers(channel)
            value = corner[at:at + deep]
            if masked:
                value = jnp.where(inside, value, 0.0)
            first = HALO - deep if end == 0 else planes - HALO
            field[first:first + deep, rows:] = value
            far = first - 1 if end == 0 else first + deep
            field[far, rows:] = jnp.zeros(corner_shape, jnp.float32)

        for c in range(3):
            ua[end, c, outer:outer + HALO, :rows] = jnp.where(present, halo[HALO * c:HALO * (c + 1)], 0.0)
            put_corner(ua.at[end, c], c, True)
            nearest = HALO if end == 0 else planes - HALO - 2
            ua[end, c, nearest:nearest + 2] = u_edge[0, end, c]
            beyond = 1 if end == 0 else planes - HALO
            f[end, c, beyond:beyond + count_f, :rows] = halo[at_f + count_f * c:at_f + count_f * (c + 1)]
            put_corner(f.at[end, c], 3 + c, False)
            own_f = HALO if end == 0 else planes - 2 * HALO
            f[end, c, own_f:own_f + HALO] = f_edge[end, c]
        m[end, outer:outer + HALO, :rows] = jnp.where(present, halo[at_m:], 0.0)
        put_corner(m.at[end], 6, True)
        m[end, inner:inner + HALO + 1] = m_edge[end]
        parts = (cx.at[end], cym.at[end], cyp.at[end], czm.at[end], czp.at[end])
        u_a, u_b, f_e, w_e, d_e = ua.at[end], ub.at[end], f.at[end], weight.at[end], diag.at[end]
        make_coefficients(1.0, 1, planes - 1, m.at[end], *parts, w_e, d_e, True)
        for stage, (source, target) in enumerate(((u_a, u_b), (u_b, u_a), (u_a, u_b))):
            first = 1 + stage if end == 0 else planes - 1 - HALO - stage
            relax(first, first + HALO, source, target, f_e, w_e, parts, True)
            known = first + HALO if end == 0 else first - 2
            for c in range(3):
                target[c, known:known + 2] = u_edge[stage + 1, end, c]
        at = HALO if end == 0 else 1
        residual_pairs(at, HALO // 2, HALO // 2 * end, rows, u_b, f_e, m.at[end], d_e, parts, pairs, True)
        for c in range(3):
            if end == 0:
                u_out[c, :HALO - 1] = ub[end, c, HALO:2 * HALO - 1, :rows]
            else:
                u_out[c, own - HALO + 1:] = ub[end, c, planes - 2 * HALO + 1:planes - HALO, :rows]
    u_out[:, HALO - 1:own - HALO + 1] = u_mid[...]
    ends = pool_pairs(pairs, pooled)
    for c in range(4):
        at = HALO * c
        packet[half * c:half * c + 2] = ends[at:at + 2]
        packet[half * c + 2:half * (c + 1) - 2] = packet_mid[(half - HALO) * c:(half - HALO) * (c + 1)]
        packet[half * (c + 1) - 2:half * (c + 1)] = ends[at + 2:at + 4]


def middle_kernel(scale, place, p_in, ylo, yhi, xlo, xhi, u_out, packet,
                  ua, ub, f, m, cx, cym, cyp, czm, czp, weight, diag, pairs, pooled):
    own, rows = p_in.shape[1:3]
    body = pl.ds(HALO, own)
    planes = own + 2 * HALO
    total_rows = m.shape[1]
    for c in range(4):
        if c < 3:
            field = f.at[c]
        else:
            field = m
        if total_rows > rows + 2 * HALO:
            field[body] = jnp.zeros((own,) + m.shape[1:], jnp.float32)
        field[body, :rows] = p_in[c]
        field[body, rows:rows + HALO] = yhi[c]
        field[body, total_rows - HALO:] = ylo[c]
        field[:HALO] = xlo[c]
        field[HALO + own:] = xhi[c]
    shape = m.shape[1:]
    in_rows = inside_rows(place, rows, total_rows, shape)
    in_lower = inside_rows(place, rows, total_rows, shape, place[0] > 0)
    in_upper = inside_rows(place, rows, total_rows, shape, place[0] < place[2] - 1)
    m[body] = jnp.where(in_rows, m[body], 0.0)
    m[:HALO] = jnp.where(in_lower, m[:HALO], 0.0)
    m[HALO + own:] = jnp.where(in_upper, m[HALO + own:], 0.0)
    make_coefficients(scale, 1, planes - 1, m, cx, cym, cyp, czm, czp, weight, diag, unroll=True)
    faces = (cx, cym, cyp, czm, czp)
    start_from_zero(1, planes - 1, ub, f, weight, unroll=True)
    relax(2, planes - 2, ub, ua, f, weight, faces, unroll=True)
    relax(3, planes - 3, ua, ub, f, weight, faces, unroll=True)
    lanes = u_out.shape[-1]
    for c in range(3):
        u_out[c] = ub[c, body, :rows, :lanes]
    residual_pairs(HALO, own // 2, 0, rows, ub, f, m, diag, faces, pairs, unroll=True)
    if rows > 4:
        packet[...] = pool_pairs(pairs, pooled)
    else:
        for c in range(4):
            for p in range(own // 2):
                for q in range(rows // 2):
                    at = 128 * (p * (rows // 2) + q)
                    pooled[c:c + 1, at:at + 128] = (
                        pairs[c, p, 2 * q:2 * q + 1] + pairs[c, p, 2 * q + 1:2 * q + 2]
                    )
        depth = pooled.shape[1]
        source = lax.broadcasted_iota(jnp.int32, (depth, 128), 0)
        target = lax.broadcasted_iota(jnp.int32, (depth, 128), 1)
        hit = (source // 128 * 32 + source % 128 // 2 == target) & (source % 128 < 64)
        pool = jnp.where(hit, 0.125, 0.0).astype(jnp.bfloat16)
        packet[...] = split_dot(pooled[...], pool)[:4]


def last_kernel(place, g, u3_out, u4_out, r4_out, fw, mw, ua, ub, faces, weight, diag,
                f4, m4, faces4, weight4, diag4, va, vb, rows_out):
    count = g.shape[0]
    rows, lanes = g.shape[2:]
    shape = (rows, lanes)
    lane = lax.broadcasted_iota(jnp.int32, shape, 1)
    row = lax.broadcasted_iota(jnp.int32, shape, 0)
    x_one, y_one, z = lane // 64 == 1, lane // 32 % 2 == 1, lane % 32
    first_row, last_row = row == 0, row == rows - 1
    zero = jnp.zeros(shape, jnp.float32)
    x_at, y_at = place[0], place[1]
    window = 2 * REACH + 1
    for w in range(window):
        i = y_at + (w - REACH)
        inside = (i >= 0) & (i < count)
        i = jnp.clip(i, 0, count - 1)
        for c in range(3):
            fw[c, w] = jnp.where(inside, g[i, c], 0.0)
        mw[w] = jnp.where(inside, g[i, 3], 0.0)

    def shifted_rows(value):
        return pltpu.roll(value, 1, 0), pltpu.roll(value, rows - 1, 0)

    def near3(get, w):
        centre = get(w)
        other = pltpu.roll(centre, 64, 1)
        lower, upper = shifted_rows(other)
        x_out = jnp.where(x_one, upper, lower)
        y_in = jnp.where(y_one, pltpu.roll(centre, 32, 1), pltpu.roll(centre, lanes - 32, 1))
        below = pltpu.roll(get(w - 1), lanes - 32, 1) if w > 0 else zero
        above = pltpu.roll(get(w + 1), 32, 1) if w < window - 1 else zero
        y_out = jnp.where(y_one, above, below)
        return centre, (other, x_out, y_in, y_out, pltpu.roll(centre, 1, 1), pltpu.roll(centre, lanes - 1, 1))

    x_edge = (x_one & last_row) | (jnp.logical_not(x_one) & first_row)
    outside3 = (None, x_edge, None, None, z == 0, z == 31)

    def near4(get, w):
        centre = get(w)
        lower, upper = shifted_rows(centre)
        return centre, (lower, upper, get(w - 1), get(w + 1),
                        pltpu.roll(centre, 2, 1), pltpu.roll(centre, lanes - 2, 1))

    outside4 = (first_row, last_row, None, None, z < 2, z >= 30)

    def level(scale, near, outside, f, m, faces, weight, diag, ua, ub, spans, residual):
        half = 0.5 * scale
        for w in spans[0]:
            centre, sides = near(lambda j: m[j], w)
            total = jnp.full(shape, mass_term, jnp.float32)
            for k in range(6):
                side = sides[k] if outside[k] is None else jnp.where(outside[k], 0.0, sides[k])
                face = half * (centre + side)
                total = total + face
                faces[k, w] = face if outside[k] is None else jnp.where(outside[k], 0.0, face)
            diag[w] = total
            weight[w] = jnp.where(centre > 0.0, damping / total, 0.0)
            for c in range(3):
                ua[c, w] = weight[w] * f[c, w]

        def flux_at(u, c, w):
            centre, sides = near(lambda j: u[c, j], w)
            flux = faces[0, w] * sides[0]
            for k in range(1, 6):
                flux = flux + faces[k, w] * sides[k]
            return centre, flux

        for source, target, span in ((ua, ub, spans[1]), (ub, ua, spans[2])):
            for w in span:
                for c in range(3):
                    centre, flux = flux_at(source, c, w)
                    target[c, w] = (1.0 - damping) * centre + weight[w] * (f[c, w] + flux)
        for w in spans[3]:
            for c in range(3):
                centre, flux = flux_at(ua, c, w)
                residual(c, w, f[c, w] + flux - diag[w] * centre)

    def pool(value):
        value = value + pltpu.roll(value, 64, 1)
        value = value + pltpu.roll(value, 32, 1)
        return 0.125 * (value + pltpu.roll(value, lanes - 1, 1))

    def to_level4(c, w, value):
        f4[c, w] = pool(value)

    spans = (range(window), range(1, window - 1), range(1, window - 1), range(2, window - 2))
    level(0.25**3, near3, outside3, fw, mw, faces, weight, diag, ua, ub, spans, to_level4)
    for w in range(1, window - 1):
        m4[w] = pool(mw[w])
    mine = row == x_at

    def own_row(value):
        return jnp.sum(jnp.where(mine, value, 0.0), axis=0, keepdims=True)

    def keep(c, w, value):
        rows_out[3 + c:4 + c] = own_row(value)

    spans = tuple(range(2 + k, window - 2 - k) for k in range(4))
    level(0.25**4, near4, outside4, f4, m4, faces4, weight4, diag4, va, vb, spans, keep)
    for c in range(3):
        value = own_row(ua[c, REACH])
        rows_out[c:c + 1] = own_row(va[c, REACH])
        for k in range(4):
            turned = value if k == 0 else pltpu.roll(value, lanes - 32 * k, 1)
            u3_out[c, k // 2, k % 2:k % 2 + 1] = turned[:, :32]
    source = lax.broadcasted_iota(jnp.int32, (lanes, lanes), 0)
    target = lax.broadcasted_iota(jnp.int32, (lanes, lanes), 1)
    take = jnp.where((source == 2 * target) & (target < 16), 1.0, 0.0).astype(jnp.bfloat16)
    ends = split_dot(rows_out[...], take)
    for c in range(3):
        u4_out[c, 0] = ends[c:c + 1, :16]
        r4_out[c, 0] = ends[3 + c:4 + c, :16]


def viscosity_of(kind, viscosities):
    return jnp.where(
        kind < 2,
        jnp.where(kind == 0, viscosities[0], viscosities[1]),
        jnp.where(kind == 2, viscosities[2], viscosities[3]),
    )


def pack_kernel(viscosities, u_in, f_in, types, y_up, y_down, x_up, x_down, kinds, done):
    own, rows = types.shape[:2]
    pairs = [(types, kinds)]
    at = 3 * HALO
    for c in range(3):
        for k, field in ((0, u_in), (3, f_in)):
            pairs.append((field.at[c, :, pl.ds(rows - HALO, HALO)], y_up.at[k + c]))
            pairs.append((field.at[c, :, pl.ds(0, HALO)], y_down.at[k + c]))
        pairs.append((u_in.at[c, pl.ds(own - HALO, HALO)], x_up.at[pl.ds(HALO * c, HALO)]))
        pairs.append((u_in.at[c, pl.ds(0, HALO)], x_down.at[pl.ds(HALO * c, HALO)]))
        pairs.append((f_in.at[c, pl.ds(own - HALO + 1, HALO - 1)], x_up.at[pl.ds(at, HALO - 1)]))
        pairs.append((f_in.at[c, pl.ds(0, HALO - 1)], x_down.at[pl.ds(at, HALO - 1)]))
        at += HALO - 1
    copies = [pltpu.make_async_copy(*pair, done.at[i]) for i, pair in enumerate(pairs)]
    for copy in copies:
        copy.start()
    copies[0].wait()
    y_up[6] = viscosity_of(kinds[:, rows - HALO:], viscosities)
    y_down[6] = viscosity_of(kinds[:, :HALO], viscosities)
    x_up[at:] = viscosity_of(kinds[own - HALO:], viscosities)
    x_down[at:] = viscosity_of(kinds[:HALO], viscosities)
    for copy in copies[1:]:
        copy.wait()


def corner_layers(count):
    at = 0
    for channel in range(7):
        deep = HALO - 2 if 3 <= channel < 6 else HALO - 1
        if channel == count:
            return at, deep
        at += deep
    return at, 0


def corner_kernel(ylo, yhi, up, down):
    own = ylo.shape[1]
    for channel in range(7):
        at, deep = corner_layers(channel)
        for target, first in ((up, own - deep), (down, 0)):
            target[at:at + deep, :HALO] = yhi[channel, first:first + deep]
            target[at:at + deep, HALO:] = ylo[channel, first:first + deep]


def on_chip(count):
    return [pl.BlockSpec(memory_space=pltpu.VMEM)] * count


def planes_scratch(planes, rows, lanes, pairs, own_rows, pooled, ends=()):
    block = (planes, rows, lanes)
    return (
        [pltpu.VMEM(ends + (3,) + block, jnp.float32)] * 3
        + [pltpu.VMEM(ends + block, jnp.float32)] * 8
        + [pltpu.VMEM((4, pairs, own_rows, lanes), jnp.float32), pltpu.VMEM(pooled, jnp.float32)]
    )


PACK_LIMIT = 62 * 1024 * 1024
LIMIT = pltpu.CompilerParams(vmem_limit_bytes=20 * 1024 * 1024)


def on_device(velocity_guess, forcing, cell_type, viscosities):
    f32 = jnp.float32
    count_x, count_y = lax.axis_size("gx"), lax.axis_size("gy")
    place = jnp.stack([lax.axis_index("gx"), lax.axis_index("gy"), count_x, count_y]).astype(jnp.int32)
    in_smem = [pl.BlockSpec(memory_space=pltpu.SMEM)]
    own, rows, lanes = cell_type.shape
    y_edge = jax.ShapeDtypeStruct((7, own, HALO, lanes), f32)
    x_edge = jax.ShapeDtypeStruct((7 * HALO - 3, rows, lanes), f32)
    y_up, y_down, x_up, x_down = pl.pallas_call(
        pack_kernel,
        out_shape=(y_edge, y_edge, x_edge, x_edge),
        in_specs=in_smem + [pl.BlockSpec(memory_space=pl.ANY)] * 3,
        out_specs=tuple(on_chip(4)),
        scratch_shapes=[pltpu.VMEM(cell_type.shape, jnp.int32), pltpu.SemaphoreType.DMA((25,))],
        compiler_params=pltpu.CompilerParams(vmem_limit_bytes=PACK_LIMIT),
    )(viscosities, velocity_guess, forcing, cell_type)
    ylo = passed_round(y_up, "gy", 1)
    yhi = passed_round(y_down, "gy", -1)
    xlo = passed_round(x_up, "gx", 1)
    xhi = passed_round(x_down, "gx", -1)
    corner = jax.ShapeDtypeStruct((corner_layers(7)[0], 2 * HALO, lanes), f32)
    up, down = pl.pallas_call(
        corner_kernel,
        out_shape=(corner, corner),
        in_specs=on_chip(2),
        out_specs=tuple(on_chip(2)),
        compiler_params=LIMIT,
    )(ylo, yhi)
    clo = passed_round(up, "gx", 1)
    chi = passed_round(down, "gx", -1)
    tall = rows + 2 * HALO
    middle = own // 2 - HALO
    state = (
        (3, own - 2 * HALO + 2, rows, lanes),
        (4 * middle, rows // 2, lanes // 2),
        (4, 2, 3, 2, tall, lanes),
        (2, 3, HALO, tall, lanes),
        (2, HALO + 1, tall, lanes),
    )
    known = pl.pallas_call(
        inner_kernel,
        out_shape=tuple(jax.ShapeDtypeStruct(shape, f32) for shape in state),
        in_specs=in_smem * 2 + on_chip(5),
        out_specs=tuple(on_chip(5)),
        scratch_shapes=planes_scratch(own + 2 * HALO, tall, lanes, middle, rows, (4 * middle, rows, 128)),
        compiler_params=LIMIT,
        cost_estimate=pl.CostEstimate(flops=60_000_000, bytes_accessed=6_000_000, transcendentals=0),
    )(place, viscosities, velocity_guess, forcing, cell_type, ylo, yhi)
    u0, packet = pl.pallas_call(
        outer_kernel,
        out_shape=(
            jax.ShapeDtypeStruct(velocity_guess.shape, f32),
            jax.ShapeDtypeStruct((4 * own // 2, rows // 2, lanes // 2), f32),
        ),
        in_specs=in_smem + on_chip(9),
        out_specs=tuple(on_chip(2)),
        scratch_shapes=planes_scratch(2 * HALO + 1, tall, lanes, HALO, rows, (4 * HALO, rows, 128), (2,)),
        compiler_params=LIMIT,
    )(place, *known, xlo, xhi, clo, chi)
    results = [u0]
    for grid_level in (1, 2):
        own, rows = own // 2, rows // 2
        packet = packet.reshape(4, own, rows, 128)
        valid = 256 >> grid_level
        ylo = passed_round(packet[:, :, rows - HALO:], "gy", 1)
        yhi = passed_round(packet[:, :, :HALO], "gy", -1)
        parts = [packet, yhi, ylo]
        total_rows = rows + 2 * HALO
        if total_rows % 8:
            parts = [packet, yhi, jnp.zeros_like(yhi), ylo]
            total_rows += HALO
        tall = jnp.concatenate(parts, axis=2)
        xlo = passed_round(tall[:, own - HALO:], "gx", 1)
        xhi = passed_round(tall[:, :HALO], "gx", -1)
        if grid_level == 1:
            packet_shape, pooled_shape = (4 * own // 2, rows // 2, 128), (4 * own // 2, rows, 128)
        else:
            packet_shape, pooled_shape = (4, 128), (8, 512)
        u_own, packet = pl.pallas_call(
            functools.partial(middle_kernel, 0.25**grid_level),
            out_shape=(
                jax.ShapeDtypeStruct((3, own, rows, valid), f32),
                jax.ShapeDtypeStruct(packet_shape, f32),
            ),
            in_specs=in_smem + on_chip(5),
            out_specs=tuple(on_chip(2)),
            scratch_shapes=planes_scratch(own + 2 * HALO, total_rows, 128, own // 2, rows, pooled_shape),
            compiler_params=LIMIT,
        )(place, packet, ylo, yhi, xlo, xhi)
        results.append(u_own)
    column = lax.all_to_all(jnp.broadcast_to(packet[None], (count_x, 4, 128)), "gx", 0, 0)
    column = column.transpose(1, 0, 2)
    gathered = lax.all_to_all(
        jnp.broadcast_to(column[None], (count_y, 4, count_x, 128)), "gy", 0, 0
    )
    block = (2 * REACH + 1, count_x, 128)
    field, vector, six = (pltpu.VMEM(lead + block, f32) for lead in ((), (3,), (6,)))
    last = pl.pallas_call(
        last_kernel,
        out_shape=tuple(jax.ShapeDtypeStruct(shape, f32) for shape in ((3, 2, 2, 32), (3, 1, 1, 16), (3, 1, 1, 16))),
        in_specs=in_smem + on_chip(1),
        out_specs=tuple(on_chip(3)),
        scratch_shapes=[vector, field, vector, vector, six, field, field,
                        vector, field, six, field, field, vector, vector, pltpu.VMEM((8, 128), f32)],
        compiler_params=LIMIT,
    )(place, gathered)
    return (*results, *last)


def solution(mesh):
    return jax.shard_map(
        on_device,
        mesh=mesh,
        in_specs=(P(None, "gx", "gy", None), P(None, "gx", "gy", None), P("gx", "gy", None), P()),
        out_specs=(P(None, "gx", "gy", None),) * 6,
        check_vma=False,
    )
```

```python
import functools

import jax
import jax.numpy as jnp
from jax import lax
from jax.experimental import pallas as pl
from jax.experimental.pallas import tpu as pltpu
from jax.sharding import PartitionSpec as P

SWEEPS = 3
LEVELS = 4
HALO = SWEEPS + 1
REACH = 5

damping = 0.8
mass_term = 0.05


def pair_swap(value, axis, odd):
    sizes = {name: lax.axis_size(name) for name in ("gx", "gy")}
    route = []
    for x in range(sizes["gx"]):
        for y in range(sizes["gy"]):
            place = {"gx": x, "gy": y}
            other = ((place[axis] + odd) ^ 1) - odd
            if 0 <= other < sizes[axis]:
                place[axis] = other
            else:
                across = "gy" if axis == "gx" else "gx"
                place[across] ^= 1
            route.append((x * sizes["gy"] + y, place["gx"] * sizes["gy"] + place["gy"]))
    return lax.ppermute(value, ("gx", "gy"), route)


def swapped(to_even, to_odd, axis):
    return pair_swap(to_even, axis, 0), pair_swap(to_odd, axis, 1)


def own_place():
    return lax.axis_index("gx"), lax.axis_index("gy"), lax.axis_size("gx"), lax.axis_size("gy")


def is_even(position):
    return position % 2 == 0


def split_dot(rows, pool):
    total = None
    for part in range(3):
        piece = rows.astype(jnp.bfloat16)
        term = jnp.dot(piece, pool, preferred_element_type=jnp.float32)
        total = term if total is None else total + term
        if part < 2:
            rows = rows - piece.astype(jnp.float32)
    return total


def inside_rows(place, own_rows, total_rows, shape, along_x=True):
    row = lax.broadcasted_iota(jnp.int32, shape, 0)
    above = jnp.where(place[1] < place[3] - 1, own_rows + HALO, own_rows)
    below = jnp.where(place[1] > 0, total_rows - HALO, total_rows)
    above = jnp.where(along_x, above, 0)
    below = jnp.where(along_x, below, total_rows)
    return (row < above) | (row >= below)


def pair_pool(lanes):
    source = lax.broadcasted_iota(jnp.int32, (lanes, 128), 0)
    target = lax.broadcasted_iota(jnp.int32, (lanes, 128), 1)
    return jnp.where(source // 2 == target, 0.125, 0.0).astype(jnp.bfloat16)


def make_coefficients(scale, lo, hi, m, cx, cym, cyp, czm, czp, weight, diag, unroll=False):
    rows, lanes = m.shape[1:]
    half = 0.5 * scale
    lane = lax.broadcasted_iota(jnp.int32, (rows, lanes), 1)
    cx[lo - 1] = half * (m[lo - 1] + m[lo])

    def plane(i, _):
        centre = m[i]
        upper = m[i + 1]
        y_lower = pltpu.roll(centre, 1, 0)
        y_upper = pltpu.roll(centre, rows - 1, 0)
        z_lower = jnp.where(lane == 0, 0.0, pltpu.roll(centre, 1, 1))
        z_upper = jnp.where(lane == lanes - 1, 0.0, pltpu.roll(centre, lanes - 1, 1))
        f_xl, f_xu = half * (centre + m[i - 1]), half * (centre + upper)
        f_yl, f_yu = half * (centre + y_lower), half * (centre + y_upper)
        f_zl, f_zu = half * (centre + z_lower), half * (centre + z_upper)
        total = mass_term + (f_xl + f_xu + f_yl + f_yu + f_zl + f_zu)
        cx[i] = f_xu
        cym[i], cyp[i] = f_yl, f_yu
        czm[i] = jnp.where(lane == 0, 0.0, f_zl)
        czp[i] = jnp.where(lane == lanes - 1, 0.0, f_zu)
        diag[i] = total
        weight[i] = jnp.where(centre > 0.0, damping / total, 0.0)
        return 0

    lax.fori_loop(lo, hi, plane, 0, unroll=unroll)


def flux_of(u, c, i, cx, cym, cyp, czm, czp):
    rows, lanes = u.shape[2:]
    centre = u[c, i]
    flux = cx[i - 1] * u[c, i - 1] + cx[i] * u[c, i + 1]
    flux += cym[i] * pltpu.roll(centre, 1, 0) + cyp[i] * pltpu.roll(centre, rows - 1, 0)
    flux += czm[i] * pltpu.roll(centre, 1, 1) + czp[i] * pltpu.roll(centre, lanes - 1, 1)
    return centre, flux


def relax(lo, hi, source, target, f, weight, faces, unroll=False):
    def plane(i, _):
        for c in range(3):
            centre, flux = flux_of(source, c, i, *faces)
            target[c, i] = (1.0 - damping) * centre + weight[i] * (f[c, i] + flux)
        return 0

    lax.fori_loop(lo, hi, plane, 0, unroll=unroll)


def start_from_zero(lo, hi, target, f, weight, unroll=False):
    def plane(i, _):
        for c in range(3):
            target[c, i] = weight[i] * f[c, i]
        return 0

    lax.fori_loop(lo, hi, plane, 0, unroll=unroll)


def residual_pairs(at, count, first, own_rows, u, f, m, diag, faces, pairs, unroll=False):
    def pair(p, _):
        i = at + 2 * p
        for c in range(3):
            both = None
            for j in (i, i + 1):
                centre, flux = flux_of(u, c, j, *faces)
                value = f[c, j] + flux - diag[j] * centre
                both = value if both is None else both + value
            pairs[c, first + p] = both[:own_rows]
        pairs[3, first + p] = (m[i] + m[i + 1])[:own_rows]
        return 0

    lax.fori_loop(0, count, pair, 0, unroll=unroll)


def pool_pairs(pairs, pooled):
    lanes = pairs.shape[-1]
    rows = pooled.shape[1]
    summed = split_dot(pairs[...].reshape(-1, lanes), pair_pool(lanes))
    pooled[...] = summed.reshape(pooled.shape)
    return pooled[:, pl.ds(0, rows // 2, 2), :] + pooled[:, pl.ds(1, rows // 2, 2), :]


def inner_kernel(viscosities, u_in, f_in, types, y_first, y_second, u_mid, packet_mid, u_edge, f_edge, m_edge,
                 ua, ub, f, m, cx, cym, cyp, czm, czp, weight, diag, pairs, pooled):
    place = own_place()
    own, rows = u_in.shape[1:3]
    body = pl.ds(HALO, own)
    last = HALO + own
    has_lower, has_upper = place[1] > 0, place[1] < place[3] - 1
    even = is_even(place[1])

    def put_rows(field, channel, masked):
        first, second = y_first[channel], y_second[channel]
        upper, lower = jnp.where(even, first, second), jnp.where(even, second, first)
        field[body, rows:rows + HALO] = jnp.where(has_upper, upper, 0.0) if masked else upper
        field[body, rows + HALO:] = jnp.where(has_lower, lower, 0.0) if masked else lower

    for c in range(3):
        ua[c, body, :rows] = u_in[c]
        put_rows(ua.at[c], c, True)
        f[c, body, :rows] = f_in[c]
        put_rows(f.at[c], 3 + c, False)
    m[body, :rows] = viscosity_of(types[...], viscosities)
    put_rows(m, 6, True)

    def edges(stage, u, depth):
        u_edge[stage, 0] = u[:, HALO + depth:HALO + depth + 2]
        u_edge[stage, 1] = u[:, last - depth - 2:last - depth]

    edges(0, ua, 0)
    f_edge[0], f_edge[1] = f[:, HALO:2 * HALO], f[:, last - HALO:last]
    m_edge[0], m_edge[1] = m[HALO:2 * HALO + 1], m[last - HALO - 1:last]
    make_coefficients(1.0, HALO + 1, last - 1, m, cx, cym, cyp, czm, czp, weight, diag, True)
    faces = (cx, cym, cyp, czm, czp)
    relax(HALO + 1, last - 1, ua, ub, f, weight, faces, True)
    edges(1, ub, 1)
    relax(HALO + 2, last - 2, ub, ua, f, weight, faces, True)
    edges(2, ua, 2)
    relax(HALO + 3, last - 3, ua, ub, f, weight, faces, True)
    edges(3, ub, 3)
    u_mid[...] = ub[:, HALO + 3:last - 3, :rows]
    residual_pairs(2 * HALO, own // 2 - HALO, 0, rows, ub, f, m, diag, faces, pairs, True)
    packet_mid[...] = pool_pairs(pairs, pooled)


def outer_kernel(u_mid, packet_mid, u_edge, f_edge, m_edge, x_first, x_second, corner_first, corner_second, u_out, packet,
                 ua, ub, f, m, cx, cym, cyp, czm, czp, weight, diag, pairs, pooled):
    place = own_place()
    own, rows = u_out.shape[1:3]
    planes = m.shape[1]
    count_f = HALO - 1
    at_f, at_m = 3 * HALO, 3 * HALO + 3 * count_f
    half = own // 2
    corner_shape = corner_first.shape[1:]
    even, even_y = is_even(place[0]), is_even(place[1])

    for end in range(2):
        take_first = even if end == 1 else jnp.logical_not(even)

        def halo(at, count):
            return jnp.where(take_first, x_first[at:at + count], x_second[at:at + count])

        def corner(at, count):
            rows_of = [corner_first[at + i] for i in range(count)], [corner_second[at + i] for i in range(count)]
            chosen = [jnp.where(take_first, one, two) for one, two in zip(*rows_of)]
            return jnp.stack([jnp.where(even_y, one, pltpu.roll(one, HALO, 0)) for one in chosen])

        outer = 0 if end == 0 else planes - HALO
        inner = HALO if end == 0 else 0
        present = place[0] > 0 if end == 0 else place[0] < place[2] - 1
        inside = inside_rows(place, 0, 2 * HALO, corner_shape, present)

        def put_corner(field, channel, masked):
            at, deep = corner_layers(channel)
            value = corner(at, deep)
            if masked:
                value = jnp.where(inside, value, 0.0)
            first = HALO - deep if end == 0 else planes - HALO
            field[first:first + deep, rows:] = value
            far = first - 1 if end == 0 else first + deep
            field[far, rows:] = jnp.zeros(corner_shape, jnp.float32)

        for c in range(3):
            ua[end, c, outer:outer + HALO, :rows] = jnp.where(present, halo(HALO * c, HALO), 0.0)
            put_corner(ua.at[end, c], c, True)
            nearest = HALO if end == 0 else planes - HALO - 2
            ua[end, c, nearest:nearest + 2] = u_edge[0, end, c]
            beyond = 1 if end == 0 else planes - HALO
            f[end, c, beyond:beyond + count_f, :rows] = halo(at_f + count_f * c, count_f)
            put_corner(f.at[end, c], 3 + c, False)
            own_f = HALO if end == 0 else planes - 2 * HALO
            f[end, c, own_f:own_f + HALO] = f_edge[end, c]
        m[end, outer:outer + HALO, :rows] = jnp.where(present, halo(at_m, HALO), 0.0)
        put_corner(m.at[end], 6, True)
        m[end, inner:inner + HALO + 1] = m_edge[end]
        parts = (cx.at[end], cym.at[end], cyp.at[end], czm.at[end], czp.at[end])
        u_a, u_b, f_e, w_e, d_e = ua.at[end], ub.at[end], f.at[end], weight.at[end], diag.at[end]
        make_coefficients(1.0, 1, planes - 1, m.at[end], *parts, w_e, d_e, True)
        for stage, (source, target) in enumerate(((u_a, u_b), (u_b, u_a), (u_a, u_b))):
            first = 1 + stage if end == 0 else planes - 1 - HALO - stage
            relax(first, first + HALO, source, target, f_e, w_e, parts, True)
            known = first + HALO if end == 0 else first - 2
            for c in range(3):
                target[c, known:known + 2] = u_edge[stage + 1, end, c]
        at = HALO if end == 0 else 1
        residual_pairs(at, HALO // 2, HALO // 2 * end, rows, u_b, f_e, m.at[end], d_e, parts, pairs, True)
        for c in range(3):
            if end == 0:
                u_out[c, :HALO - 1] = ub[end, c, HALO:2 * HALO - 1, :rows]
            else:
                u_out[c, own - HALO + 1:] = ub[end, c, planes - 2 * HALO + 1:planes - HALO, :rows]
    u_out[:, HALO - 1:own - HALO + 1] = u_mid[...]
    ends = pool_pairs(pairs, pooled)
    for c in range(4):
        at = HALO * c
        packet[half * c:half * c + 2] = ends[at:at + 2]
        packet[half * c + 2:half * (c + 1) - 2] = packet_mid[(half - HALO) * c:(half - HALO) * (c + 1)]
        packet[half * (c + 1) - 2:half * (c + 1)] = ends[at + 2:at + 4]


def middle_kernel(scale, p_in, y_first, y_second, x_first, x_second, u_out, packet,
                  ua, ub, f, m, cx, cym, cyp, czm, czp, weight, diag, pairs, pooled):
    place = own_place()
    own, rows = p_in.shape[1:3]
    body = pl.ds(HALO, own)
    planes = own + 2 * HALO
    total_rows = m.shape[1]
    even_x, even_y = is_even(place[0]), is_even(place[1])
    for c in range(4):
        if c < 3:
            field = f.at[c]
        else:
            field = m
        if total_rows > rows + 2 * HALO:
            field[body] = jnp.zeros((own,) + m.shape[1:], jnp.float32)
        field[body, :rows] = p_in[c]
        field[body, rows:rows + HALO] = jnp.where(even_y, y_first[c], y_second[c])
        field[body, total_rows - HALO:] = jnp.where(even_y, y_second[c], y_first[c])
        field[:HALO] = jnp.where(even_x, x_second[c], x_first[c])
        field[HALO + own:] = jnp.where(even_x, x_first[c], x_second[c])
    shape = m.shape[1:]
    in_rows = inside_rows(place, rows, total_rows, shape)
    in_lower = inside_rows(place, rows, total_rows, shape, place[0] > 0)
    in_upper = inside_rows(place, rows, total_rows, shape, place[0] < place[2] - 1)
    m[body] = jnp.where(in_rows, m[body], 0.0)
    m[:HALO] = jnp.where(in_lower, m[:HALO], 0.0)
    m[HALO + own:] = jnp.where(in_upper, m[HALO + own:], 0.0)
    make_coefficients(scale, 1, planes - 1, m, cx, cym, cyp, czm, czp, weight, diag, unroll=True)
    faces = (cx, cym, cyp, czm, czp)
    start_from_zero(1, planes - 1, ub, f, weight, unroll=True)
    relax(2, planes - 2, ub, ua, f, weight, faces, unroll=True)
    relax(3, planes - 3, ua, ub, f, weight, faces, unroll=True)
    lanes = u_out.shape[-1]
    for c in range(3):
        u_out[c] = ub[c, body, :rows, :lanes]
    residual_pairs(HALO, own // 2, 0, rows, ub, f, m, diag, faces, pairs, unroll=True)
    if rows > 4:
        packet[...] = pool_pairs(pairs, pooled)
    else:
        for c in range(4):
            for p in range(own // 2):
                for q in range(rows // 2):
                    at = 128 * (p * (rows // 2) + q)
                    pooled[c:c + 1, at:at + 128] = (
                        pairs[c, p, 2 * q:2 * q + 1] + pairs[c, p, 2 * q + 1:2 * q + 2]
                    )
        depth = pooled.shape[1]
        source = lax.broadcasted_iota(jnp.int32, (depth, 128), 0)
        target = lax.broadcasted_iota(jnp.int32, (depth, 128), 1)
        hit = (source // 128 * 32 + source % 128 // 2 == target) & (source % 128 < 64)
        pool = jnp.where(hit, 0.125, 0.0).astype(jnp.bfloat16)
        packet[...] = split_dot(pooled[...], pool)[:4]


def last_kernel(g, u3_out, u4_out, r4_out, fw, mw, ua, ub, faces, weight, diag,
                f4, m4, faces4, weight4, diag4, va, vb, rows_out):
    count = g.shape[0]
    rows, lanes = g.shape[2:]
    shape = (rows, lanes)
    lane = lax.broadcasted_iota(jnp.int32, shape, 1)
    row = lax.broadcasted_iota(jnp.int32, shape, 0)
    x_one, y_one, z = lane // 64 == 1, lane // 32 % 2 == 1, lane % 32
    first_row, last_row = row == 0, row == rows - 1
    zero = jnp.zeros(shape, jnp.float32)
    x_at, y_at = lax.axis_index("gx"), lax.axis_index("gy")
    window = 2 * REACH + 1
    for w in range(window):
        i = y_at + (w - REACH)
        inside = (i >= 0) & (i < count)
        i = jnp.clip(i, 0, count - 1)
        for c in range(3):
            fw[c, w] = jnp.where(inside, g[i, c], 0.0)
        mw[w] = jnp.where(inside, g[i, 3], 0.0)

    def shifted_rows(value):
        return pltpu.roll(value, 1, 0), pltpu.roll(value, rows - 1, 0)

    def near3(get, w):
        centre = get(w)
        other = pltpu.roll(centre, 64, 1)
        lower, upper = shifted_rows(other)
        x_out = jnp.where(x_one, upper, lower)
        y_in = jnp.where(y_one, pltpu.roll(centre, 32, 1), pltpu.roll(centre, lanes - 32, 1))
        below = pltpu.roll(get(w - 1), lanes - 32, 1) if w > 0 else zero
        above = pltpu.roll(get(w + 1), 32, 1) if w < window - 1 else zero
        y_out = jnp.where(y_one, above, below)
        return centre, (other, x_out, y_in, y_out, pltpu.roll(centre, 1, 1), pltpu.roll(centre, lanes - 1, 1))

    x_edge = (x_one & last_row) | (jnp.logical_not(x_one) & first_row)
    outside3 = (None, x_edge, None, None, z == 0, z == 31)

    def near4(get, w):
        centre = get(w)
        lower, upper = shifted_rows(centre)
        return centre, (lower, upper, get(w - 1), get(w + 1),
                        pltpu.roll(centre, 2, 1), pltpu.roll(centre, lanes - 2, 1))

    outside4 = (first_row, last_row, None, None, z < 2, z >= 30)

    def level(scale, near, outside, f, m, faces, weight, diag, ua, ub, spans, residual):
        half = 0.5 * scale
        for w in spans[0]:
            centre, sides = near(lambda j: m[j], w)
            total = jnp.full(shape, mass_term, jnp.float32)
            for k in range(6):
                side = sides[k] if outside[k] is None else jnp.where(outside[k], 0.0, sides[k])
                face = half * (centre + side)
                total = total + face
                faces[k, w] = face if outside[k] is None else jnp.where(outside[k], 0.0, face)
            diag[w] = total
            weight[w] = jnp.where(centre > 0.0, damping / total, 0.0)
            for c in range(3):
                ua[c, w] = weight[w] * f[c, w]

        def flux_at(u, c, w):
            centre, sides = near(lambda j: u[c, j], w)
            flux = faces[0, w] * sides[0]
            for k in range(1, 6):
                flux = flux + faces[k, w] * sides[k]
            return centre, flux

        for source, target, span in ((ua, ub, spans[1]), (ub, ua, spans[2])):
            for w in span:
                for c in range(3):
                    centre, flux = flux_at(source, c, w)
                    target[c, w] = (1.0 - damping) * centre + weight[w] * (f[c, w] + flux)
        for w in spans[3]:
            for c in range(3):
                centre, flux = flux_at(ua, c, w)
                residual(c, w, f[c, w] + flux - diag[w] * centre)

    def pool(value):
        value = value + pltpu.roll(value, 64, 1)
        value = value + pltpu.roll(value, 32, 1)
        return 0.125 * (value + pltpu.roll(value, lanes - 1, 1))

    def to_level4(c, w, value):
        f4[c, w] = pool(value)

    spans = (range(window), range(1, window - 1), range(1, window - 1), range(2, window - 2))
    level(0.25**3, near3, outside3, fw, mw, faces, weight, diag, ua, ub, spans, to_level4)
    for w in range(1, window - 1):
        m4[w] = pool(mw[w])
    mine = row == x_at

    def own_row(value):
        return jnp.sum(jnp.where(mine, value, 0.0), axis=0, keepdims=True)

    def keep(c, w, value):
        rows_out[3 + c:4 + c] = own_row(value)

    spans = tuple(range(2 + k, window - 2 - k) for k in range(4))
    level(0.25**4, near4, outside4, f4, m4, faces4, weight4, diag4, va, vb, spans, keep)
    for c in range(3):
        value = own_row(ua[c, REACH])
        rows_out[c:c + 1] = own_row(va[c, REACH])
        for k in range(4):
            turned = value if k == 0 else pltpu.roll(value, lanes - 32 * k, 1)
            u3_out[c, k // 2, k % 2:k % 2 + 1] = turned[:, :32]
    source = lax.broadcasted_iota(jnp.int32, (lanes, lanes), 0)
    target = lax.broadcasted_iota(jnp.int32, (lanes, lanes), 1)
    take = jnp.where((source == 2 * target) & (target < 16), 1.0, 0.0).astype(jnp.bfloat16)
    ends = split_dot(rows_out[...], take)
    for c in range(3):
        u4_out[c, 0] = ends[c:c + 1, :16]
        r4_out[c, 0] = ends[3 + c:4 + c, :16]


def viscosity_of(kind, viscosities):
    return jnp.where(
        kind < 2,
        jnp.where(kind == 0, viscosities[0], viscosities[1]),
        jnp.where(kind == 2, viscosities[2], viscosities[3]),
    )


def pack_kernel(viscosities, u_in, f_in, types, y_first, y_second, x_first, x_second, kinds, done):
    place = own_place()
    own, rows = types.shape[:2]
    even_x, even_y = is_even(place[0]), is_even(place[1])
    upper, upper_f, lower = own - HALO, own - HALO + 1, 0
    at_first, at_second = jnp.where(even_x, upper, lower), jnp.where(even_x, lower, upper)
    f_first, f_second = jnp.where(even_x, upper_f, lower), jnp.where(even_x, lower, upper_f)
    always, if_even, if_odd = [(types, kinds)], [], []
    at = 3 * HALO
    for c in range(3):
        for k, field in ((0, u_in), (3, f_in)):
            top, bottom = field.at[c, :, pl.ds(rows - HALO, HALO)], field.at[c, :, pl.ds(0, HALO)]
            if_even += [(top, y_first.at[k + c]), (bottom, y_second.at[k + c])]
            if_odd += [(bottom, y_first.at[k + c]), (top, y_second.at[k + c])]
        here = pl.ds(HALO * c, HALO)
        always.append((u_in.at[c, pl.ds(at_first, HALO)], x_first.at[here]))
        always.append((u_in.at[c, pl.ds(at_second, HALO)], x_second.at[here]))
        here = pl.ds(at, HALO - 1)
        always.append((f_in.at[c, pl.ds(f_first, HALO - 1)], x_first.at[here]))
        always.append((f_in.at[c, pl.ds(f_second, HALO - 1)], x_second.at[here]))
        at += HALO - 1

    def copies(pairs, first):
        return [pltpu.make_async_copy(*pair, done.at[first + i]) for i, pair in enumerate(pairs)]

    def start(pairs, first):
        for copy in copies(pairs, first):
            copy.start()

    start(always[:1], 0)
    pl.when(even_y)(lambda: start(if_even, len(always)))
    pl.when(jnp.logical_not(even_y))(lambda: start(if_odd, len(always)))
    start(always[1:], 1)
    copies(always[:1], 0)[0].wait()
    top = viscosity_of(kinds[:, rows - HALO:], viscosities)
    bottom = viscosity_of(kinds[:, :HALO], viscosities)
    y_first[6], y_second[6] = jnp.where(even_y, top, bottom), jnp.where(even_y, bottom, top)
    x_first[at:] = viscosity_of(kinds[pl.ds(at_first, HALO)], viscosities)
    x_second[at:] = viscosity_of(kinds[pl.ds(at_second, HALO)], viscosities)
    for copy in copies(always[1:], 1) + copies(if_even, len(always)):
        copy.wait()


def corner_layers(count):
    at = 0
    for channel in range(7):
        deep = HALO - 2 if 3 <= channel < 6 else HALO - 1
        if channel == count:
            return at, deep
        at += deep
    return at, 0


def corner_kernel(y_first, y_second, first, second):
    own = y_first.shape[1]
    even = is_even(lax.axis_index("gx"))
    for channel in range(7):
        at, deep = corner_layers(channel)
        for target, upper in ((first, even), (second, jnp.logical_not(even))):
            planes = pl.ds(jnp.where(upper, own - deep, 0), deep)
            target[at:at + deep, :HALO] = y_first[channel, planes]
            target[at:at + deep, HALO:] = y_second[channel, planes]


def on_chip(count):
    return [pl.BlockSpec(memory_space=pltpu.VMEM)] * count


def planes_scratch(planes, rows, lanes, pairs, own_rows, pooled, ends=()):
    block = (planes, rows, lanes)
    return (
        [pltpu.VMEM(ends + (3,) + block, jnp.float32)] * 3
        + [pltpu.VMEM(ends + block, jnp.float32)] * 8
        + [pltpu.VMEM((4, pairs, own_rows, lanes), jnp.float32), pltpu.VMEM(pooled, jnp.float32)]
    )


PACK_LIMIT = 62 * 1024 * 1024
LIMIT = pltpu.CompilerParams(vmem_limit_bytes=20 * 1024 * 1024)


def on_device(velocity_guess, forcing, cell_type, viscosities):
    f32 = jnp.float32
    count_x, count_y = lax.axis_size("gx"), lax.axis_size("gy")
    even_x, even_y = is_even(lax.axis_index("gx")), is_even(lax.axis_index("gy"))
    in_smem = [pl.BlockSpec(memory_space=pltpu.SMEM)]
    own, rows, lanes = cell_type.shape
    y_edge = jax.ShapeDtypeStruct((7, own, HALO, lanes), f32)
    x_edge = jax.ShapeDtypeStruct((7 * HALO - 3, rows, lanes), f32)
    y_out, y_out_odd, x_out, x_out_odd = pl.pallas_call(
        pack_kernel,
        out_shape=(y_edge, y_edge, x_edge, x_edge),
        in_specs=in_smem + [pl.BlockSpec(memory_space=pl.ANY)] * 3,
        out_specs=tuple(on_chip(4)),
        scratch_shapes=[pltpu.VMEM(cell_type.shape, jnp.int32), pltpu.SemaphoreType.DMA((25,))],
        compiler_params=pltpu.CompilerParams(vmem_limit_bytes=PACK_LIMIT),
    )(viscosities, velocity_guess, forcing, cell_type)
    y_halo = swapped(y_out, y_out_odd, "gy")
    x_halo = swapped(x_out, x_out_odd, "gx")
    corner = jax.ShapeDtypeStruct((corner_layers(7)[0], 2 * HALO, lanes), f32)
    corners = pl.pallas_call(
        corner_kernel,
        out_shape=(corner, corner),
        in_specs=on_chip(2),
        out_specs=tuple(on_chip(2)),
        compiler_params=LIMIT,
    )(*y_halo)
    corner_halo = swapped(*corners, "gx")
    tall = rows + 2 * HALO
    middle = own // 2 - HALO
    state = (
        (3, own - 2 * HALO + 2, rows, lanes),
        (4 * middle, rows // 2, lanes // 2),
        (4, 2, 3, 2, tall, lanes),
        (2, 3, HALO, tall, lanes),
        (2, HALO + 1, tall, lanes),
    )
    known = pl.pallas_call(
        inner_kernel,
        out_shape=tuple(jax.ShapeDtypeStruct(shape, f32) for shape in state),
        in_specs=in_smem + on_chip(5),
        out_specs=tuple(on_chip(5)),
        scratch_shapes=planes_scratch(own + 2 * HALO, tall, lanes, middle, rows, (4 * middle, rows, 128)),
        compiler_params=LIMIT,
        cost_estimate=pl.CostEstimate(flops=60_000_000, bytes_accessed=6_000_000, transcendentals=0),
    )(viscosities, velocity_guess, forcing, cell_type, *y_halo)
    u0, packet = pl.pallas_call(
        outer_kernel,
        out_shape=(
            jax.ShapeDtypeStruct(velocity_guess.shape, f32),
            jax.ShapeDtypeStruct((4 * own // 2, rows // 2, lanes // 2), f32),
        ),
        in_specs=on_chip(9),
        out_specs=tuple(on_chip(2)),
        scratch_shapes=planes_scratch(2 * HALO + 1, tall, lanes, HALO, rows, (4 * HALO, rows, 128), (2,)),
        compiler_params=LIMIT,
    )(*known, *x_halo, *corner_halo)
    results = [u0]
    for grid_level in (1, 2):
        own, rows = own // 2, rows // 2
        packet = packet.reshape(4, own, rows, 128)
        valid = 256 >> grid_level
        top, bottom = packet[:, :, rows - HALO:], packet[:, :, :HALO]
        y_halo = swapped(jnp.where(even_y, top, bottom), jnp.where(even_y, bottom, top), "gy")
        upper, lower = jnp.where(even_y, y_halo[0], y_halo[1]), jnp.where(even_y, y_halo[1], y_halo[0])
        parts = [packet, upper, lower]
        total_rows = rows + 2 * HALO
        if total_rows % 8:
            parts = [packet, upper, jnp.zeros_like(upper), lower]
            total_rows += HALO
        top, bottom = (
            jnp.concatenate([part[:, at:at + HALO] for part in parts], axis=2) for at in (own - HALO, 0)
        )
        x_halo = swapped(jnp.where(even_x, top, bottom), jnp.where(even_x, bottom, top), "gx")
        if grid_level == 1:
            packet_shape, pooled_shape = (4 * own // 2, rows // 2, 128), (4 * own // 2, rows, 128)
        else:
            packet_shape, pooled_shape = (4, 128), (8, 512)
        u_own, packet = pl.pallas_call(
            functools.partial(middle_kernel, 0.25**grid_level),
            out_shape=(
                jax.ShapeDtypeStruct((3, own, rows, valid), f32),
                jax.ShapeDtypeStruct(packet_shape, f32),
            ),
            in_specs=on_chip(5),
            out_specs=tuple(on_chip(2)),
            scratch_shapes=planes_scratch(own + 2 * HALO, total_rows, 128, own // 2, rows, pooled_shape),
            compiler_params=LIMIT,
        )(packet, *y_halo, *x_halo)
        results.append(u_own)
    column = lax.all_to_all(jnp.broadcast_to(packet[None], (count_x, 4, 128)), "gx", 0, 0)
    column = column.transpose(1, 0, 2)
    gathered = lax.all_to_all(
        jnp.broadcast_to(column[None], (count_y, 4, count_x, 128)), "gy", 0, 0
    )
    block = (2 * REACH + 1, count_x, 128)
    field, vector, six = (pltpu.VMEM(lead + block, f32) for lead in ((), (3,), (6,)))
    last = pl.pallas_call(
        last_kernel,
        out_shape=tuple(jax.ShapeDtypeStruct(shape, f32) for shape in ((3, 2, 2, 32), (3, 1, 1, 16), (3, 1, 1, 16))),
        in_specs=on_chip(1),
        out_specs=tuple(on_chip(3)),
        scratch_shapes=[vector, field, vector, vector, six, field, field,
                        vector, field, six, field, field, vector, vector, pltpu.VMEM((8, 128), f32)],
        compiler_params=LIMIT,
    )(gathered)
    return (*results, *last)


def solution(mesh):
    return jax.shard_map(
        on_device,
        mesh=mesh,
        in_specs=(P(None, "gx", "gy", None), P(None, "gx", "gy", None), P("gx", "gy", None), P()),
        out_specs=(P(None, "gx", "gy", None),) * 6,
        check_vma=False,
    )
```

```python
import functools

import jax
import jax.numpy as jnp
from jax import lax
from jax.experimental import pallas as pl
from jax.experimental.pallas import tpu as pltpu
from jax.sharding import PartitionSpec as P

SWEEPS = 3
LEVELS = 4
HALO = SWEEPS + 1
REACH = 5

damping = 0.8
mass_term = 0.05


def pair_swap(value, axis, odd):
    sizes = {name: lax.axis_size(name) for name in ("gx", "gy")}
    route = []
    for x in range(sizes["gx"]):
        for y in range(sizes["gy"]):
            place = {"gx": x, "gy": y}
            other = ((place[axis] + odd) ^ 1) - odd
            if 0 <= other < sizes[axis]:
                place[axis] = other
            else:
                across = "gy" if axis == "gx" else "gx"
                place[across] ^= 1
            route.append((x * sizes["gy"] + y, place["gx"] * sizes["gy"] + place["gy"]))
    return lax.ppermute(value, ("gx", "gy"), route)


def swapped(to_even, to_odd, axis):
    return pair_swap(to_even, axis, 0), pair_swap(to_odd, axis, 1)


def own_place():
    return lax.axis_index("gx"), lax.axis_index("gy"), lax.axis_size("gx"), lax.axis_size("gy")


def is_even(position):
    return position % 2 == 0


def split_dot(rows, pool):
    total = None
    for part in range(3):
        piece = rows.astype(jnp.bfloat16)
        term = jnp.dot(piece, pool, preferred_element_type=jnp.float32)
        total = term if total is None else total + term
        if part < 2:
            rows = rows - piece.astype(jnp.float32)
    return total


def inside_rows(place, own_rows, total_rows, shape, along_x=True):
    row = lax.broadcasted_iota(jnp.int32, shape, 0)
    above = jnp.where(place[1] < place[3] - 1, own_rows + HALO, own_rows)
    below = jnp.where(place[1] > 0, total_rows - HALO, total_rows)
    above = jnp.where(along_x, above, 0)
    below = jnp.where(along_x, below, total_rows)
    return (row < above) | (row >= below)


def pair_pool(lanes):
    source = lax.broadcasted_iota(jnp.int32, (lanes, 128), 0)
    target = lax.broadcasted_iota(jnp.int32, (lanes, 128), 1)
    return jnp.where(source // 2 == target, 0.125, 0.0).astype(jnp.bfloat16)


def make_coefficients(scale, lo, hi, m, cx, cym, cyp, czm, czp, weight, diag, unroll=False):
    rows, lanes = m.shape[1:]
    half = 0.5 * scale
    lane = lax.broadcasted_iota(jnp.int32, (rows, lanes), 1)
    cx[lo - 1] = half * (m[lo - 1] + m[lo])

    def plane(i, _):
        centre = m[i]
        upper = m[i + 1]
        y_lower = pltpu.roll(centre, 1, 0)
        y_upper = pltpu.roll(centre, rows - 1, 0)
        z_lower = jnp.where(lane == 0, 0.0, pltpu.roll(centre, 1, 1))
        z_upper = jnp.where(lane == lanes - 1, 0.0, pltpu.roll(centre, lanes - 1, 1))
        f_xl, f_xu = half * (centre + m[i - 1]), half * (centre + upper)
        f_yl, f_yu = half * (centre + y_lower), half * (centre + y_upper)
        f_zl, f_zu = half * (centre + z_lower), half * (centre + z_upper)
        total = mass_term + (f_xl + f_xu + f_yl + f_yu + f_zl + f_zu)
        cx[i] = f_xu
        cym[i], cyp[i] = f_yl, f_yu
        czm[i] = jnp.where(lane == 0, 0.0, f_zl)
        czp[i] = jnp.where(lane == lanes - 1, 0.0, f_zu)
        diag[i] = total
        weight[i] = jnp.where(centre > 0.0, damping / total, 0.0)
        return 0

    lax.fori_loop(lo, hi, plane, 0, unroll=unroll)


def flux_of(u, c, i, cx, cym, cyp, czm, czp):
    rows, lanes = u.shape[2:]
    centre = u[c, i]
    flux = cx[i - 1] * u[c, i - 1] + cx[i] * u[c, i + 1]
    flux += cym[i] * pltpu.roll(centre, 1, 0) + cyp[i] * pltpu.roll(centre, rows - 1, 0)
    flux += czm[i] * pltpu.roll(centre, 1, 1) + czp[i] * pltpu.roll(centre, lanes - 1, 1)
    return centre, flux


def relax(lo, hi, source, target, f, weight, faces, unroll=False):
    def plane(i, _):
        for c in range(3):
            centre, flux = flux_of(source, c, i, *faces)
            target[c, i] = (1.0 - damping) * centre + weight[i] * (f[c, i] + flux)
        return 0

    lax.fori_loop(lo, hi, plane, 0, unroll=unroll)


def start_from_zero(lo, hi, target, f, weight, unroll=False):
    def plane(i, _):
        for c in range(3):
            target[c, i] = weight[i] * f[c, i]
        return 0

    lax.fori_loop(lo, hi, plane, 0, unroll=unroll)


def residual_pairs(at, count, first, own_rows, u, f, m, diag, faces, pairs, unroll=False):
    def pair(p, _):
        i = at + 2 * p
        for c in range(3):
            both = None
            for j in (i, i + 1):
                centre, flux = flux_of(u, c, j, *faces)
                value = f[c, j] + flux - diag[j] * centre
                both = value if both is None else both + value
            pairs[c, first + p] = both[:own_rows]
        pairs[3, first + p] = (m[i] + m[i + 1])[:own_rows]
        return 0

    lax.fori_loop(0, count, pair, 0, unroll=unroll)


def pool_pairs(pairs, pooled):
    lanes = pairs.shape[-1]
    rows = pooled.shape[1]
    summed = split_dot(pairs[...].reshape(-1, lanes), pair_pool(lanes))
    pooled[...] = summed.reshape(pooled.shape)
    return pooled[:, pl.ds(0, rows // 2, 2), :] + pooled[:, pl.ds(1, rows // 2, 2), :]


def inner_kernel(viscosities, u_in, f_in, types, y_first, y_second, u_mid, packet_mid, u_edge, f_edge, m_edge,
                 ua, ub, f, m, cx, cym, cyp, czm, czp, weight, diag, pairs, pooled):
    place = own_place()
    own, rows = u_in.shape[1:3]
    body = pl.ds(HALO, own)
    last = HALO + own
    has_lower, has_upper = place[1] > 0, place[1] < place[3] - 1
    even = is_even(place[1])

    def put_rows(field, channel, masked):
        first, second = y_first[channel], y_second[channel]
        upper, lower = jnp.where(even, first, second), jnp.where(even, second, first)
        field[body, rows:rows + HALO] = jnp.where(has_upper, upper, 0.0) if masked else upper
        field[body, rows + HALO:] = jnp.where(has_lower, lower, 0.0) if masked else lower

    for c in range(3):
        ua[c, body, :rows] = u_in[c]
        put_rows(ua.at[c], c, True)
        f[c, body, :rows] = f_in[c]
        put_rows(f.at[c], 3 + c, False)
    m[body, :rows] = viscosity_of(types[...], viscosities)
    put_rows(m, 6, True)

    def edges(stage, u, depth):
        u_edge[stage, 0] = u[:, HALO + depth:HALO + depth + 2]
        u_edge[stage, 1] = u[:, last - depth - 2:last - depth]

    edges(0, ua, 0)
    f_edge[0], f_edge[1] = f[:, HALO:2 * HALO], f[:, last - HALO:last]
    m_edge[0], m_edge[1] = m[HALO:2 * HALO + 1], m[last - HALO - 1:last]
    make_coefficients(1.0, HALO + 1, last - 1, m, cx, cym, cyp, czm, czp, weight, diag, True)
    faces = (cx, cym, cyp, czm, czp)
    relax(HALO + 1, last - 1, ua, ub, f, weight, faces, True)
    edges(1, ub, 1)
    relax(HALO + 2, last - 2, ub, ua, f, weight, faces, True)
    edges(2, ua, 2)
    relax(HALO + 3, last - 3, ua, ub, f, weight, faces, True)
    edges(3, ub, 3)
    u_mid[...] = ub[:, HALO + 3:last - 3, :rows]
    residual_pairs(2 * HALO, own // 2 - HALO, 0, rows, ub, f, m, diag, faces, pairs, True)
    packet_mid[...] = pool_pairs(pairs, pooled)


def outer_kernel(u_mid, packet_mid, u_edge, f_edge, m_edge, x_first, x_second, corner_first, corner_second, u_out, packet,
                 ua, ub, f, m, cx, cym, cyp, czm, czp, weight, diag, pairs, pooled):
    place = own_place()
    own, rows = u_out.shape[1:3]
    planes = m.shape[1]
    count_f = HALO - 1
    at_f, at_m = 3 * HALO, 3 * HALO + 3 * count_f
    half = own // 2
    corner_shape = corner_first.shape[1:]
    even, even_y = is_even(place[0]), is_even(place[1])

    for end in range(2):
        take_first = even if end == 1 else jnp.logical_not(even)

        def halo(at, count):
            return jnp.where(take_first, x_first[at:at + count], x_second[at:at + count])

        def corner(at, count):
            rows_of = [corner_first[at + i] for i in range(count)], [corner_second[at + i] for i in range(count)]
            chosen = [jnp.where(take_first, one, two) for one, two in zip(*rows_of)]
            return jnp.stack([jnp.where(even_y, one, pltpu.roll(one, HALO, 0)) for one in chosen])

        outer = 0 if end == 0 else planes - HALO
        inner = HALO if end == 0 else 0
        present = place[0] > 0 if end == 0 else place[0] < place[2] - 1
        inside = inside_rows(place, 0, 2 * HALO, corner_shape, present)

        def put_corner(field, channel, masked):
            at, deep = corner_layers(channel)
            value = corner(at, deep)
            if masked:
                value = jnp.where(inside, value, 0.0)
            first = HALO - deep if end == 0 else planes - HALO
            field[first:first + deep, rows:] = value
            far = first - 1 if end == 0 else first + deep
            field[far, rows:] = jnp.zeros(corner_shape, jnp.float32)

        for c in range(3):
            ua[end, c, outer:outer + HALO, :rows] = jnp.where(present, halo(HALO * c, HALO), 0.0)
            put_corner(ua.at[end, c], c, True)
            nearest = HALO if end == 0 else planes - HALO - 2
            ua[end, c, nearest:nearest + 2] = u_edge[0, end, c]
            beyond = 1 if end == 0 else planes - HALO
            f[end, c, beyond:beyond + count_f, :rows] = halo(at_f + count_f * c, count_f)
            put_corner(f.at[end, c], 3 + c, False)
            own_f = HALO if end == 0 else planes - 2 * HALO
            f[end, c, own_f:own_f + HALO] = f_edge[end, c]
        m[end, outer:outer + HALO, :rows] = jnp.where(present, halo(at_m, HALO), 0.0)
        put_corner(m.at[end], 6, True)
        m[end, inner:inner + HALO + 1] = m_edge[end]
        parts = (cx.at[end], cym.at[end], cyp.at[end], czm.at[end], czp.at[end])
        u_a, u_b, f_e, w_e, d_e = ua.at[end], ub.at[end], f.at[end], weight.at[end], diag.at[end]
        make_coefficients(1.0, 1, planes - 1, m.at[end], *parts, w_e, d_e, True)
        for stage, (source, target) in enumerate(((u_a, u_b), (u_b, u_a), (u_a, u_b))):
            first = 1 + stage if end == 0 else planes - 1 - HALO - stage
            relax(first, first + HALO, source, target, f_e, w_e, parts, True)
            known = first + HALO if end == 0 else first - 2
            for c in range(3):
                target[c, known:known + 2] = u_edge[stage + 1, end, c]
        at = HALO if end == 0 else 1
        residual_pairs(at, HALO // 2, HALO // 2 * end, rows, u_b, f_e, m.at[end], d_e, parts, pairs, True)
        for c in range(3):
            if end == 0:
                u_out[c, :HALO - 1] = ub[end, c, HALO:2 * HALO - 1, :rows]
            else:
                u_out[c, own - HALO + 1:] = ub[end, c, planes - 2 * HALO + 1:planes - HALO, :rows]
    u_out[:, HALO - 1:own - HALO + 1] = u_mid[...]
    ends = pool_pairs(pairs, pooled)
    for c in range(4):
        at = HALO * c
        packet[half * c:half * c + 2] = ends[at:at + 2]
        packet[half * c + 2:half * (c + 1) - 2] = packet_mid[(half - HALO) * c:(half - HALO) * (c + 1)]
        packet[half * (c + 1) - 2:half * (c + 1)] = ends[at + 2:at + 4]


def middle_kernel(scale, p_in, y_first, y_second, x_first, x_second, u_out, packet,
                  ua, ub, f, m, cx, cym, cyp, czm, czp, weight, diag, pairs, pooled):
    place = own_place()
    own, rows = p_in.shape[1:3]
    body = pl.ds(HALO, own)
    planes = own + 2 * HALO
    total_rows = m.shape[1]
    even_x, even_y = is_even(place[0]), is_even(place[1])
    for c in range(4):
        if c < 3:
            field = f.at[c]
        else:
            field = m
        if total_rows > rows + 2 * HALO:
            field[body] = jnp.zeros((own,) + m.shape[1:], jnp.float32)
        field[body, :rows] = p_in[c]
        field[body, rows:rows + HALO] = jnp.where(even_y, y_first[c], y_second[c])
        field[body, total_rows - HALO:] = jnp.where(even_y, y_second[c], y_first[c])
        field[:HALO] = jnp.where(even_x, x_second[c], x_first[c])
        field[HALO + own:] = jnp.where(even_x, x_first[c], x_second[c])
    shape = m.shape[1:]
    in_rows = inside_rows(place, rows, total_rows, shape)
    in_lower = inside_rows(place, rows, total_rows, shape, place[0] > 0)
    in_upper = inside_rows(place, rows, total_rows, shape, place[0] < place[2] - 1)
    m[body] = jnp.where(in_rows, m[body], 0.0)
    m[:HALO] = jnp.where(in_lower, m[:HALO], 0.0)
    m[HALO + own:] = jnp.where(in_upper, m[HALO + own:], 0.0)
    make_coefficients(scale, 1, planes - 1, m, cx, cym, cyp, czm, czp, weight, diag, unroll=True)
    faces = (cx, cym, cyp, czm, czp)
    start_from_zero(1, planes - 1, ub, f, weight, unroll=True)
    relax(2, planes - 2, ub, ua, f, weight, faces, unroll=True)
    relax(3, planes - 3, ua, ub, f, weight, faces, unroll=True)
    lanes = u_out.shape[-1]
    for c in range(3):
        u_out[c] = ub[c, body, :rows, :lanes]
    residual_pairs(HALO, own // 2, 0, rows, ub, f, m, diag, faces, pairs, unroll=True)
    if rows > 4:
        packet[...] = pool_pairs(pairs, pooled)
    else:
        for c in range(4):
            for p in range(own // 2):
                for q in range(rows // 2):
                    at = 128 * (p * (rows // 2) + q)
                    pooled[c:c + 1, at:at + 128] = (
                        pairs[c, p, 2 * q:2 * q + 1] + pairs[c, p, 2 * q + 1:2 * q + 2]
                    )
        depth = pooled.shape[1]
        source = lax.broadcasted_iota(jnp.int32, (depth, 128), 0)
        target = lax.broadcasted_iota(jnp.int32, (depth, 128), 1)
        hit = (source // 128 * 32 + source % 128 // 2 == target) & (source % 128 < 64)
        pool = jnp.where(hit, 0.125, 0.0).astype(jnp.bfloat16)
        packet[...] = split_dot(pooled[...], pool)[:4]


def window_kernel(column, out, rows_of):
    count = column.shape[0]
    width = rows_of.shape[0] // 4
    x_at = lax.axis_index("gx")
    for r in range(width):
        i = x_at + (r - REACH)
        value = jnp.where((i >= 0) & (i < count), column[jnp.clip(i, 0, count - 1)], 0.0)
        for c in range(4):
            rows_of[width * c + r:width * c + r + 1] = value[c:c + 1]
    out[...] = jnp.broadcast_to(rows_of[...][None], out.shape)


def last_kernel(g, u3_out, u4_out, r4_out, fw, mw, ua, ub, faces, weight, diag,
                f4, m4, faces4, weight4, diag4, va, vb, rows_out):
    count, width = g.shape[0], g.shape[1] // 4
    rows, lanes = mw.shape[1:]
    shape = (rows, lanes)
    lane = lax.broadcasted_iota(jnp.int32, shape, 1)
    x_one, y_one, z = lane // 64 == 1, lane // 32 % 2 == 1, lane % 32
    zero = jnp.zeros(shape, jnp.float32)
    y_at = lax.axis_index("gy")
    window = 2 * REACH + 1
    for w in range(window):
        i = y_at + (w - REACH)
        inside = (i >= 0) & (i < count)
        i = jnp.clip(i, 0, count - 1)
        for c in range(4):
            place = fw.at[c, w] if c < 3 else mw.at[w]
            place[:width] = jnp.where(inside, g[i, width * c:width * (c + 1)], 0.0)
            place[width:] = zero[width:]

    def shifted_rows(value):
        return pltpu.roll(value, 1, 0), pltpu.roll(value, rows - 1, 0)

    def near3(get, w, turned):
        for j in (w - 1, w, w + 1):
            if j not in turned:
                inside = 0 <= j < window
                turned[j] = (pltpu.roll(get(j), 32, 1), pltpu.roll(get(j), lanes - 32, 1)) if inside else (zero, zero)
        centre = get(w)
        other = pltpu.roll(centre, 64, 1)
        lower, upper = shifted_rows(other)
        x_out = jnp.where(x_one, upper, lower)
        y_in = jnp.where(y_one, turned[w][0], turned[w][1])
        y_out = jnp.where(y_one, turned[w + 1][0], turned[w - 1][1])
        return centre, (other, x_out, y_in, y_out, pltpu.roll(centre, 1, 1), pltpu.roll(centre, lanes - 1, 1))

    outside3 = (None, None, None, None, z == 0, z == 31)

    def near4(get, w, turned):
        centre = get(w)
        lower, upper = shifted_rows(centre)
        return centre, (lower, upper, get(w - 1), get(w + 1),
                        pltpu.roll(centre, 2, 1), pltpu.roll(centre, lanes - 2, 1))

    outside4 = (None, None, None, None, z < 2, z >= 30)

    def level(scale, near, outside, f, m, faces, weight, diag, ua, ub, spans, residual):
        half = 0.5 * scale
        turned = {}
        for w in spans[0]:
            centre, sides = near(lambda j: m[j], w, turned)
            total = jnp.full(shape, mass_term, jnp.float32)
            for k in range(6):
                side = sides[k] if outside[k] is None else jnp.where(outside[k], 0.0, sides[k])
                face = half * (centre + side)
                total = total + face
                faces[k, w] = face if outside[k] is None else jnp.where(outside[k], 0.0, face)
            diag[w] = total
            weight[w] = jnp.where(centre > 0.0, damping / total, 0.0)
            for c in range(3):
                ua[c, w] = weight[w] * f[c, w]

        def flux_at(u, c, w, turned):
            centre, sides = near(lambda j: u[c, j], w, turned)
            flux = faces[0, w] * sides[0]
            for k in range(1, 6):
                flux = flux + faces[k, w] * sides[k]
            return centre, flux

        for source, target, span in ((ua, ub, spans[1]), (ub, ua, spans[2])):
            for c in range(3):
                turned = {}
                for w in span:
                    centre, flux = flux_at(source, c, w, turned)
                    target[c, w] = (1.0 - damping) * centre + weight[w] * (f[c, w] + flux)
        for c in range(3):
            turned = {}
            for w in spans[3]:
                centre, flux = flux_at(ua, c, w, turned)
                residual(c, w, f[c, w] + flux - diag[w] * centre)

    def pool(value):
        value = value + pltpu.roll(value, 64, 1)
        value = value + pltpu.roll(value, 32, 1)
        return 0.125 * (value + pltpu.roll(value, lanes - 1, 1))

    def to_level4(c, w, value):
        f4[c, w] = pool(value)

    spans = (range(window), range(1, window - 1), range(1, window - 1), range(2, window - 2))
    level(0.25**3, near3, outside3, fw, mw, faces, weight, diag, ua, ub, spans, to_level4)
    for w in range(1, window - 1):
        m4[w] = pool(mw[w])

    def own_row(value):
        return value[REACH:REACH + 1]

    def keep(c, w, value):
        rows_out[3 + c:4 + c] = own_row(value)

    spans = tuple(range(2 + k, window - 2 - k) for k in range(4))
    level(0.25**4, near4, outside4, f4, m4, faces4, weight4, diag4, va, vb, spans, keep)
    for c in range(3):
        value = own_row(ua[c, REACH])
        rows_out[c:c + 1] = own_row(va[c, REACH])
        for k in range(4):
            turned = value if k == 0 else pltpu.roll(value, lanes - 32 * k, 1)
            u3_out[c, k // 2, k % 2:k % 2 + 1] = turned[:, :32]
    source = lax.broadcasted_iota(jnp.int32, (lanes, lanes), 0)
    target = lax.broadcasted_iota(jnp.int32, (lanes, lanes), 1)
    take = jnp.where((source == 2 * target) & (target < 16), 1.0, 0.0).astype(jnp.bfloat16)
    ends = split_dot(rows_out[...], take)
    for c in range(3):
        u4_out[c, 0] = ends[c:c + 1, :16]
        r4_out[c, 0] = ends[3 + c:4 + c, :16]


def viscosity_of(kind, viscosities):
    return jnp.where(
        kind < 2,
        jnp.where(kind == 0, viscosities[0], viscosities[1]),
        jnp.where(kind == 2, viscosities[2], viscosities[3]),
    )


def pack_kernel(viscosities, u_in, f_in, types, y_first, y_second, x_first, x_second, kinds, done):
    place = own_place()
    own, rows = types.shape[:2]
    even_x, even_y = is_even(place[0]), is_even(place[1])
    upper, upper_f, lower = own - HALO, own - HALO + 1, 0
    at_first, at_second = jnp.where(even_x, upper, lower), jnp.where(even_x, lower, upper)
    f_first, f_second = jnp.where(even_x, upper_f, lower), jnp.where(even_x, lower, upper_f)
    always, if_even, if_odd = [(types, kinds)], [], []
    at = 3 * HALO
    for c in range(3):
        for k, field in ((0, u_in), (3, f_in)):
            top, bottom = field.at[c, :, pl.ds(rows - HALO, HALO)], field.at[c, :, pl.ds(0, HALO)]
            if_even += [(top, y_first.at[k + c]), (bottom, y_second.at[k + c])]
            if_odd += [(bottom, y_first.at[k + c]), (top, y_second.at[k + c])]
        here = pl.ds(HALO * c, HALO)
        always.append((u_in.at[c, pl.ds(at_first, HALO)], x_first.at[here]))
        always.append((u_in.at[c, pl.ds(at_second, HALO)], x_second.at[here]))
        here = pl.ds(at, HALO - 1)
        always.append((f_in.at[c, pl.ds(f_first, HALO - 1)], x_first.at[here]))
        always.append((f_in.at[c, pl.ds(f_second, HALO - 1)], x_second.at[here]))
        at += HALO - 1

    def copies(pairs, first):
        return [pltpu.make_async_copy(*pair, done.at[first + i]) for i, pair in enumerate(pairs)]

    def start(pairs, first):
        for copy in copies(pairs, first):
            copy.start()

    start(always[:1], 0)
    pl.when(even_y)(lambda: start(if_even, len(always)))
    pl.when(jnp.logical_not(even_y))(lambda: start(if_odd, len(always)))
    start(always[1:], 1)
    copies(always[:1], 0)[0].wait()
    top = viscosity_of(kinds[:, rows - HALO:], viscosities)
    bottom = viscosity_of(kinds[:, :HALO], viscosities)
    y_first[6], y_second[6] = jnp.where(even_y, top, bottom), jnp.where(even_y, bottom, top)
    x_first[at:] = viscosity_of(kinds[pl.ds(at_first, HALO)], viscosities)
    x_second[at:] = viscosity_of(kinds[pl.ds(at_second, HALO)], viscosities)
    for copy in copies(always[1:], 1) + copies(if_even, len(always)):
        copy.wait()


def corner_layers(count):
    at = 0
    for channel in range(7):
        deep = HALO - 2 if 3 <= channel < 6 else HALO - 1
        if channel == count:
            return at, deep
        at += deep
    return at, 0


def corner_kernel(y_first, y_second, first, second):
    own = y_first.shape[1]
    even = is_even(lax.axis_index("gx"))
    for channel in range(7):
        at, deep = corner_layers(channel)
        for target, upper in ((first, even), (second, jnp.logical_not(even))):
            planes = pl.ds(jnp.where(upper, own - deep, 0), deep)
            target[at:at + deep, :HALO] = y_first[channel, planes]
            target[at:at + deep, HALO:] = y_second[channel, planes]


def on_chip(count):
    return [pl.BlockSpec(memory_space=pltpu.VMEM)] * count


def planes_scratch(planes, rows, lanes, pairs, own_rows, pooled, ends=()):
    block = (planes, rows, lanes)
    return (
        [pltpu.VMEM(ends + (3,) + block, jnp.float32)] * 3
        + [pltpu.VMEM(ends + block, jnp.float32)] * 8
        + [pltpu.VMEM((4, pairs, own_rows, lanes), jnp.float32), pltpu.VMEM(pooled, jnp.float32)]
    )


PACK_LIMIT = 62 * 1024 * 1024
LIMIT = pltpu.CompilerParams(vmem_limit_bytes=20 * 1024 * 1024)


def on_device(velocity_guess, forcing, cell_type, viscosities):
    f32 = jnp.float32
    count_x, count_y = lax.axis_size("gx"), lax.axis_size("gy")
    even_x, even_y = is_even(lax.axis_index("gx")), is_even(lax.axis_index("gy"))
    in_smem = [pl.BlockSpec(memory_space=pltpu.SMEM)]
    own, rows, lanes = cell_type.shape
    y_edge = jax.ShapeDtypeStruct((7, own, HALO, lanes), f32)
    x_edge = jax.ShapeDtypeStruct((7 * HALO - 3, rows, lanes), f32)
    y_out, y_out_odd, x_out, x_out_odd = pl.pallas_call(
        pack_kernel,
        out_shape=(y_edge, y_edge, x_edge, x_edge),
        in_specs=in_smem + [pl.BlockSpec(memory_space=pl.ANY)] * 3,
        out_specs=tuple(on_chip(4)),
        scratch_shapes=[pltpu.VMEM(cell_type.shape, jnp.int32), pltpu.SemaphoreType.DMA((25,))],
        compiler_params=pltpu.CompilerParams(vmem_limit_bytes=PACK_LIMIT),
    )(viscosities, velocity_guess, forcing, cell_type)
    y_halo = swapped(y_out, y_out_odd, "gy")
    x_halo = swapped(x_out, x_out_odd, "gx")
    corner = jax.ShapeDtypeStruct((corner_layers(7)[0], 2 * HALO, lanes), f32)
    corners = pl.pallas_call(
        corner_kernel,
        out_shape=(corner, corner),
        in_specs=on_chip(2),
        out_specs=tuple(on_chip(2)),
        compiler_params=LIMIT,
    )(*y_halo)
    corner_halo = swapped(*corners, "gx")
    tall = rows + 2 * HALO
    middle = own // 2 - HALO
    state = (
        (3, own - 2 * HALO + 2, rows, lanes),
        (4 * middle, rows // 2, lanes // 2),
        (4, 2, 3, 2, tall, lanes),
        (2, 3, HALO, tall, lanes),
        (2, HALO + 1, tall, lanes),
    )
    known = pl.pallas_call(
        inner_kernel,
        out_shape=tuple(jax.ShapeDtypeStruct(shape, f32) for shape in state),
        in_specs=in_smem + on_chip(5),
        out_specs=tuple(on_chip(5)),
        scratch_shapes=planes_scratch(own + 2 * HALO, tall, lanes, middle, rows, (4 * middle, rows, 128)),
        compiler_params=LIMIT,
        cost_estimate=pl.CostEstimate(flops=60_000_000, bytes_accessed=6_000_000, transcendentals=0),
    )(viscosities, velocity_guess, forcing, cell_type, *y_halo)
    u0, packet = pl.pallas_call(
        outer_kernel,
        out_shape=(
            jax.ShapeDtypeStruct(velocity_guess.shape, f32),
            jax.ShapeDtypeStruct((4 * own // 2, rows // 2, lanes // 2), f32),
        ),
        in_specs=on_chip(9),
        out_specs=tuple(on_chip(2)),
        scratch_shapes=planes_scratch(2 * HALO + 1, tall, lanes, HALO, rows, (4 * HALO, rows, 128), (2,)),
        compiler_params=LIMIT,
    )(*known, *x_halo, *corner_halo)
    results = [u0]
    for grid_level in (1, 2):
        own, rows = own // 2, rows // 2
        packet = packet.reshape(4, own, rows, 128)
        valid = 256 >> grid_level
        top, bottom = packet[:, :, rows - HALO:], packet[:, :, :HALO]
        y_halo = swapped(jnp.where(even_y, top, bottom), jnp.where(even_y, bottom, top), "gy")
        upper, lower = jnp.where(even_y, y_halo[0], y_halo[1]), jnp.where(even_y, y_halo[1], y_halo[0])
        parts = [packet, upper, lower]
        total_rows = rows + 2 * HALO
        if total_rows % 8:
            parts = [packet, upper, jnp.zeros_like(upper), lower]
            total_rows += HALO
        top, bottom = (
            jnp.concatenate([part[:, at:at + HALO] for part in parts], axis=2) for at in (own - HALO, 0)
        )
        x_halo = swapped(jnp.where(even_x, top, bottom), jnp.where(even_x, bottom, top), "gx")
        if grid_level == 1:
            packet_shape, pooled_shape = (4 * own // 2, rows // 2, 128), (4 * own // 2, rows, 128)
        else:
            packet_shape, pooled_shape = (4, 128), (8, 512)
        u_own, packet = pl.pallas_call(
            functools.partial(middle_kernel, 0.25**grid_level),
            out_shape=(
                jax.ShapeDtypeStruct((3, own, rows, valid), f32),
                jax.ShapeDtypeStruct(packet_shape, f32),
            ),
            in_specs=on_chip(5),
            out_specs=tuple(on_chip(2)),
            scratch_shapes=planes_scratch(own + 2 * HALO, total_rows, 128, own // 2, rows, pooled_shape),
            compiler_params=LIMIT,
        )(packet, *y_halo, *x_halo)
        results.append(u_own)
    column = lax.all_to_all(jnp.broadcast_to(packet[None], (count_x, 4, 128)), "gx", 0, 0)
    width = 2 * REACH + 2
    window = pl.pallas_call(
        window_kernel,
        out_shape=jax.ShapeDtypeStruct((count_y, 4 * width, 128), f32),
        in_specs=on_chip(1),
        out_specs=on_chip(1)[0],
        scratch_shapes=[pltpu.VMEM((4 * width, 128), f32)],
        compiler_params=LIMIT,
    )(column)
    gathered = lax.all_to_all(window, "gy", 0, 0)
    block = (2 * REACH + 1, 16, 128)
    field, vector, six = (pltpu.VMEM(lead + block, f32) for lead in ((), (3,), (6,)))
    last = pl.pallas_call(
        last_kernel,
        out_shape=tuple(jax.ShapeDtypeStruct(shape, f32) for shape in ((3, 2, 2, 32), (3, 1, 1, 16), (3, 1, 1, 16))),
        in_specs=on_chip(1),
        out_specs=tuple(on_chip(3)),
        scratch_shapes=[vector, field, vector, vector, six, field, field,
                        vector, field, six, field, field, vector, vector, pltpu.VMEM((8, 128), f32)],
        compiler_params=LIMIT,
    )(gathered)
    return (*results, *last)


def solution(mesh):
    return jax.shard_map(
        on_device,
        mesh=mesh,
        in_specs=(P(None, "gx", "gy", None), P(None, "gx", "gy", None), P("gx", "gy", None), P()),
        out_specs=(P(None, "gx", "gy", None),) * 6,
        check_vma=False,
    )
```

```python
import functools

import jax
import jax.numpy as jnp
from jax import lax
from jax.experimental import pallas as pl
from jax.experimental.pallas import tpu as pltpu
from jax.sharding import PartitionSpec as P

SWEEPS = 3
LEVELS = 4
HALO = SWEEPS + 1
REACH = 5

damping = 0.8
mass_term = 0.05


def pair_swap(value, axis, odd):
    sizes = {name: lax.axis_size(name) for name in ("gx", "gy")}
    route = []
    for x in range(sizes["gx"]):
        for y in range(sizes["gy"]):
            place = {"gx": x, "gy": y}
            other = ((place[axis] + odd) ^ 1) - odd
            if 0 <= other < sizes[axis]:
                place[axis] = other
            else:
                across = "gy" if axis == "gx" else "gx"
                place[across] ^= 1
            route.append((x * sizes["gy"] + y, place["gx"] * sizes["gy"] + place["gy"]))
    return lax.ppermute(value, ("gx", "gy"), route)


def swapped(to_even, to_odd, axis):
    return pair_swap(to_even, axis, 0), pair_swap(to_odd, axis, 1)


def own_place():
    return lax.axis_index("gx"), lax.axis_index("gy"), lax.axis_size("gx"), lax.axis_size("gy")


def is_even(position):
    return position % 2 == 0


def split_dot(rows, pool):
    total = None
    for part in range(3):
        piece = rows.astype(jnp.bfloat16)
        term = jnp.dot(piece, pool, preferred_element_type=jnp.float32)
        total = term if total is None else total + term
        if part < 2:
            rows = rows - piece.astype(jnp.float32)
    return total


def inside_rows(place, own_rows, total_rows, shape, along_x=True):
    row = lax.broadcasted_iota(jnp.int32, shape, 0)
    above = jnp.where(place[1] < place[3] - 1, own_rows + HALO, own_rows)
    below = jnp.where(place[1] > 0, total_rows - HALO, total_rows)
    above = jnp.where(along_x, above, 0)
    below = jnp.where(along_x, below, total_rows)
    return (row < above) | (row >= below)


def pair_pool(lanes):
    source = lax.broadcasted_iota(jnp.int32, (lanes, 128), 0)
    target = lax.broadcasted_iota(jnp.int32, (lanes, 128), 1)
    return jnp.where(source // 2 == target, 0.125, 0.0).astype(jnp.bfloat16)


def make_coefficients(scale, lo, hi, m, cx, cym, cyp, czm, czp, weight, diag, unroll=False):
    rows, lanes = m.shape[1:]
    half = 0.5 * scale
    lane = lax.broadcasted_iota(jnp.int32, (rows, lanes), 1)
    cx[lo - 1] = half * (m[lo - 1] + m[lo])

    def plane(i, _):
        centre = m[i]
        upper = m[i + 1]
        y_lower = pltpu.roll(centre, 1, 0)
        y_upper = pltpu.roll(centre, rows - 1, 0)
        z_lower = jnp.where(lane == 0, 0.0, pltpu.roll(centre, 1, 1))
        z_upper = jnp.where(lane == lanes - 1, 0.0, pltpu.roll(centre, lanes - 1, 1))
        f_xl, f_xu = half * (centre + m[i - 1]), half * (centre + upper)
        f_yl, f_yu = half * (centre + y_lower), half * (centre + y_upper)
        f_zl, f_zu = half * (centre + z_lower), half * (centre + z_upper)
        total = mass_term + (f_xl + f_xu + f_yl + f_yu + f_zl + f_zu)
        cx[i] = f_xu
        cym[i], cyp[i] = f_yl, f_yu
        czm[i] = jnp.where(lane == 0, 0.0, f_zl)
        czp[i] = jnp.where(lane == lanes - 1, 0.0, f_zu)
        diag[i] = total
        weight[i] = jnp.where(centre > 0.0, damping / total, 0.0)
        return 0

    lax.fori_loop(lo, hi, plane, 0, unroll=unroll)


def flux_of(u, c, i, cx, cym, cyp, czm, czp):
    rows, lanes = u.shape[2:]
    centre = u[c, i]
    flux = cx[i - 1] * u[c, i - 1] + cx[i] * u[c, i + 1]
    flux += cym[i] * pltpu.roll(centre, 1, 0) + cyp[i] * pltpu.roll(centre, rows - 1, 0)
    flux += czm[i] * pltpu.roll(centre, 1, 1) + czp[i] * pltpu.roll(centre, lanes - 1, 1)
    return centre, flux


def relax(lo, hi, source, target, f, weight, faces, unroll=False):
    def plane(i, _):
        for c in range(3):
            centre, flux = flux_of(source, c, i, *faces)
            target[c, i] = (1.0 - damping) * centre + weight[i] * (f[c, i] + flux)
        return 0

    lax.fori_loop(lo, hi, plane, 0, unroll=unroll)


def start_from_zero(lo, hi, target, f, weight, unroll=False):
    def plane(i, _):
        for c in range(3):
            target[c, i] = weight[i] * f[c, i]
        return 0

    lax.fori_loop(lo, hi, plane, 0, unroll=unroll)


def residual_pairs(at, count, first, own_rows, u, f, m, diag, faces, pairs, unroll=False):
    def pair(p, _):
        i = at + 2 * p
        for c in range(3):
            both = None
            for j in (i, i + 1):
                centre, flux = flux_of(u, c, j, *faces)
                value = f[c, j] + flux - diag[j] * centre
                both = value if both is None else both + value
            pairs[c, first + p] = both[:own_rows]
        pairs[3, first + p] = (m[i] + m[i + 1])[:own_rows]
        return 0

    lax.fori_loop(0, count, pair, 0, unroll=unroll)


def pool_pairs(pairs, pooled):
    lanes = pairs.shape[-1]
    rows = pooled.shape[1]
    summed = split_dot(pairs[...].reshape(-1, lanes), pair_pool(lanes))
    pooled[...] = summed.reshape(pooled.shape)
    return pooled[:, pl.ds(0, rows // 2, 2), :] + pooled[:, pl.ds(1, rows // 2, 2), :]


def inner_kernel(viscosities, u_in, f_in, types, y_first, y_second, u_mid, packet_mid, u_edge, f_edge, m_edge,
                 ua, ub, f, m, cx, cym, cyp, czm, czp, weight, diag, pairs, pooled):
    place = own_place()
    own, rows = u_in.shape[1:3]
    body = pl.ds(HALO, own)
    last = HALO + own
    has_lower, has_upper = place[1] > 0, place[1] < place[3] - 1
    even = is_even(place[1])

    def put_rows(field, channel, masked):
        first, second = y_first[channel], y_second[channel]
        upper, lower = jnp.where(even, first, second), jnp.where(even, second, first)
        field[body, rows:rows + HALO] = jnp.where(has_upper, upper, 0.0) if masked else upper
        field[body, rows + HALO:] = jnp.where(has_lower, lower, 0.0) if masked else lower

    for c in range(3):
        ua[c, body, :rows] = u_in[c]
        put_rows(ua.at[c], c, True)
        f[c, body, :rows] = f_in[c]
        put_rows(f.at[c], 3 + c, False)
    m[body, :rows] = viscosity_of(types[...], viscosities)
    put_rows(m, 6, True)

    def edges(stage, u, depth):
        u_edge[stage, 0] = u[:, HALO + depth:HALO + depth + 2]
        u_edge[stage, 1] = u[:, last - depth - 2:last - depth]

    edges(0, ua, 0)
    f_edge[0], f_edge[1] = f[:, HALO:2 * HALO], f[:, last - HALO:last]
    m_edge[0], m_edge[1] = m[HALO:2 * HALO + 1], m[last - HALO - 1:last]
    make_coefficients(1.0, HALO + 1, last - 1, m, cx, cym, cyp, czm, czp, weight, diag, True)
    faces = (cx, cym, cyp, czm, czp)
    relax(HALO + 1, last - 1, ua, ub, f, weight, faces, True)
    edges(1, ub, 1)
    relax(HALO + 2, last - 2, ub, ua, f, weight, faces, True)
    edges(2, ua, 2)
    relax(HALO + 3, last - 3, ua, ub, f, weight, faces, True)
    edges(3, ub, 3)
    u_mid[...] = ub[:, HALO + 3:last - 3, :rows]
    residual_pairs(2 * HALO, own // 2 - HALO, 0, rows, ub, f, m, diag, faces, pairs, True)
    packet_mid[...] = pool_pairs(pairs, pooled)


def outer_kernel(u_mid, packet_mid, u_edge, f_edge, m_edge, x_first, x_second, corner_first, corner_second, u_out, packet,
                 ua, ub, f, m, cx, cym, cyp, czm, czp, weight, diag, pairs, pooled):
    place = own_place()
    own, rows = u_out.shape[1:3]
    planes = m.shape[1]
    count_f = HALO - 1
    at_f, at_m = 3 * HALO, 3 * HALO + 3 * count_f
    half = own // 2
    corner_shape = corner_first.shape[1:]
    even, even_y = is_even(place[0]), is_even(place[1])

    for end in range(2):
        take_first = even if end == 1 else jnp.logical_not(even)

        def halo(at, count):
            return jnp.where(take_first, x_first[at:at + count], x_second[at:at + count])

        def corner(at, count):
            rows_of = [corner_first[at + i] for i in range(count)], [corner_second[at + i] for i in range(count)]
            chosen = [jnp.where(take_first, one, two) for one, two in zip(*rows_of)]
            return jnp.stack([jnp.where(even_y, one, pltpu.roll(one, HALO, 0)) for one in chosen])

        outer = 0 if end == 0 else planes - HALO
        inner = HALO if end == 0 else 0
        present = place[0] > 0 if end == 0 else place[0] < place[2] - 1
        inside = inside_rows(place, 0, 2 * HALO, corner_shape, present)

        def put_corner(field, channel, masked):
            at, deep = corner_layers(channel)
            value = corner(at, deep)
            if masked:
                value = jnp.where(inside, value, 0.0)
            first = HALO - deep if end == 0 else planes - HALO
            field[first:first + deep, rows:] = value
            far = first - 1 if end == 0 else first + deep
            field[far, rows:] = jnp.zeros(corner_shape, jnp.float32)

        for c in range(3):
            ua[end, c, outer:outer + HALO, :rows] = jnp.where(present, halo(HALO * c, HALO), 0.0)
            put_corner(ua.at[end, c], c, True)
            nearest = HALO if end == 0 else planes - HALO - 2
            ua[end, c, nearest:nearest + 2] = u_edge[0, end, c]
            beyond = 1 if end == 0 else planes - HALO
            f[end, c, beyond:beyond + count_f, :rows] = halo(at_f + count_f * c, count_f)
            put_corner(f.at[end, c], 3 + c, False)
            own_f = HALO if end == 0 else planes - 2 * HALO
            f[end, c, own_f:own_f + HALO] = f_edge[end, c]
        m[end, outer:outer + HALO, :rows] = jnp.where(present, halo(at_m, HALO), 0.0)
        put_corner(m.at[end], 6, True)
        m[end, inner:inner + HALO + 1] = m_edge[end]
        parts = (cx.at[end], cym.at[end], cyp.at[end], czm.at[end], czp.at[end])
        u_a, u_b, f_e, w_e, d_e = ua.at[end], ub.at[end], f.at[end], weight.at[end], diag.at[end]
        make_coefficients(1.0, 1, planes - 1, m.at[end], *parts, w_e, d_e, True)
        for stage, (source, target) in enumerate(((u_a, u_b), (u_b, u_a), (u_a, u_b))):
            first = 1 + stage if end == 0 else planes - 1 - HALO - stage
            relax(first, first + HALO, source, target, f_e, w_e, parts, True)
            known = first + HALO if end == 0 else first - 2
            for c in range(3):
                target[c, known:known + 2] = u_edge[stage + 1, end, c]
        at = HALO if end == 0 else 1
        residual_pairs(at, HALO // 2, HALO // 2 * end, rows, u_b, f_e, m.at[end], d_e, parts, pairs, True)
        for c in range(3):
            if end == 0:
                u_out[c, :HALO - 1] = ub[end, c, HALO:2 * HALO - 1, :rows]
            else:
                u_out[c, own - HALO + 1:] = ub[end, c, planes - 2 * HALO + 1:planes - HALO, :rows]
    u_out[:, HALO - 1:own - HALO + 1] = u_mid[...]
    ends = pool_pairs(pairs, pooled)
    for c in range(4):
        at = HALO * c
        packet[half * c:half * c + 2] = ends[at:at + 2]
        packet[half * c + 2:half * (c + 1) - 2] = packet_mid[(half - HALO) * c:(half - HALO) * (c + 1)]
        packet[half * (c + 1) - 2:half * (c + 1)] = ends[at + 2:at + 4]


def middle_kernel(scale, p_in, y_first, y_second, x_first, x_second, u_out, packet,
                  ua, ub, f, m, cx, cym, cyp, czm, czp, weight, diag, pairs, pooled):
    place = own_place()
    own, rows = p_in.shape[1:3]
    body = pl.ds(HALO, own)
    planes = own + 2 * HALO
    total_rows = m.shape[1]
    even_x, even_y = is_even(place[0]), is_even(place[1])
    for c in range(4):
        if c < 3:
            field = f.at[c]
        else:
            field = m
        if total_rows > rows + 2 * HALO:
            field[body] = jnp.zeros((own,) + m.shape[1:], jnp.float32)
        field[body, :rows] = p_in[c]
        field[body, rows:rows + HALO] = jnp.where(even_y, y_first[c], y_second[c])
        field[body, total_rows - HALO:] = jnp.where(even_y, y_second[c], y_first[c])
        below = jnp.where(even_x, x_second[c], x_first[c])
        above = jnp.where(even_x, x_first[c], x_second[c])
        for start, value in ((0, below), (HALO + own, above)):
            if value.shape[1] == total_rows:
                field[start:start + HALO] = value
                continue
            half = value.shape[1]
            left = lax.broadcasted_iota(jnp.int32, value.shape[1:], 1) < 64
            for i in range(HALO):
                field[start + i, :half] = jnp.where(left, value[i], 0.0)
                field[start + i, half:] = jnp.where(left, pltpu.roll(value[i], 64, 1), 0.0)
    shape = m.shape[1:]
    in_rows = inside_rows(place, rows, total_rows, shape)
    in_lower = inside_rows(place, rows, total_rows, shape, place[0] > 0)
    in_upper = inside_rows(place, rows, total_rows, shape, place[0] < place[2] - 1)
    m[body] = jnp.where(in_rows, m[body], 0.0)
    m[:HALO] = jnp.where(in_lower, m[:HALO], 0.0)
    m[HALO + own:] = jnp.where(in_upper, m[HALO + own:], 0.0)
    make_coefficients(scale, 1, planes - 1, m, cx, cym, cyp, czm, czp, weight, diag, unroll=True)
    faces = (cx, cym, cyp, czm, czp)
    start_from_zero(1, planes - 1, ub, f, weight, unroll=True)
    relax(2, planes - 2, ub, ua, f, weight, faces, unroll=True)
    relax(3, planes - 3, ua, ub, f, weight, faces, unroll=True)
    lanes = u_out.shape[-1]
    for c in range(3):
        u_out[c] = ub[c, body, :rows, :lanes]
    residual_pairs(HALO, own // 2, 0, rows, ub, f, m, diag, faces, pairs, unroll=True)
    if rows > 4:
        packet[...] = pool_pairs(pairs, pooled)
    else:
        for c in range(4):
            for p in range(own // 2):
                for q in range(rows // 2):
                    at = 128 * (p * (rows // 2) + q)
                    pooled[c:c + 1, at:at + 128] = (
                        pairs[c, p, 2 * q:2 * q + 1] + pairs[c, p, 2 * q + 1:2 * q + 2]
                    )
        depth = pooled.shape[1]
        source = lax.broadcasted_iota(jnp.int32, (depth, 128), 0)
        target = lax.broadcasted_iota(jnp.int32, (depth, 128), 1)
        hit = (source // 128 * 32 + source % 128 // 2 == target) & (source % 128 < 64)
        pool = jnp.where(hit, 0.125, 0.0).astype(jnp.bfloat16)
        packet[...] = split_dot(pooled[...], pool)[:4]


def window_kernel(column, out, rows_of):
    count = column.shape[0]
    width = rows_of.shape[0] // 4
    x_at = lax.axis_index("gx")
    for r in range(width):
        i = x_at + (r - REACH)
        value = jnp.where((i >= 0) & (i < count), column[jnp.clip(i, 0, count - 1)], 0.0)
        for c in range(4):
            rows_of[width * c + r:width * c + r + 1] = value[c:c + 1]
    out[...] = jnp.broadcast_to(rows_of[...][None], out.shape)


def last_kernel(g, u3_out, u4_out, r4_out, fw, mw, ua, ub, faces, weight, diag,
                f4, m4, faces4, weight4, diag4, va, vb, rows_out):
    count, width = g.shape[0], g.shape[1] // 4
    rows, lanes = mw.shape[1:]
    shape = (rows, lanes)
    lane = lax.broadcasted_iota(jnp.int32, shape, 1)
    x_one, y_one, z = lane // 64 == 1, lane // 32 % 2 == 1, lane % 32
    zero = jnp.zeros(shape, jnp.float32)
    y_at = lax.axis_index("gy")
    window = 2 * REACH + 1
    for w in range(window):
        i = y_at + (w - REACH)
        inside = (i >= 0) & (i < count)
        i = jnp.clip(i, 0, count - 1)
        for c in range(4):
            place = fw.at[c, w] if c < 3 else mw.at[w]
            place[:width] = jnp.where(inside, g[i, width * c:width * (c + 1)], 0.0)
            place[width:] = zero[width:]

    def shifted_rows(value):
        return pltpu.roll(value, 1, 0), pltpu.roll(value, rows - 1, 0)

    def near3(get, w, turned):
        for j in (w - 1, w, w + 1):
            if j not in turned:
                inside = 0 <= j < window
                turned[j] = (pltpu.roll(get(j), 32, 1), pltpu.roll(get(j), lanes - 32, 1)) if inside else (zero, zero)
        centre = get(w)
        other = pltpu.roll(centre, 64, 1)
        lower, upper = shifted_rows(other)
        x_out = jnp.where(x_one, upper, lower)
        y_in = jnp.where(y_one, turned[w][0], turned[w][1])
        y_out = jnp.where(y_one, turned[w + 1][0], turned[w - 1][1])
        return centre, (other, x_out, y_in, y_out, pltpu.roll(centre, 1, 1), pltpu.roll(centre, lanes - 1, 1))

    outside3 = (None, None, None, None, z == 0, z == 31)

    def near4(get, w, turned):
        centre = get(w)
        lower, upper = shifted_rows(centre)
        return centre, (lower, upper, get(w - 1), get(w + 1),
                        pltpu.roll(centre, 2, 1), pltpu.roll(centre, lanes - 2, 1))

    outside4 = (None, None, None, None, z < 2, z >= 30)

    def level(scale, near, outside, f, m, faces, weight, diag, ua, ub, spans, residual):
        half = 0.5 * scale
        turned = {}
        for w in spans[0]:
            centre, sides = near(lambda j: m[j], w, turned)
            total = jnp.full(shape, mass_term, jnp.float32)
            for k in range(6):
                side = sides[k] if outside[k] is None else jnp.where(outside[k], 0.0, sides[k])
                face = half * (centre + side)
                total = total + face
                faces[k, w] = face if outside[k] is None else jnp.where(outside[k], 0.0, face)
            diag[w] = total
            weight[w] = jnp.where(centre > 0.0, damping / total, 0.0)
            for c in range(3):
                ua[c, w] = weight[w] * f[c, w]

        def flux_at(u, c, w, turned):
            centre, sides = near(lambda j: u[c, j], w, turned)
            flux = faces[0, w] * sides[0]
            for k in range(1, 6):
                flux = flux + faces[k, w] * sides[k]
            return centre, flux

        for source, target, span in ((ua, ub, spans[1]), (ub, ua, spans[2])):
            for c in range(3):
                turned = {}
                for w in span:
                    centre, flux = flux_at(source, c, w, turned)
                    target[c, w] = (1.0 - damping) * centre + weight[w] * (f[c, w] + flux)
        for c in range(3):
            turned = {}
            for w in spans[3]:
                centre, flux = flux_at(ua, c, w, turned)
                residual(c, w, f[c, w] + flux - diag[w] * centre)

    def pool(value):
        value = value + pltpu.roll(value, 64, 1)
        value = value + pltpu.roll(value, 32, 1)
        return 0.125 * (value + pltpu.roll(value, lanes - 1, 1))

    def to_level4(c, w, value):
        f4[c, w] = pool(value)

    spans = (range(window), range(1, window - 1), range(1, window - 1), range(2, window - 2))
    level(0.25**3, near3, outside3, fw, mw, faces, weight, diag, ua, ub, spans, to_level4)
    for w in range(1, window - 1):
        m4[w] = pool(mw[w])

    def own_row(value):
        return value[REACH:REACH + 1]

    def keep(c, w, value):
        rows_out[3 + c:4 + c] = own_row(value)

    spans = tuple(range(2 + k, window - 2 - k) for k in range(4))
    level(0.25**4, near4, outside4, f4, m4, faces4, weight4, diag4, va, vb, spans, keep)
    for c in range(3):
        value = own_row(ua[c, REACH])
        rows_out[c:c + 1] = own_row(va[c, REACH])
        for k in range(4):
            turned = value if k == 0 else pltpu.roll(value, lanes - 32 * k, 1)
            u3_out[c, k // 2, k % 2:k % 2 + 1] = turned[:, :32]
    source = lax.broadcasted_iota(jnp.int32, (lanes, lanes), 0)
    target = lax.broadcasted_iota(jnp.int32, (lanes, lanes), 1)
    take = jnp.where((source == 2 * target) & (target < 16), 1.0, 0.0).astype(jnp.bfloat16)
    ends = split_dot(rows_out[...], take)
    for c in range(3):
        u4_out[c, 0] = ends[c:c + 1, :16]
        r4_out[c, 0] = ends[3 + c:4 + c, :16]


def viscosity_of(kind, viscosities):
    return jnp.where(
        kind < 2,
        jnp.where(kind == 0, viscosities[0], viscosities[1]),
        jnp.where(kind == 2, viscosities[2], viscosities[3]),
    )


def start_all(pairs, done):
    copies = [pltpu.make_async_copy(*pair, done.at[i]) for i, pair in enumerate(pairs)]
    for copy in copies:
        copy.start()
    return copies


def pack_rows_kernel(viscosities, u_in, f_in, types, first, second, turn, kinds, done):
    own, rows = types.shape[:2]
    even = is_even(lax.axis_index("gy"))
    if_even, if_odd = [(types, kinds)], [(types, kinds)]
    for c in range(6):
        field = u_in.at[c] if c < 3 else f_in.at[c - 3]
        top, bottom = field.at[:, pl.ds(rows - HALO, HALO)], field.at[:, pl.ds(0, HALO)]
        if_even += [(top, first.at[c]), (bottom, second.at[c])]
        if_odd += [(bottom, first.at[c]), (top, second.at[c])]
    pl.when(even)(lambda: start_all(if_even, done) and None)
    pl.when(jnp.logical_not(even))(lambda: start_all(if_odd, done) and None)
    turn[...] = jnp.zeros(turn.shape, jnp.float32)
    waits = [pltpu.make_async_copy(*pair, done.at[i]) for i, pair in enumerate(if_even)]
    waits[0].wait()
    top = viscosity_of(kinds[:, rows - HALO:], viscosities)
    bottom = viscosity_of(kinds[:, :HALO], viscosities)
    first[6], second[6] = jnp.where(even, top, bottom), jnp.where(even, bottom, top)
    for copy in waits[1:]:
        copy.wait()


def pack_planes_kernel(viscosities, turn, u_in, f_in, types, first, second, kinds, done):
    own = types.shape[0]
    even = is_even(lax.axis_index("gx"))
    starts = [
        (jnp.where(upper, own - HALO, 0), jnp.where(upper, own - HALO + 1, 0))
        for upper in (even, jnp.logical_not(even))
    ]
    pairs = [(types.at[pl.ds(starts[k][0], HALO)], kinds.at[k]) for k in range(2)]
    at = 3 * HALO
    for c in range(3):
        for target, (start, start_f) in zip((first, second), starts):
            pairs.append((u_in.at[c, pl.ds(start, HALO)], target.at[pl.ds(HALO * c, HALO)]))
            pairs.append((f_in.at[c, pl.ds(start_f, HALO - 1)], target.at[pl.ds(at, HALO - 1)]))
        at += HALO - 1
    copies = start_all(pairs, done)
    for k, target in enumerate((first, second)):
        copies[k].wait()
        target[at:] = viscosity_of(kinds[k], viscosities)
    for copy in copies[2:]:
        copy.wait()


def corner_layers(count):
    at = 0
    for channel in range(7):
        deep = HALO - 2 if 3 <= channel < 6 else HALO - 1
        if channel == count:
            return at, deep
        at += deep
    return at, 0


def corner_kernel(y_first, y_second, first, second):
    own = y_first.shape[1]
    even = is_even(lax.axis_index("gx"))
    for channel in range(7):
        at, deep = corner_layers(channel)
        for target, upper in ((first, even), (second, jnp.logical_not(even))):
            planes = pl.ds(jnp.where(upper, own - deep, 0), deep)
            target[at:at + deep, :HALO] = y_first[channel, planes]
            target[at:at + deep, HALO:] = y_second[channel, planes]


def on_chip(count):
    return [pl.BlockSpec(memory_space=pltpu.VMEM)] * count


def planes_scratch(planes, rows, lanes, pairs, own_rows, pooled, ends=()):
    block = (planes, rows, lanes)
    return (
        [pltpu.VMEM(ends + (3,) + block, jnp.float32)] * 3
        + [pltpu.VMEM(ends + block, jnp.float32)] * 8
        + [pltpu.VMEM((4, pairs, own_rows, lanes), jnp.float32), pltpu.VMEM(pooled, jnp.float32)]
    )


PACK_LIMIT = 62 * 1024 * 1024
LIMIT = pltpu.CompilerParams(vmem_limit_bytes=20 * 1024 * 1024)


def on_device(velocity_guess, forcing, cell_type, viscosities):
    f32 = jnp.float32
    count_x, count_y = lax.axis_size("gx"), lax.axis_size("gy")
    even_x, even_y = is_even(lax.axis_index("gx")), is_even(lax.axis_index("gy"))
    in_smem = [pl.BlockSpec(memory_space=pltpu.SMEM)]
    own, rows, lanes = cell_type.shape
    y_edge = jax.ShapeDtypeStruct((7, own, HALO, lanes), f32)
    x_edge = jax.ShapeDtypeStruct((7 * HALO - 3, rows, lanes), f32)
    anywhere = [pl.BlockSpec(memory_space=pl.ANY)]
    pack_params = pltpu.CompilerParams(vmem_limit_bytes=PACK_LIMIT)
    y_out, y_out_odd, turn = pl.pallas_call(
        pack_rows_kernel,
        out_shape=(y_edge, y_edge, jax.ShapeDtypeStruct((8, 128), f32)),
        in_specs=in_smem + anywhere * 3,
        out_specs=tuple(on_chip(3)),
        scratch_shapes=[pltpu.VMEM(cell_type.shape, jnp.int32), pltpu.SemaphoreType.DMA((13,))],
        compiler_params=pack_params,
    )(viscosities, velocity_guess, forcing, cell_type)
    y_halo = swapped(y_out, y_out_odd, "gy")
    x_out, x_out_odd = pl.pallas_call(
        pack_planes_kernel,
        out_shape=(x_edge, x_edge),
        in_specs=in_smem + on_chip(1) + anywhere * 3,
        out_specs=tuple(on_chip(2)),
        scratch_shapes=[pltpu.VMEM((2, HALO, rows, lanes), jnp.int32), pltpu.SemaphoreType.DMA((14,))],
        compiler_params=pack_params,
    )(viscosities, turn, velocity_guess, forcing, cell_type)
    x_halo = swapped(x_out, x_out_odd, "gx")
    corner = jax.ShapeDtypeStruct((corner_layers(7)[0], 2 * HALO, lanes), f32)
    corners = pl.pallas_call(
        corner_kernel,
        out_shape=(corner, corner),
        in_specs=on_chip(2),
        out_specs=tuple(on_chip(2)),
        compiler_params=LIMIT,
    )(*y_halo)
    corner_halo = swapped(*corners, "gx")
    tall = rows + 2 * HALO
    middle = own // 2 - HALO
    state = (
        (3, own - 2 * HALO + 2, rows, lanes),
        (4 * middle, rows // 2, lanes // 2),
        (4, 2, 3, 2, tall, lanes),
        (2, 3, HALO, tall, lanes),
        (2, HALO + 1, tall, lanes),
    )
    known = pl.pallas_call(
        inner_kernel,
        out_shape=tuple(jax.ShapeDtypeStruct(shape, f32) for shape in state),
        in_specs=in_smem + on_chip(5),
        out_specs=tuple(on_chip(5)),
        scratch_shapes=planes_scratch(own + 2 * HALO, tall, lanes, middle, rows, (4 * middle, rows, 128)),
        compiler_params=LIMIT,
        cost_estimate=pl.CostEstimate(flops=60_000_000, bytes_accessed=6_000_000, transcendentals=0),
    )(viscosities, velocity_guess, forcing, cell_type, *y_halo)
    u0, packet = pl.pallas_call(
        outer_kernel,
        out_shape=(
            jax.ShapeDtypeStruct(velocity_guess.shape, f32),
            jax.ShapeDtypeStruct((4 * own // 2, rows // 2, lanes // 2), f32),
        ),
        in_specs=on_chip(9),
        out_specs=tuple(on_chip(2)),
        scratch_shapes=planes_scratch(2 * HALO + 1, tall, lanes, HALO, rows, (4 * HALO, rows, 128), (2,)),
        compiler_params=LIMIT,
    )(*known, *x_halo, *corner_halo)
    results = [u0]
    for grid_level in (1, 2):
        own, rows = own // 2, rows // 2
        packet = packet.reshape(4, own, rows, 128)
        valid = 256 >> grid_level
        top, bottom = packet[:, :, rows - HALO:], packet[:, :, :HALO]
        y_halo = swapped(jnp.where(even_y, top, bottom), jnp.where(even_y, bottom, top), "gy")
        upper, lower = jnp.where(even_y, y_halo[0], y_halo[1]), jnp.where(even_y, y_halo[1], y_halo[0])
        parts = [packet, upper, lower]
        total_rows = rows + 2 * HALO
        if total_rows % 8:
            parts = [packet, upper, jnp.zeros_like(upper), lower]
            total_rows += HALO
        top, bottom = (
            jnp.concatenate([part[:, at:at + HALO] for part in parts], axis=2) for at in (own - HALO, 0)
        )
        if valid <= 64:
            top, bottom = (
                jnp.concatenate([tall[:, :, :2 * HALO, :64], tall[:, :, 2 * HALO:, :64]], axis=3)
                for tall in (top, bottom)
            )
        x_halo = swapped(jnp.where(even_x, top, bottom), jnp.where(even_x, bottom, top), "gx")
        if grid_level == 1:
            packet_shape, pooled_shape = (4 * own // 2, rows // 2, 128), (4 * own // 2, rows, 128)
        else:
            packet_shape, pooled_shape = (4, 128), (8, 512)
        u_own, packet = pl.pallas_call(
            functools.partial(middle_kernel, 0.25**grid_level),
            out_shape=(
                jax.ShapeDtypeStruct((3, own, rows, valid), f32),
                jax.ShapeDtypeStruct(packet_shape, f32),
            ),
            in_specs=on_chip(5),
            out_specs=tuple(on_chip(2)),
            scratch_shapes=planes_scratch(own + 2 * HALO, total_rows, 128, own // 2, rows, pooled_shape),
            compiler_params=LIMIT,
        )(packet, *y_halo, *x_halo)
        results.append(u_own)
    column = lax.all_to_all(jnp.broadcast_to(packet[None], (count_x, 4, 128)), "gx", 0, 0)
    width = 2 * REACH + 2
    window = pl.pallas_call(
        window_kernel,
        out_shape=jax.ShapeDtypeStruct((count_y, 4 * width, 128), f32),
        in_specs=on_chip(1),
        out_specs=on_chip(1)[0],
        scratch_shapes=[pltpu.VMEM((4 * width, 128), f32)],
        compiler_params=LIMIT,
    )(column)
    gathered = lax.all_to_all(window, "gy", 0, 0)
    block = (2 * REACH + 1, 16, 128)
    field, vector, six = (pltpu.VMEM(lead + block, f32) for lead in ((), (3,), (6,)))
    last = pl.pallas_call(
        last_kernel,
        out_shape=tuple(jax.ShapeDtypeStruct(shape, f32) for shape in ((3, 2, 2, 32), (3, 1, 1, 16), (3, 1, 1, 16))),
        in_specs=on_chip(1),
        out_specs=tuple(on_chip(3)),
        scratch_shapes=[vector, field, vector, vector, six, field, field,
                        vector, field, six, field, field, vector, vector, pltpu.VMEM((8, 128), f32)],
        compiler_params=LIMIT,
    )(gathered)
    return (*results, *last)


def solution(mesh):
    return jax.shard_map(
        on_device,
        mesh=mesh,
        in_specs=(P(None, "gx", "gy", None), P(None, "gx", "gy", None), P("gx", "gy", None), P()),
        out_specs=(P(None, "gx", "gy", None),) * 6,
        check_vma=False,
    )
```

```python
import functools

import jax
import jax.numpy as jnp
from jax import lax
from jax.experimental import pallas as pl
from jax.experimental.pallas import tpu as pltpu
from jax.sharding import PartitionSpec as P

SWEEPS = 3
LEVELS = 4
HALO = SWEEPS + 1
REACH = 5

damping = 0.8
mass_term = 0.05


def pair_swap(value, axis, odd):
    sizes = {name: lax.axis_size(name) for name in ("gx", "gy")}
    route = []
    for x in range(sizes["gx"]):
        for y in range(sizes["gy"]):
            place = {"gx": x, "gy": y}
            other = ((place[axis] + odd) ^ 1) - odd
            if 0 <= other < sizes[axis]:
                place[axis] = other
            else:
                across = "gy" if axis == "gx" else "gx"
                place[across] ^= 1
            route.append((x * sizes["gy"] + y, place["gx"] * sizes["gy"] + place["gy"]))
    return lax.ppermute(value, ("gx", "gy"), route)


def swapped(to_even, to_odd, axis):
    return pair_swap(to_even, axis, 0), pair_swap(to_odd, axis, 1)


def own_place():
    return lax.axis_index("gx"), lax.axis_index("gy"), lax.axis_size("gx"), lax.axis_size("gy")


def is_even(position):
    return position % 2 == 0


def split_dot(rows, pool):
    total = None
    for part in range(3):
        piece = rows.astype(jnp.bfloat16)
        term = jnp.dot(piece, pool, preferred_element_type=jnp.float32)
        total = term if total is None else total + term
        if part < 2:
            rows = rows - piece.astype(jnp.float32)
    return total


def inside_rows(place, own_rows, total_rows, shape, along_x=True):
    row = lax.broadcasted_iota(jnp.int32, shape, 0)
    above = jnp.where(place[1] < place[3] - 1, own_rows + HALO, own_rows)
    below = jnp.where(place[1] > 0, total_rows - HALO, total_rows)
    above = jnp.where(along_x, above, 0)
    below = jnp.where(along_x, below, total_rows)
    return (row < above) | (row >= below)


def pair_pool(lanes):
    source = lax.broadcasted_iota(jnp.int32, (lanes, 128), 0)
    target = lax.broadcasted_iota(jnp.int32, (lanes, 128), 1)
    return jnp.where(source // 2 == target, 0.125, 0.0).astype(jnp.bfloat16)


def make_coefficients(scale, lo, hi, m, cx, cym, cyp, czm, czp, weight, diag, unroll=False):
    rows, lanes = m.shape[1:]
    half = 0.5 * scale
    lane = lax.broadcasted_iota(jnp.int32, (rows, lanes), 1)
    cx[lo - 1] = half * (m[lo - 1] + m[lo])

    def plane(i, _):
        centre = m[i]
        upper = m[i + 1]
        y_lower = pltpu.roll(centre, 1, 0)
        y_upper = pltpu.roll(centre, rows - 1, 0)
        z_lower = jnp.where(lane == 0, 0.0, pltpu.roll(centre, 1, 1))
        z_upper = jnp.where(lane == lanes - 1, 0.0, pltpu.roll(centre, lanes - 1, 1))
        f_xl, f_xu = half * (centre + m[i - 1]), half * (centre + upper)
        f_yl, f_yu = half * (centre + y_lower), half * (centre + y_upper)
        f_zl, f_zu = half * (centre + z_lower), half * (centre + z_upper)
        total = mass_term + (f_xl + f_xu + f_yl + f_yu + f_zl + f_zu)
        cx[i] = f_xu
        cym[i], cyp[i] = f_yl, f_yu
        czm[i] = jnp.where(lane == 0, 0.0, f_zl)
        czp[i] = jnp.where(lane == lanes - 1, 0.0, f_zu)
        diag[i] = total
        weight[i] = jnp.where(centre > 0.0, damping / total, 0.0)
        return 0

    lax.fori_loop(lo, hi, plane, 0, unroll=unroll)


def flux_of(u, c, i, cx, cym, cyp, czm, czp):
    rows, lanes = u.shape[2:]
    centre = u[c, i]
    flux = cx[i - 1] * u[c, i - 1] + cx[i] * u[c, i + 1]
    flux += cym[i] * pltpu.roll(centre, 1, 0) + cyp[i] * pltpu.roll(centre, rows - 1, 0)
    flux += czm[i] * pltpu.roll(centre, 1, 1) + czp[i] * pltpu.roll(centre, lanes - 1, 1)
    return centre, flux


def relax(lo, hi, source, target, f, weight, faces, unroll=False):
    def plane(i, _):
        for c in range(3):
            centre, flux = flux_of(source, c, i, *faces)
            target[c, i] = (1.0 - damping) * centre + weight[i] * (f[c, i] + flux)
        return 0

    lax.fori_loop(lo, hi, plane, 0, unroll=unroll)


def start_from_zero(lo, hi, target, f, weight, unroll=False):
    def plane(i, _):
        for c in range(3):
            target[c, i] = weight[i] * f[c, i]
        return 0

    lax.fori_loop(lo, hi, plane, 0, unroll=unroll)


def residual_pairs(at, count, first, own_rows, u, f, m, diag, faces, pairs, unroll=False):
    def pair(p, _):
        i = at + 2 * p
        for c in range(3):
            both = None
            for j in (i, i + 1):
                centre, flux = flux_of(u, c, j, *faces)
                value = f[c, j] + flux - diag[j] * centre
                both = value if both is None else both + value
            pairs[c, first + p] = both[:own_rows]
        pairs[3, first + p] = (m[i] + m[i + 1])[:own_rows]
        return 0

    lax.fori_loop(0, count, pair, 0, unroll=unroll)


def pool_pairs(pairs, pooled):
    lanes = pairs.shape[-1]
    rows = pooled.shape[1]
    summed = split_dot(pairs[...].reshape(-1, lanes), pair_pool(lanes))
    pooled[...] = summed.reshape(pooled.shape)
    return pooled[:, pl.ds(0, rows // 2, 2), :] + pooled[:, pl.ds(1, rows // 2, 2), :]


def inner_kernel(viscosities, u_in, f_in, types, y_first, y_second, u_mid, packet_mid, u_edge, f_edge, m_edge,
                 ua, ub, f, m, cx, cym, cyp, czm, czp, weight, diag, pairs, pooled):
    place = own_place()
    own, rows = u_in.shape[1:3]
    body = pl.ds(HALO, own)
    last = HALO + own
    has_lower, has_upper = place[1] > 0, place[1] < place[3] - 1
    even = is_even(place[1])

    def put_rows(field, channel, masked):
        first, second = y_first[channel], y_second[channel]
        upper, lower = jnp.where(even, first, second), jnp.where(even, second, first)
        field[body, rows:rows + HALO] = jnp.where(has_upper, upper, 0.0) if masked else upper
        field[body, rows + HALO:] = jnp.where(has_lower, lower, 0.0) if masked else lower

    for c in range(3):
        ua[c, body, :rows] = u_in[c]
        put_rows(ua.at[c], c, True)
        f[c, body, :rows] = f_in[c]
        put_rows(f.at[c], 3 + c, False)
    m[body, :rows] = viscosity_of(types[...], viscosities)
    put_rows(m, 6, True)

    def edges(stage, u, depth):
        u_edge[stage, 0] = u[:, HALO + depth:HALO + depth + 2]
        u_edge[stage, 1] = u[:, last - depth - 2:last - depth]

    edges(0, ua, 0)
    f_edge[0], f_edge[1] = f[:, HALO:2 * HALO], f[:, last - HALO:last]
    m_edge[0], m_edge[1] = m[HALO:2 * HALO + 1], m[last - HALO - 1:last]
    make_coefficients(1.0, HALO + 1, last - 1, m, cx, cym, cyp, czm, czp, weight, diag, True)
    faces = (cx, cym, cyp, czm, czp)
    relax(HALO + 1, last - 1, ua, ub, f, weight, faces, True)
    edges(1, ub, 1)
    relax(HALO + 2, last - 2, ub, ua, f, weight, faces, True)
    edges(2, ua, 2)
    relax(HALO + 3, last - 3, ua, ub, f, weight, faces, True)
    edges(3, ub, 3)
    u_mid[...] = ub[:, HALO + 3:last - 3, :rows]
    residual_pairs(2 * HALO, own // 2 - HALO, 0, rows, ub, f, m, diag, faces, pairs, True)
    packet_mid[...] = pool_pairs(pairs, pooled)


def outer_kernel(u_mid, packet_mid, u_edge, f_edge, m_edge, x_first, x_second, corner_first, corner_second, u_out, packet,
                 ua, ub, f, m, cx, cym, cyp, czm, czp, weight, diag, pairs, pooled):
    place = own_place()
    own, rows = u_out.shape[1:3]
    planes = m.shape[1]
    count_f = HALO - 1
    at_f, at_m = 3 * HALO, 3 * HALO + 3 * count_f
    half = own // 2
    corner_shape = corner_first.shape[1:]
    even, even_y = is_even(place[0]), is_even(place[1])

    for end in range(2):
        take_first = even if end == 1 else jnp.logical_not(even)

        def halo(at, count):
            return jnp.where(take_first, x_first[at:at + count], x_second[at:at + count])

        def corner(at, count):
            rows_of = [corner_first[at + i] for i in range(count)], [corner_second[at + i] for i in range(count)]
            chosen = [jnp.where(take_first, one, two) for one, two in zip(*rows_of)]
            return jnp.stack([jnp.where(even_y, one, pltpu.roll(one, HALO, 0)) for one in chosen])

        outer = 0 if end == 0 else planes - HALO
        inner = HALO if end == 0 else 0
        present = place[0] > 0 if end == 0 else place[0] < place[2] - 1
        inside = inside_rows(place, 0, 2 * HALO, corner_shape, present)

        def put_corner(field, channel, masked):
            at, deep = corner_layers(channel)
            value = corner(at, deep)
            if masked:
                value = jnp.where(inside, value, 0.0)
            first = HALO - deep if end == 0 else planes - HALO
            field[first:first + deep, rows:] = value
            far = first - 1 if end == 0 else first + deep
            field[far, rows:] = jnp.zeros(corner_shape, jnp.float32)

        for c in range(3):
            ua[end, c, outer:outer + HALO, :rows] = jnp.where(present, halo(HALO * c, HALO), 0.0)
            put_corner(ua.at[end, c], c, True)
            nearest = HALO if end == 0 else planes - HALO - 2
            ua[end, c, nearest:nearest + 2] = u_edge[0, end, c]
            beyond = 1 if end == 0 else planes - HALO
            f[end, c, beyond:beyond + count_f, :rows] = halo(at_f + count_f * c, count_f)
            put_corner(f.at[end, c], 3 + c, False)
            own_f = HALO if end == 0 else planes - 2 * HALO
            f[end, c, own_f:own_f + HALO] = f_edge[end, c]
        m[end, outer:outer + HALO, :rows] = jnp.where(present, halo(at_m, HALO), 0.0)
        put_corner(m.at[end], 6, True)
        m[end, inner:inner + HALO + 1] = m_edge[end]
        parts = (cx.at[end], cym.at[end], cyp.at[end], czm.at[end], czp.at[end])
        u_a, u_b, f_e, w_e, d_e = ua.at[end], ub.at[end], f.at[end], weight.at[end], diag.at[end]
        make_coefficients(1.0, 1, planes - 1, m.at[end], *parts, w_e, d_e, True)
        for stage, (source, target) in enumerate(((u_a, u_b), (u_b, u_a), (u_a, u_b))):
            first = 1 + stage if end == 0 else planes - 1 - HALO - stage
            relax(first, first + HALO, source, target, f_e, w_e, parts, True)
            known = first + HALO if end == 0 else first - 2
            for c in range(3):
                target[c, known:known + 2] = u_edge[stage + 1, end, c]
        at = HALO if end == 0 else 1
        residual_pairs(at, HALO // 2, HALO // 2 * end, rows, u_b, f_e, m.at[end], d_e, parts, pairs, True)
        for c in range(3):
            if end == 0:
                u_out[c, :HALO - 1] = ub[end, c, HALO:2 * HALO - 1, :rows]
            else:
                u_out[c, own - HALO + 1:] = ub[end, c, planes - 2 * HALO + 1:planes - HALO, :rows]
    u_out[:, HALO - 1:own - HALO + 1] = u_mid[...]
    ends = pool_pairs(pairs, pooled)
    for c in range(4):
        at = HALO * c
        packet[half * c:half * c + 2] = ends[at:at + 2]
        packet[half * c + 2:half * (c + 1) - 2] = packet_mid[(half - HALO) * c:(half - HALO) * (c + 1)]
        packet[half * (c + 1) - 2:half * (c + 1)] = ends[at + 2:at + 4]


def middle_kernel(scale, p_in, y_first, y_second, x_first, x_second, u_out, packet,
                  ua, ub, f, m, cx, cym, cyp, czm, czp, weight, diag, pairs, pooled):
    place = own_place()
    own, rows = p_in.shape[1:3]
    body = pl.ds(HALO, own)
    planes = own + 2 * HALO
    total_rows = m.shape[1]
    even_x, even_y = is_even(place[0]), is_even(place[1])
    for c in range(4):
        if c < 3:
            field = f.at[c]
        else:
            field = m
        if total_rows > rows + 2 * HALO:
            field[body] = jnp.zeros((own,) + m.shape[1:], jnp.float32)
        field[body, :rows] = p_in[c]
        field[body, rows:rows + HALO] = jnp.where(even_y, y_first[c], y_second[c])
        field[body, total_rows - HALO:] = jnp.where(even_y, y_second[c], y_first[c])
        width = HALO - 1 if c < 3 else HALO
        first, second = (packet_x[(HALO - 1) * c:(HALO - 1) * c + width] for packet_x in (x_first, x_second))
        below, above = jnp.where(even_x, second, first), jnp.where(even_x, first, second)
        for start, value in ((HALO - width, below), (HALO + own, above)):
            if value.shape[1] == total_rows:
                field[start:start + width] = value
                continue
            half = value.shape[1]
            left = lax.broadcasted_iota(jnp.int32, value.shape[1:], 1) < 64
            for i in range(width):
                field[start + i, :half] = jnp.where(left, value[i], 0.0)
                field[start + i, half:] = jnp.where(left, pltpu.roll(value[i], 64, 1), 0.0)
    shape = m.shape[1:]
    in_rows = inside_rows(place, rows, total_rows, shape)
    in_lower = inside_rows(place, rows, total_rows, shape, place[0] > 0)
    in_upper = inside_rows(place, rows, total_rows, shape, place[0] < place[2] - 1)
    m[body] = jnp.where(in_rows, m[body], 0.0)
    m[:HALO] = jnp.where(in_lower, m[:HALO], 0.0)
    m[HALO + own:] = jnp.where(in_upper, m[HALO + own:], 0.0)
    make_coefficients(scale, 1, planes - 1, m, cx, cym, cyp, czm, czp, weight, diag, unroll=True)
    faces = (cx, cym, cyp, czm, czp)
    start_from_zero(1, planes - 1, ub, f, weight, unroll=True)
    relax(2, planes - 2, ub, ua, f, weight, faces, unroll=True)
    relax(3, planes - 3, ua, ub, f, weight, faces, unroll=True)
    lanes = u_out.shape[-1]
    for c in range(3):
        u_out[c] = ub[c, body, :rows, :lanes]
    residual_pairs(HALO, own // 2, 0, rows, ub, f, m, diag, faces, pairs, unroll=True)
    if rows > 4:
        packet[...] = pool_pairs(pairs, pooled)
    else:
        for c in range(4):
            for p in range(own // 2):
                for q in range(rows // 2):
                    at = 128 * (p * (rows // 2) + q)
                    pooled[c:c + 1, at:at + 128] = (
                        pairs[c, p, 2 * q:2 * q + 1] + pairs[c, p, 2 * q + 1:2 * q + 2]
                    )
        depth = pooled.shape[1]
        source = lax.broadcasted_iota(jnp.int32, (depth, 128), 0)
        target = lax.broadcasted_iota(jnp.int32, (depth, 128), 1)
        hit = (source // 128 * 32 + source % 128 // 2 == target) & (source % 128 < 64)
        pool = jnp.where(hit, 0.125, 0.0).astype(jnp.bfloat16)
        packet[...] = split_dot(pooled[...], pool)[:4]


def window_kernel(column, out, rows_of):
    count = column.shape[0]
    width = rows_of.shape[0] // 4
    x_at = lax.axis_index("gx")
    for r in range(width):
        i = x_at + (r - REACH)
        value = jnp.where((i >= 0) & (i < count), column[jnp.clip(i, 0, count - 1)], 0.0)
        for c in range(4):
            rows_of[width * c + r:width * c + r + 1] = value[c:c + 1]
    out[...] = jnp.broadcast_to(rows_of[...][None], out.shape)


def last_kernel(g, u3_out, u4_out, r4_out, fw, mw, ua, ub, faces, weight, diag,
                f4, m4, faces4, weight4, diag4, va, vb, rows_out):
    count, width = g.shape[0], g.shape[1] // 4
    rows, lanes = mw.shape[1:]
    shape = (rows, lanes)
    lane = lax.broadcasted_iota(jnp.int32, shape, 1)
    x_one, y_one, z = lane // 64 == 1, lane // 32 % 2 == 1, lane % 32
    zero = jnp.zeros(shape, jnp.float32)
    y_at = lax.axis_index("gy")
    window = 2 * REACH + 1
    for w in range(window):
        i = y_at + (w - REACH)
        inside = (i >= 0) & (i < count)
        i = jnp.clip(i, 0, count - 1)
        for c in range(4):
            place = fw.at[c, w] if c < 3 else mw.at[w]
            place[:width] = jnp.where(inside, g[i, width * c:width * (c + 1)], 0.0)
            place[width:] = zero[width:]

    def shifted_rows(value):
        return pltpu.roll(value, 1, 0), pltpu.roll(value, rows - 1, 0)

    def near3(get, w, turned):
        for j in (w - 1, w, w + 1):
            if j not in turned:
                inside = 0 <= j < window
                turned[j] = (pltpu.roll(get(j), 32, 1), pltpu.roll(get(j), lanes - 32, 1)) if inside else (zero, zero)
        centre = get(w)
        other = pltpu.roll(centre, 64, 1)
        lower, upper = shifted_rows(other)
        x_out = jnp.where(x_one, upper, lower)
        y_in = jnp.where(y_one, turned[w][0], turned[w][1])
        y_out = jnp.where(y_one, turned[w + 1][0], turned[w - 1][1])
        return centre, (other, x_out, y_in, y_out, pltpu.roll(centre, 1, 1), pltpu.roll(centre, lanes - 1, 1))

    outside3 = (None, None, None, None, z == 0, z == 31)

    def near4(get, w, turned):
        centre = get(w)
        lower, upper = shifted_rows(centre)
        return centre, (lower, upper, get(w - 1), get(w + 1),
                        pltpu.roll(centre, 2, 1), pltpu.roll(centre, lanes - 2, 1))

    outside4 = (None, None, None, None, z < 2, z >= 30)

    def level(scale, near, outside, f, m, faces, weight, diag, ua, ub, spans, residual):
        half = 0.5 * scale
        turned = {}
        for w in spans[0]:
            centre, sides = near(lambda j: m[j], w, turned)
            total = jnp.full(shape, mass_term, jnp.float32)
            for k in range(6):
                side = sides[k] if outside[k] is None else jnp.where(outside[k], 0.0, sides[k])
                face = half * (centre + side)
                total = total + face
                faces[k, w] = face if outside[k] is None else jnp.where(outside[k], 0.0, face)
            diag[w] = total
            weight[w] = jnp.where(centre > 0.0, damping / total, 0.0)
            for c in range(3):
                ua[c, w] = weight[w] * f[c, w]

        def flux_at(u, c, w, turned):
            centre, sides = near(lambda j: u[c, j], w, turned)
            flux = faces[0, w] * sides[0]
            for k in range(1, 6):
                flux = flux + faces[k, w] * sides[k]
            return centre, flux

        for source, target, span in ((ua, ub, spans[1]), (ub, ua, spans[2])):
            for c in range(3):
                turned = {}
                for w in span:
                    centre, flux = flux_at(source, c, w, turned)
                    target[c, w] = (1.0 - damping) * centre + weight[w] * (f[c, w] + flux)
        for c in range(3):
            turned = {}
            for w in spans[3]:
                centre, flux = flux_at(ua, c, w, turned)
                residual(c, w, f[c, w] + flux - diag[w] * centre)

    def pool(value):
        value = value + pltpu.roll(value, 64, 1)
        value = value + pltpu.roll(value, 32, 1)
        return 0.125 * (value + pltpu.roll(value, lanes - 1, 1))

    def to_level4(c, w, value):
        f4[c, w] = pool(value)

    spans = (range(window), range(1, window - 1), range(1, window - 1), range(2, window - 2))
    level(0.25**3, near3, outside3, fw, mw, faces, weight, diag, ua, ub, spans, to_level4)
    for w in range(1, window - 1):
        m4[w] = pool(mw[w])

    def own_row(value):
        return value[REACH:REACH + 1]

    def keep(c, w, value):
        rows_out[3 + c:4 + c] = own_row(value)

    spans = tuple(range(2 + k, window - 2 - k) for k in range(4))
    level(0.25**4, near4, outside4, f4, m4, faces4, weight4, diag4, va, vb, spans, keep)
    for c in range(3):
        value = own_row(ua[c, REACH])
        rows_out[c:c + 1] = own_row(va[c, REACH])
        for k in range(4):
            turned = value if k == 0 else pltpu.roll(value, lanes - 32 * k, 1)
            u3_out[c, k // 2, k % 2:k % 2 + 1] = turned[:, :32]
    source = lax.broadcasted_iota(jnp.int32, (lanes, lanes), 0)
    target = lax.broadcasted_iota(jnp.int32, (lanes, lanes), 1)
    take = jnp.where((source == 2 * target) & (target < 16), 1.0, 0.0).astype(jnp.bfloat16)
    ends = split_dot(rows_out[...], take)
    for c in range(3):
        u4_out[c, 0] = ends[c:c + 1, :16]
        r4_out[c, 0] = ends[3 + c:4 + c, :16]


def viscosity_of(kind, viscosities):
    return jnp.where(
        kind < 2,
        jnp.where(kind == 0, viscosities[0], viscosities[1]),
        jnp.where(kind == 2, viscosities[2], viscosities[3]),
    )


def start_all(pairs, done):
    copies = [pltpu.make_async_copy(*pair, done.at[i]) for i, pair in enumerate(pairs)]
    for copy in copies:
        copy.start()
    return copies


def pack_rows_kernel(viscosities, u_in, f_in, types, first, second, turn, kinds, done):
    own, rows = types.shape[:2]
    even = is_even(lax.axis_index("gy"))
    if_even, if_odd = [(types, kinds)], [(types, kinds)]
    for c in range(6):
        field = u_in.at[c] if c < 3 else f_in.at[c - 3]
        top, bottom = field.at[:, pl.ds(rows - HALO, HALO)], field.at[:, pl.ds(0, HALO)]
        if_even += [(top, first.at[c]), (bottom, second.at[c])]
        if_odd += [(bottom, first.at[c]), (top, second.at[c])]
    pl.when(even)(lambda: start_all(if_even, done) and None)
    pl.when(jnp.logical_not(even))(lambda: start_all(if_odd, done) and None)
    turn[...] = jnp.zeros(turn.shape, jnp.float32)
    waits = [pltpu.make_async_copy(*pair, done.at[i]) for i, pair in enumerate(if_even)]
    waits[0].wait()
    top = viscosity_of(kinds[:, rows - HALO:], viscosities)
    bottom = viscosity_of(kinds[:, :HALO], viscosities)
    first[6], second[6] = jnp.where(even, top, bottom), jnp.where(even, bottom, top)
    for copy in waits[1:]:
        copy.wait()


def pack_planes_kernel(viscosities, turn, u_in, f_in, types, first, second, kinds, done):
    own = types.shape[0]
    even = is_even(lax.axis_index("gx"))
    starts = [
        (jnp.where(upper, own - HALO, 0), jnp.where(upper, own - HALO + 1, 0))
        for upper in (even, jnp.logical_not(even))
    ]
    pairs = [(types.at[pl.ds(starts[k][0], HALO)], kinds.at[k]) for k in range(2)]
    at = 3 * HALO
    for c in range(3):
        for target, (start, start_f) in zip((first, second), starts):
            pairs.append((u_in.at[c, pl.ds(start, HALO)], target.at[pl.ds(HALO * c, HALO)]))
            pairs.append((f_in.at[c, pl.ds(start_f, HALO - 1)], target.at[pl.ds(at, HALO - 1)]))
        at += HALO - 1
    copies = start_all(pairs, done)
    for k, target in enumerate((first, second)):
        copies[k].wait()
        target[at:] = viscosity_of(kinds[k], viscosities)
    for copy in copies[2:]:
        copy.wait()


def corner_layers(count):
    at = 0
    for channel in range(7):
        deep = HALO - 2 if 3 <= channel < 6 else HALO - 1
        if channel == count:
            return at, deep
        at += deep
    return at, 0


def corner_kernel(y_first, y_second, first, second):
    own = y_first.shape[1]
    even = is_even(lax.axis_index("gx"))
    for channel in range(7):
        at, deep = corner_layers(channel)
        for target, upper in ((first, even), (second, jnp.logical_not(even))):
            planes = pl.ds(jnp.where(upper, own - deep, 0), deep)
            target[at:at + deep, :HALO] = y_first[channel, planes]
            target[at:at + deep, HALO:] = y_second[channel, planes]


def on_chip(count):
    return [pl.BlockSpec(memory_space=pltpu.VMEM)] * count


def planes_scratch(planes, rows, lanes, pairs, own_rows, pooled, ends=()):
    block = (planes, rows, lanes)
    return (
        [pltpu.VMEM(ends + (3,) + block, jnp.float32)] * 3
        + [pltpu.VMEM(ends + block, jnp.float32)] * 8
        + [pltpu.VMEM((4, pairs, own_rows, lanes), jnp.float32), pltpu.VMEM(pooled, jnp.float32)]
    )


PACK_LIMIT = 62 * 1024 * 1024
LIMIT = pltpu.CompilerParams(vmem_limit_bytes=20 * 1024 * 1024)


def on_device(velocity_guess, forcing, cell_type, viscosities):
    f32 = jnp.float32
    count_x, count_y = lax.axis_size("gx"), lax.axis_size("gy")
    even_x, even_y = is_even(lax.axis_index("gx")), is_even(lax.axis_index("gy"))
    in_smem = [pl.BlockSpec(memory_space=pltpu.SMEM)]
    own, rows, lanes = cell_type.shape
    y_edge = jax.ShapeDtypeStruct((7, own, HALO, lanes), f32)
    x_edge = jax.ShapeDtypeStruct((7 * HALO - 3, rows, lanes), f32)
    anywhere = [pl.BlockSpec(memory_space=pl.ANY)]
    pack_params = pltpu.CompilerParams(vmem_limit_bytes=PACK_LIMIT)
    y_out, y_out_odd, turn = pl.pallas_call(
        pack_rows_kernel,
        out_shape=(y_edge, y_edge, jax.ShapeDtypeStruct((8, 128), f32)),
        in_specs=in_smem + anywhere * 3,
        out_specs=tuple(on_chip(3)),
        scratch_shapes=[pltpu.VMEM(cell_type.shape, jnp.int32), pltpu.SemaphoreType.DMA((13,))],
        compiler_params=pack_params,
    )(viscosities, velocity_guess, forcing, cell_type)
    y_halo = swapped(y_out, y_out_odd, "gy")
    x_out, x_out_odd = pl.pallas_call(
        pack_planes_kernel,
        out_shape=(x_edge, x_edge),
        in_specs=in_smem + on_chip(1) + anywhere * 3,
        out_specs=tuple(on_chip(2)),
        scratch_shapes=[pltpu.VMEM((2, HALO, rows, lanes), jnp.int32), pltpu.SemaphoreType.DMA((14,))],
        compiler_params=pack_params,
    )(viscosities, turn, velocity_guess, forcing, cell_type)
    x_halo = swapped(x_out, x_out_odd, "gx")
    corner = jax.ShapeDtypeStruct((corner_layers(7)[0], 2 * HALO, lanes), f32)
    corners = pl.pallas_call(
        corner_kernel,
        out_shape=(corner, corner),
        in_specs=on_chip(2),
        out_specs=tuple(on_chip(2)),
        compiler_params=LIMIT,
    )(*y_halo)
    corner_halo = swapped(*corners, "gx")
    tall = rows + 2 * HALO
    middle = own // 2 - HALO
    state = (
        (3, own - 2 * HALO + 2, rows, lanes),
        (4 * middle, rows // 2, lanes // 2),
        (4, 2, 3, 2, tall, lanes),
        (2, 3, HALO, tall, lanes),
        (2, HALO + 1, tall, lanes),
    )
    known = pl.pallas_call(
        inner_kernel,
        out_shape=tuple(jax.ShapeDtypeStruct(shape, f32) for shape in state),
        in_specs=in_smem + on_chip(5),
        out_specs=tuple(on_chip(5)),
        scratch_shapes=planes_scratch(own + 2 * HALO, tall, lanes, middle, rows, (4 * middle, rows, 128)),
        compiler_params=LIMIT,
        cost_estimate=pl.CostEstimate(flops=60_000_000, bytes_accessed=6_000_000, transcendentals=0),
    )(viscosities, velocity_guess, forcing, cell_type, *y_halo)
    u0, packet = pl.pallas_call(
        outer_kernel,
        out_shape=(
            jax.ShapeDtypeStruct(velocity_guess.shape, f32),
            jax.ShapeDtypeStruct((4 * own // 2, rows // 2, lanes // 2), f32),
        ),
        in_specs=on_chip(9),
        out_specs=tuple(on_chip(2)),
        scratch_shapes=planes_scratch(2 * HALO + 1, tall, lanes, HALO, rows, (4 * HALO, rows, 128), (2,)),
        compiler_params=LIMIT,
    )(*known, *x_halo, *corner_halo)
    results = [u0]
    for grid_level in (1, 2):
        own, rows = own // 2, rows // 2
        packet = packet.reshape(4, own, rows, 128)
        valid = 256 >> grid_level
        top, bottom = packet[:, :, rows - HALO:], packet[:, :, :HALO]
        y_halo = swapped(jnp.where(even_y, top, bottom), jnp.where(even_y, bottom, top), "gy")
        upper, lower = jnp.where(even_y, y_halo[0], y_halo[1]), jnp.where(even_y, y_halo[1], y_halo[0])
        parts = [packet, upper, lower]
        total_rows = rows + 2 * HALO
        if total_rows % 8:
            parts = [packet, upper, jnp.zeros_like(upper), lower]
            total_rows += HALO
        top, bottom = (
            jnp.concatenate([part[:, at:at + HALO] for part in parts], axis=2) for at in (own - HALO, 0)
        )
        if valid <= 64:
            top, bottom = (
                jnp.concatenate([tall[:, :, :2 * HALO, :64], tall[:, :, 2 * HALO:, :64]], axis=3)
                for tall in (top, bottom)
            )
        top, bottom = (
            jnp.concatenate([planes[c, at:at + HALO - 1] for c in range(3)] + [planes[3]], axis=0)
            for planes, at in ((top, 1), (bottom, 0))
        )
        x_halo = swapped(jnp.where(even_x, top, bottom), jnp.where(even_x, bottom, top), "gx")
        if grid_level == 1:
            packet_shape, pooled_shape = (4 * own // 2, rows // 2, 128), (4 * own // 2, rows, 128)
        else:
            packet_shape, pooled_shape = (4, 128), (8, 512)
        u_own, packet = pl.pallas_call(
            functools.partial(middle_kernel, 0.25**grid_level),
            out_shape=(
                jax.ShapeDtypeStruct((3, own, rows, valid), f32),
                jax.ShapeDtypeStruct(packet_shape, f32),
            ),
            in_specs=on_chip(5),
            out_specs=tuple(on_chip(2)),
            scratch_shapes=planes_scratch(own + 2 * HALO, total_rows, 128, own // 2, rows, pooled_shape),
            compiler_params=LIMIT,
        )(packet, *y_halo, *x_halo)
        results.append(u_own)
    column = lax.all_to_all(jnp.broadcast_to(packet[None], (count_x, 4, 128)), "gx", 0, 0)
    width = 2 * REACH + 2
    window = pl.pallas_call(
        window_kernel,
        out_shape=jax.ShapeDtypeStruct((count_y, 4 * width, 128), f32),
        in_specs=on_chip(1),
        out_specs=on_chip(1)[0],
        scratch_shapes=[pltpu.VMEM((4 * width, 128), f32)],
        compiler_params=LIMIT,
    )(column)
    gathered = lax.all_to_all(window, "gy", 0, 0)
    block = (2 * REACH + 1, 16, 128)
    field, vector, six = (pltpu.VMEM(lead + block, f32) for lead in ((), (3,), (6,)))
    last = pl.pallas_call(
        last_kernel,
        out_shape=tuple(jax.ShapeDtypeStruct(shape, f32) for shape in ((3, 2, 2, 32), (3, 1, 1, 16), (3, 1, 1, 16))),
        in_specs=on_chip(1),
        out_specs=tuple(on_chip(3)),
        scratch_shapes=[vector, field, vector, vector, six, field, field,
                        vector, field, six, field, field, vector, vector, pltpu.VMEM((8, 128), f32)],
        compiler_params=LIMIT,
    )(gathered)
    return (*results, *last)


def solution(mesh):
    return jax.shard_map(
        on_device,
        mesh=mesh,
        in_specs=(P(None, "gx", "gy", None), P(None, "gx", "gy", None), P("gx", "gy", None), P()),
        out_specs=(P(None, "gx", "gy", None),) * 6,
        check_vma=False,
    )
```
